32 devices in a mesh: dp: 4 (over x, core), seq: 8 (over z, y).
Axes of the slice: x: 2, y: 2, z: 4, core: 2. Of those that a mesh axis runs over, the one named last changes fastest.
Arguments:
- tokens: float32 [2, 16384, 512], P(None, ('dp', 'seq')), may hold values from -6 to 6
- cotangent: float32 [2, 16384, 512], P(None, ('dp', 'seq')), may hold values from -6 to 6
- segments: int32 [2, 16384], P(None, ('dp', 'seq')), may hold values from 0 to 11, as said below
- input_weight: bfloat16 [2, 512, 1536], P(None, 'dp'), may hold values from -0.25 to 0.25
- input_bias: bfloat16 [2, 1536], P(None, 'dp'), may hold values from -2 to 2
- output_weight: bfloat16 [2, 512, 512], P(None, 'dp'), may hold values from -2 to 2
- output_bias: bfloat16 [2, 512], P(None, 'dp'), may hold values from -2 to 2
- up_weight: bfloat16 [2, 512, 2048], P(None, 'dp'), may hold values from -0.25 to 0.25
- up_bias: bfloat16 [2, 2048], P(None, 'dp'), may hold values from -2 to 2
- down_weight: bfloat16 [2, 2048, 512], P(None, 'dp'), may hold values from -0.125 to 0.125
- down_bias: bfloat16 [2, 512], P(None, 'dp'), may hold values from -2 to 2
- norm_gain: bfloat16 [2, 2, 512], P(None, None, 'dp'), may hold values from 0.5 to 1.5
- norm_shift: bfloat16 [2, 2, 512], P(None, None, 'dp'), may hold values from -2 to 2
Outputs:
- result: float32 [2, 16384, 512], P(None, ('dp', 'seq'))
- token_grad: float32 [2, 16384, 512], P(None, ('dp', 'seq'))
- input_weight_grad: float32 [2, 512, 1536], P(None, 'dp')
- input_bias_grad: float32 [2, 1536], P(None, 'dp')
- output_weight_grad: float32 [2, 512, 512], P(None, 'dp')
- output_bias_grad: float32 [2, 512], P(None, 'dp')
- up_weight_grad: float32 [2, 512, 2048], P(None, 'dp')
- up_bias_grad: float32 [2, 2048], P(None, 'dp')
- down_weight_grad: float32 [2, 2048, 512], P(None, 'dp')
- down_bias_grad: float32 [2, 512], P(None, 'dp')
- norm_gain_grad: float32 [2, 2, 512], P(None, None, 'dp')
- norm_shift_grad: float32 [2, 2, 512], P(None, None, 'dp')
The draws below stay inside these ranges and needn't reach their ends.
Inputs may be any that keep to these rules, and one draw needn't show every extreme that they name: `segments`: along a micro-batch the ids never fall. Group g of 4096 rows (rows g * 4096 to (g + 1) * 4096 - 1) holds the ids 3 g, 3 g + 1 and 3 g + 2, each as one run of consecutive rows: the first run has an odd number of rows below min(784, 512), the last run 1 to min(784, 512) - 1 rows, and the middle run all the rows between.
All inputs are finite; a program needn't handle non-finite values.
Results may differ from the reference program's by a relative error of at most 0.0095.
Values may be sent and summed in bfloat16 or wider, within the bound.
No kernel may reach another device: no remote copies, remote signals or barrier semaphores. Data moves between devices by JAX's collectives and lax.ppermute only.
A program may use at most 256 MiB of HBM per device.

```python
import jax
import jax.numpy as jnp
from jax import lax

D = 512
HEADS = 8
HEAD = 64
FF = 2048
LAYERS = 2
MICRO = 2
SHORT_LEN = 784
TOK_DEV = 512
GROUP = 4096
TOKENS = 16384
N_DP = 4
N_SEQ = 8


def draw_segments(key, part):
    key = jax.random.fold_in(key, 11)
    head_key, tail_key = jax.random.split(key, 2)
    edge = min(SHORT_LEN, TOK_DEV)
    head_rows = (2 * jax.random.randint(head_key, (MICRO, N_DP, 1), 0, edge // 2) + 1).astype(jnp.int32)
    tail_rows = jax.random.randint(tail_key, (MICRO, N_DP, 1), 1, edge).astype(jnp.int32)
    positions = jnp.arange(GROUP, dtype=jnp.int32)[None, None, :]
    run_index = (positions >= head_rows).astype(jnp.int32) + (positions >= GROUP - tail_rows).astype(jnp.int32)
    group_base = 3 * jnp.arange(N_DP, dtype=jnp.int32)[None, :, None]
    return (run_index + group_base).reshape(MICRO, TOKENS).astype(jnp.int32)


def level_of(key, extent, cuts, low, largest):
    loudness, own = 1.0, jax.random.fold_in(key, 6)
    for dim, shards_of in cuts:
        steps = jnp.exp(jax.random.uniform(jax.random.fold_in(own, dim), (shards_of,), jnp.float32, low / len(cuts), largest / len(cuts)))
        loudness = loudness * jnp.repeat(steps, extent[dim] // shards_of).reshape([-1 if axis == dim else 1 for axis in range(len(extent))])
    return loudness


def bell_draw(key, shape, scale, limit, cuts=(), kind=jnp.bfloat16):
    level = level_of(key, shape, cuts, -0.22, 0.18) if cuts else 1.0
    entries = jax.random.normal(key, shape, jnp.float32) * scale * level
    return jnp.minimum(jnp.maximum(entries, -limit), limit).astype(kind)


def setup_inputs(seed: int = 0) -> dict:
    seeds = jax.random.split(jax.random.key(seed), 14)
    return {
        "tokens": bell_draw(seeds[0], (MICRO, TOKENS, D), 1.0, 6.0, ((1, 32),), jnp.float32),
        "cotangent": bell_draw(seeds[1], (MICRO, TOKENS, D), 1.0, 6.0, ((1, 32),), jnp.float32),
        "segments": draw_segments(jax.random.fold_in(seeds[13], 71), 0),
        "input_weight": bell_draw(seeds[3], (LAYERS, D, 3 * D), D ** -0.5, 0.25, ((1, 4),)),
        "input_bias": bell_draw(seeds[4], (LAYERS, 3 * D), 0.3, 2.0, ((1, 4),)),
        "output_weight": bell_draw(seeds[5], (LAYERS, D, D), (max(D // 64, 1)) ** -0.5, 2.0, ((1, 4),)),
        "output_bias": bell_draw(seeds[6], (LAYERS, D), 0.3, 2.0, ((1, 4),)),
        "up_weight": bell_draw(seeds[7], (LAYERS, D, FF), D ** -0.5, 0.25, ((1, 4),)),
        "up_bias": bell_draw(seeds[8], (LAYERS, FF), 0.3, 2.0, ((1, 4),)),
        "down_weight": bell_draw(seeds[9], (LAYERS, FF, D), FF ** -0.5, 0.125, ((1, 4),)),
        "down_bias": bell_draw(seeds[10], (LAYERS, D), 0.3, 2.0, ((1, 4),)),
        "norm_gain": jnp.clip(1.0 + 0.1 * jax.random.normal(seeds[11], (LAYERS, 2, D), jnp.float32), 0.5, 1.5).astype(jnp.bfloat16),
        "norm_shift": bell_draw(seeds[12], (LAYERS, 2, D), 0.3, 2.0, ((2, 4),)),
    }


@jax.custom_vjp
def low(v):
    return lax.optimization_barrier(v.astype(jnp.bfloat16)).astype(jnp.float32)

@jax.custom_vjp
def low_back(v):
    return v

def low_keep(v):
    return (low(v), None)

def low_pass(kept, grad):
    return (grad,)

def back_keep(v):
    return (v, None)

def back_low(kept, grad):
    return (low(grad),)
low.defvjp(low_keep, low_pass)
low_back.defvjp(back_keep, back_low)
EPSILON = 1e-05
PRECISE = lax.Precision.HIGHEST

def layer_norm(stream, gain_term, shift_term):
    row_mean = lax.optimization_barrier(jnp.mean(stream, axis=-1, keepdims=True))
    centred = stream - row_mean
    inv_scale = lax.rsqrt(lax.optimization_barrier(jnp.mean(centred * centred, axis=-1, keepdims=True)) + EPSILON)
    return centred * inv_scale * gain_term + shift_term

def block_attention(block_carry, inputs):
    carried, carried_norm, label_id = block_carry
    query_feat, key_feat, values, segment_ids = inputs
    row_count = segment_ids.shape[0]
    causal_order = lax.broadcasted_iota(jnp.int32, (row_count, row_count), 0) >= lax.broadcasted_iota(jnp.int32, (row_count, row_count), 1)
    same_mask = jnp.where(causal_order & (segment_ids[:, None] == segment_ids[None, :]), 1.0, 0.0).astype(jnp.float32)
    scores = jnp.einsum('the,she->hts', query_feat, key_feat, precision=PRECISE) * same_mask[None]
    scores = low_back(scores)
    reads_prior = jnp.where(segment_ids.astype(jnp.float32) == label_id, 1.0, 0.0).astype(jnp.float32)
    numerator = jnp.einsum('hts,she->the', low(scores), values, precision=PRECISE)
    numerator = numerator + reads_prior[:, None, None] * jnp.einsum('the,hef->thf', query_feat, carried, precision=PRECISE)
    numerator = low_back(numerator)
    denominator = lax.optimization_barrier(jnp.sum(scores, axis=2)).T + reads_prior[:, None] * jnp.einsum('the,he->th', query_feat, carried_norm, precision=PRECISE)
    attended = numerator / denominator[:, :, None]
    last_id = segment_ids[-1].astype(jnp.float32)
    keep_last = jnp.where(segment_ids == segment_ids[-1], 1.0, 0.0).astype(jnp.float32)[:, None, None]
    continues = label_id == last_id
    new_state = jnp.where(continues, carried, 0.0) + jnp.einsum('she,shf->hef', key_feat * keep_last, values, precision=PRECISE)
    new_norm = jnp.where(continues, carried_norm, 0.0) + lax.optimization_barrier(jnp.sum(key_feat * keep_last, axis=0))
    return ((new_state, new_norm, last_id), attended)

def to_blocks(source):
    grouped = source.reshape((N_DP, N_SEQ, TOK_DEV) + source.shape[1:])
    return jnp.swapaxes(grouped, 0, 1)

def apply_layer(stream, weights, segment_ids):
    in_weight, in_bias, out_weight, out_bias, up_weight, up_bias, down_weight, down_bias, gains, shifts = weights
    normed_a = low(layer_norm(stream, gains[0], shifts[0]))
    projected = low_back(jnp.dot(normed_a, in_weight, precision=PRECISE)) + in_bias
    projected = projected.reshape(TOKENS, 3, HEADS, HEAD)
    query_feat = low(jax.nn.elu(projected[:, 0]) + 1.0)
    key_feat = low(jax.nn.elu(projected[:, 1]) + 1.0)
    values = low(projected[:, 2])
    start = (jnp.zeros((N_DP, HEADS, HEAD, HEAD), jnp.float32), jnp.zeros((N_DP, HEADS, HEAD), jnp.float32), jnp.full((N_DP,), -1.0, jnp.float32))
    final_carry, attended = lax.scan(jax.checkpoint(jax.vmap(block_attention)), start, (to_blocks(query_feat), to_blocks(key_feat), to_blocks(values), to_blocks(segment_ids)))
    attended = low(jnp.swapaxes(attended, 0, 1).reshape(TOKENS, D))
    middle = stream + low_back(jnp.dot(attended, out_weight, precision=PRECISE)) + out_bias
    normed_b = low(layer_norm(middle, gains[1], shifts[1]))
    hidden = low_back(jnp.dot(normed_b, up_weight, precision=PRECISE)) + up_bias
    active = low(jax.nn.gelu(hidden, approximate=True))
    return middle + low_back(jnp.dot(active, down_weight, precision=PRECISE)) + down_bias

def reference(tokens, cotangent, segments, input_weight, input_bias, output_weight, output_bias, up_weight, up_bias, down_weight, down_bias, norm_gain, norm_shift):
    params = tuple((p.astype(jnp.float32) for p in (input_weight, input_bias, output_weight, output_bias, up_weight, up_bias, down_weight, down_bias, norm_gain, norm_shift)))

    def forward(inputs, *weights):
        results = []
        for member in range(MICRO):
            stream = inputs[member]
            for layer_at in range(LAYERS):
                stream = apply_layer(stream, tuple((w[layer_at] for w in weights)), segments[member])
            results.append(stream)
        return jnp.stack(results)
    result, pullback = jax.vjp(forward, tokens, *params)
    gradients = pullback(cotangent)
    return (result, gradients[0], gradients[1], gradients[2], gradients[3], gradients[4], gradients[5], gradients[6], gradients[7], gradients[8], gradients[9], gradients[10])
```

```python
import jax
import jax.numpy as jnp
from jax import lax
from jax.experimental import pallas as pl
from jax.experimental.pallas import tpu as pltpu
from jax.sharding import PartitionSpec as P

HEAD = 64
EPSILON = 1e-05
F32 = jnp.float32
BF16 = jnp.bfloat16
ROWS = 512
TILE = 128
QUAD = 256
NT = (((1,), (1,)), ((), ()))
TN = (((0,), (0,)), ((), ()))
GELU = 0.7978845608028654
CUBE = 0.044715


def nn(a, b):
    return jnp.dot(a, b, preferred_element_type=F32)


def nt(a, b):
    return lax.dot_general(a, b, NT, preferred_element_type=F32)


def tn(a, b):
    return lax.dot_general(a, b, TN, preferred_element_type=F32)


def norm(x):
    mean = jnp.mean(x, -1, keepdims=True)
    c = x - mean
    r = lax.rsqrt(jnp.mean(c * c, -1, keepdims=True) + EPSILON)
    return c * r, r


def norm_back(u, n, r, gain):
    s = u * gain
    return r * (s - jnp.mean(s, -1, keepdims=True) - n * jnp.mean(s * n, -1, keepdims=True))


def iota(shape, dim):
    return lax.broadcasted_iota(jnp.int32, shape, dim)


def class_of(row, bounds):
    one = jnp.int32(1)
    zero = jnp.int32(0)
    return jnp.where(row >= bounds[0], one, zero) + jnp.where(row >= bounds[1], one, zero)


def head_masks():
    lane = iota((1, QUAD), 1) // HEAD
    return [jnp.where(lane == h, 1.0, 0.0).astype(BF16) for h in range(4)]


def spread(a, masks):
    return jnp.concatenate([a * m for m in masks], 0)


def block_mask():
    return jnp.where(iota((QUAD, QUAD), 0) // HEAD == iota((QUAD, QUAD), 1) // HEAD, 1.0, 0.0).astype(F32)


def same_mask(j, bounds, row_dim):
    t = iota((TILE, TILE), row_dim) + j * TILE
    s = iota((TILE, TILE), 1 - row_dim) + j * TILE
    keep = (s <= t) & (class_of(s, bounds) == class_of(t, bounds))
    return jnp.where(keep, 1.0, 0.0).astype(F32)


def rows_of_class(j, bounds, which, width=QUAD):
    return jnp.where(class_of(iota((TILE, width), 0) + j * TILE, bounds) == which, 1.0, 0.0).astype(F32)


def unpack_state(packed, state, total):
    lane = iota((HEAD, TILE), 1)
    left = jnp.where(lane < HEAD, 1.0, 0.0).astype(F32)
    state[...] = jnp.zeros_like(state)
    for pair in range(4):
        at = pl.ds(pair % 2 * TILE, TILE)
        c = packed[pair * HEAD : (pair + 1) * HEAD, :]
        state[pair // 2, at, at] = jnp.concatenate([c * left, c * (1.0 - left)], 0)
        total[pair // 2, :, at] = jnp.broadcast_to(packed[256 + pair : 257 + pair, :], (8, TILE))


def pack_state(quads, totals, packed):
    lane = iota((HEAD, TILE), 1)
    left = jnp.where(lane < HEAD, 1.0, 0.0).astype(F32)
    for pair in range(4):
        at = pair % 2 * TILE
        block = quads[pair // 2][at : at + TILE, at : at + TILE]
        c = block[:HEAD] * left + block[HEAD:] * (1.0 - left)
        packed[pair * HEAD : (pair + 1) * HEAD, :] = c.astype(BF16)
    lines = [totals[p // 2][:1, p % 2 * TILE : (p % 2 + 1) * TILE] for p in range(4)]
    packed[256:272, :] = jnp.concatenate(lines + [jnp.zeros((12, TILE), F32)], 0).astype(BF16)


def f1_body(x, tab, win, low_a, qkv, st, bounds):
    half = ROWS // 2

    @pl.loop(0, 2)
    def _(i):
        at = pl.ds(pl.multiple_of(i * half, half), half)
        n, _ = norm(x[at, :])
        low = (n * tab[4:5, :512] + tab[6:7, :512]).astype(BF16)
        low_a[at, :] = low
        for c in range(3):
            cols = slice(c * 512, (c + 1) * 512)
            pre = nn(low, win[:, cols]) + tab[0:1, cols]
            if c < 2:
                pre = jnp.where(pre > 0, pre + 1.0, jnp.exp(jnp.minimum(pre, 0.0)))
            qkv[at, cols] = pre.astype(BF16)

    mid = jnp.where(class_of(iota((ROWS, QUAD), 0), bounds) == 1, 1.0, 0.0).astype(BF16)
    ones = jnp.ones((8, ROWS), BF16)
    quads, totals = [], []
    for h in range(2):
        k = qkv[:, 512 + h * QUAD : 512 + (h + 1) * QUAD] * mid
        quads.append(tn(k, qkv[:, 1024 + h * QUAD : 1024 + (h + 1) * QUAD]))
        totals.append(nn(ones, k))
    pack_state(quads, totals, st)


def forward_masks(j, bounds):
    first = j * TILE
    carried = jnp.where(j == 0, jnp.int32(1), class_of(first - 1, bounds))
    last = class_of(first + TILE - 1, bounds)
    go_on = jnp.where(carried == last, 1.0, 0.0).astype(F32)
    return rows_of_class(j, bounds, carried), rows_of_class(j, bounds, last).astype(BF16), go_on


def backward_masks(j, bounds):
    first = j * TILE
    carried = jnp.where(j == ROWS // TILE - 1, jnp.int32(1), class_of(first + TILE, bounds))
    here = class_of(first, bounds)
    go_on = jnp.where(carried == here, 1.0, 0.0).astype(F32)
    return rows_of_class(j, bounds, carried), rows_of_class(j, bounds, here).astype(BF16), go_on


def f2_body(x, qkv, prior, tab, wout, wup, wdn, state, total, att, inv, middle, low_b, act, slope, out, bounds, wait):
    unpack_state(prior, state, total)
    half = ROWS // 2

    @pl.loop(0, ROWS // TILE)
    def _(j):
        at = pl.ds(pl.multiple_of(j * TILE, TILE), TILE)
        masks = head_masks()
        blocks = block_mask()
        ones_block = blocks.astype(BF16)
        same = same_mask(j, bounds, 0)
        same4 = jnp.concatenate([same] * 4, 1)
        reads, keep, go_on = forward_masks(j, bounds)
        ones = jnp.ones((8, TILE), BF16)
        for h in range(2):
            q, k, v = (qkv[at, i * 512 + h * QUAD : i * 512 + (h + 1) * QUAD] for i in range(3))
            s = state[h]
            p = (nt(q, spread(k, masks)) * same4).astype(BF16)
            num = nn(p, spread(v, masks)) + reads * nn(q, s.astype(BF16))
            ksum = nn(same.astype(BF16), k) + reads * total[h, 0:1, :]
            den = nn((q.astype(F32) * ksum).astype(BF16), ones_block)
            r = 1.0 / den
            att[at, h * QUAD : (h + 1) * QUAD] = (num * r).astype(BF16)
            inv[at, h * QUAD : (h + 1) * QUAD] = r
            km = k * keep
            state[h] = go_on * s + tn(km, v) * blocks
            total[h] = go_on * total[h] + nn(ones, km)

    wait("out")

    @pl.loop(0, 2)
    def _(i):
        at = pl.ds(pl.multiple_of(i * half, half), half)
        m = x[at, :] + nn(att[at, :], wout[...]) + tab[1:2, :512]
        middle[at, :] = m
        n, _ = norm(m)
        low_b[at, :] = (n * tab[5:6, :512] + tab[7:8, :512]).astype(BF16)

    wait("up")
    wait("down")

    @pl.loop(0, 2)
    def _(i):
        at = pl.ds(pl.multiple_of(i * half, half), half)
        low = low_b[at, :]
        for c in range(4):
            cols = slice(c * 512, (c + 1) * 512)
            h = nn(low, wup[:, cols]) + tab[2:3, cols]
            h2 = h * h
            t = jnp.tanh(h * (GELU + GELU * CUBE * h2))
            up = 0.5 + 0.5 * t
            act[at, cols] = (h * up).astype(BF16)
            slope[at, cols] = (up + up * (1.0 - t) * h * (GELU + 3.0 * GELU * CUBE * h2)).astype(BF16)
        o = middle[at, :] + tab[3:4, :512]
        for c in range(4):
            o = o + nn(act[at, c * 512 : (c + 1) * 512], down_block(wdn, c))
        out[at, :] = o


def down_block(wdn, c):
    return jnp.concatenate([wdn[c, :, i * 512 : (i + 1) * 512] for i in range(4)], 0)


def b1_body(g, tab, wout, wup, wdn, qkv, att, inv, middle, slope, branch_b, hid, branch_a, dm, dnum, dden, st, small, bounds):
    half = ROWS // 2
    small[...] = jnp.zeros_like(small)

    @pl.loop(0, 2)
    def _(i):
        at = pl.ds(pl.multiple_of(i * half, half), half)
        gi = g[at, :]
        bb = gi.astype(BF16)
        branch_b[at, :] = bb
        for c in range(4):
            cols = slice(c * 512, (c + 1) * 512)
            dh = nt(bb, down_block(wdn, c)) * slope[at, cols].astype(F32)
            hid[at, cols] = dh.astype(BF16)
            small[1:2, cols] += jnp.sum(dh, 0, keepdims=True)
        u = nt(hid[at, :], wup[...])
        n, r = norm(middle[at, :])
        d = gi + norm_back(u, n, r, tab[5:6, :512])
        dm[at, :] = d
        ba = d.astype(BF16)
        branch_a[at, :] = ba
        small[0:1, :512] += jnp.sum(d, 0, keepdims=True)
        small[2:3, :512] += jnp.sum(gi, 0, keepdims=True)
        small[3:4, :512] += jnp.sum(u * n, 0, keepdims=True)
        small[4:5, :512] += jnp.sum(u, 0, keepdims=True)
        da = nt(ba, wout[...])
        ones_block = block_mask().astype(BF16)
        for h in range(2):
            cols = slice(h * QUAD, (h + 1) * QUAD)
            r = inv[at, cols]
            a = da[:, cols]
            dnum[at, cols] = (a * r).astype(BF16)
            dden[at, cols] = -r * nn((a * att[at, cols].astype(F32)).astype(BF16), ones_block)

    mid = jnp.where(class_of(iota((ROWS, QUAD), 0), bounds) == 1, 1.0, 0.0).astype(BF16)
    quads, totals = [], []
    for h in range(2):
        cols = slice(h * QUAD, (h + 1) * QUAD)
        q = qkv[:, cols] * mid
        quads.append(tn(q, dnum[:, cols]))
        totals.append(jnp.sum(q.astype(F32) * dden[:, cols], 0, keepdims=True))
    pack_state(quads, totals, st)


def b2_body(x, dm, qkv, dnum, dden, prior, later, tab, win, state, total, dpre, dx, small, bounds, wait):
    half = ROWS // 2
    count = ROWS // TILE
    small[...] = jnp.zeros_like(small)
    unpack_state(prior, state, total)

    @pl.loop(0, count)
    def _(j):
        at = pl.ds(pl.multiple_of(j * TILE, TILE), TILE)
        masks = head_masks()
        blocks = block_mask()
        same = same_mask(j, bounds, 0)
        same4 = jnp.concatenate([same] * 4, 1)
        reads, keep, go_on = forward_masks(j, bounds)
        ones = jnp.ones((8, TILE), BF16)
        for h in range(2):
            cols = slice(h * QUAD, (h + 1) * QUAD)
            q, k, v = (qkv[at, i * 512 + h * QUAD : i * 512 + (h + 1) * QUAD] for i in range(3))
            dn = dnum[at, cols]
            s = state[h]
            ds = (nt(dn, spread(v, masks)) * same4).astype(BF16)
            ksum = nn(same.astype(BF16), k) + reads * total[h, 0:1, :]
            dq = nn(ds, spread(k, masks)) + reads * nt(dn, s.astype(BF16)) + dden[at, cols] * ksum
            dq = dq * jnp.minimum(q.astype(F32), 1.0)
            dpre[at, cols] = dq.astype(BF16)
            small[0:1, cols] += jnp.sum(dq, 0, keepdims=True)
            km = k * keep
            state[h] = go_on * s + tn(km, v) * blocks
            total[h] = go_on * total[h] + nn(ones, km)

    unpack_state(later, state, total)

    @pl.loop(0, count)
    def _(back):
        j = count - 1 - back
        at = pl.ds(pl.multiple_of(j * TILE, TILE), TILE)
        masks = head_masks()
        blocks = block_mask()
        same = same_mask(j, bounds, 1)
        same4 = jnp.concatenate([same] * 4, 1)
        reads, keep, go_on = backward_masks(j, bounds)
        ones = jnp.ones((8, TILE), BF16)
        for h in range(2):
            cols = slice(h * QUAD, (h + 1) * QUAD)
            q, k, v = (qkv[at, i * 512 + h * QUAD : i * 512 + (h + 1) * QUAD] for i in range(3))
            dn = dnum[at, cols]
            s = state[h]
            low = s.astype(BF16)
            qx = spread(q, masks)
            dx_ = spread(dn, masks)
            sc = (nt(k, qx) * same4).astype(BF16)
            ds = (nt(v, dx_) * same4).astype(BF16)
            dv = nn(sc, dx_) + reads * nn(k, low)
            dd = (dden[at, cols] * q.astype(F32)).astype(BF16)
            dk = nn(ds, qx) + reads * (nt(v, low) + total[h, 0:1, :]) + nn(same.astype(BF16), dd)
            dk = dk * jnp.minimum(k.astype(F32), 1.0)
            kc = slice(512 + h * QUAD, 512 + (h + 1) * QUAD)
            vc = slice(1024 + h * QUAD, 1024 + (h + 1) * QUAD)
            dpre[at, kc] = dk.astype(BF16)
            dpre[at, vc] = dv.astype(BF16)
            small[0:1, kc] += jnp.sum(dk, 0, keepdims=True)
            small[0:1, vc] += jnp.sum(dv, 0, keepdims=True)
            state[h] = go_on * s + tn(q * keep, dn) * blocks
            total[h] = go_on * total[h] + nn(ones, dd * keep)

    wait("in")

    @pl.loop(0, 2)
    def _(i):
        at = pl.ds(pl.multiple_of(i * half, half), half)
        u = nt(dpre[at, :], win[...])
        n, r = norm(x[at, :])
        dx[at, :] = dm[at, :] + norm_back(u, n, r, tab[4:5, :512])
        small[1:2, :512] += jnp.sum(u * n, 0, keepdims=True)
        small[2:3, :512] += jnp.sum(u, 0, keepdims=True)


WEIGHT_SHAPES = {"in": (512, 1536), "out": (512, 512), "up": (512, 2048), "down": (4, 128, 2048)}
VMEM_LIMIT = 56 * 1024 * 1024


def flip(dp, j):
    if j % 2:
        dp = dp + 1 - 2 * (dp % 2)
    if j // 2:
        dp = (dp + 2) % 4
    return dp


def call(body, bounds, tab, ins, weights, outs, scratch, flops, moved):
    in_names, weight_names, out_names = list(ins), list(weights), list(outs)
    chunks = []
    for chunk, _ in weights.values():
        if not any(chunk is c for c in chunks):
            chunks.append(chunk)
    flat = [a for c in chunks for a in c]
    slots = {n: 2 * i for i, n in enumerate(in_names + out_names)}
    first_weight = 2 * len(slots)
    micros = 2

    def kernel(bounds_ref, tab_ref, *refs):
        refs = list(refs)
        take = lambda n: [refs.pop(0) for _ in range(n)]
        src = dict(zip(in_names, take(len(ins))))
        pieces = take(len(flat))
        dst = dict(zip(out_names, take(len(outs))))
        full = dict(zip(in_names, take(len(ins))))
        held = dict(zip(weight_names, take(len(weights))))
        full.update(zip(out_names, take(len(outs))))
        held.update(zip(scratch, take(len(scratch))))
        sems = refs.pop(0)
        dp = lax.axis_index("dp")

        def arriving(name, m):
            return pltpu.make_async_copy(src[name].at[m], full[name].at[m], sems.at[slots[name] + m])

        def leaving(name, m):
            return pltpu.make_async_copy(full[name].at[m], dst[name].at[m], sems.at[slots[name] + m])

        pending = {}
        for m in range(micros):
            for name in in_names:
                arriving(name, m).start()
            if m:
                continue
            for w, name in enumerate(weight_names):
                chunk, column = weights[name]
                base = 0
                for c in chunks:
                    if c is chunk:
                        break
                    base += len(c)
                width = 2048 if name == "down" else WEIGHT_SHAPES[name][1]
                for j in range(4):
                    owner = flip(dp, j)
                    piece = pieces[base + j].at[pl.ds(0, 128), pl.ds(column, width)]
                    target = held[name].at[owner] if name == "down" else held[name].at[pl.ds(pl.multiple_of(owner * 128, 128), 128), :]
                    copy = pltpu.make_async_copy(piece, target, sems.at[first_weight + 4 * w + j])
                    copy.start()
                    pending.setdefault(name, []).append(copy)

        @pl.loop(0, micros)
        def _(m):
            env = {n: r.at[m] for n, r in full.items()}
            env.update(held)

            def wait(*names):
                for name in names:
                    if name in pending:

                        @pl.when(m == 0)
                        def _():
                            for copy in pending[name]:
                                copy.wait()

                    else:
                        arriving(name, m).wait()

            def done(*names):
                for name in names:
                    leaving(name, m).start()

            body(env, wait, done, (bounds_ref[m, 0], bounds_ref[m, 1]), tab_ref)

        for m in range(micros):
            for name in out_names:
                leaving(name, m).wait()

    hbm = pl.BlockSpec(memory_space=pl.ANY)
    shapes = [pltpu.VMEM(a.shape, a.dtype) for a in ins.values()]
    shapes += [pltpu.VMEM(WEIGHT_SHAPES[w], BF16) for w in weight_names]
    shapes += [pltpu.VMEM((micros,) + s.shape, s.dtype) for s in outs.values()] + [pltpu.VMEM(s.shape, s.dtype) for s in scratch.values()]
    shapes.append(pltpu.SemaphoreType.DMA((first_weight + 4 * len(weights),)))
    results = pl.pallas_call(
        kernel,
        out_shape=[jax.ShapeDtypeStruct((micros,) + s.shape, s.dtype) for s in outs.values()],
        in_specs=[pl.BlockSpec(memory_space=pltpu.SMEM), pl.BlockSpec(memory_space=pltpu.VMEM)] + [hbm] * (len(ins) + len(flat)),
        out_specs=[hbm] * len(outs),
        scratch_shapes=shapes,
        compiler_params=pltpu.CompilerParams(vmem_limit_bytes=VMEM_LIMIT),
        cost_estimate=pl.CostEstimate(flops=int(flops), bytes_accessed=int(moved), transcendentals=0),
    )(bounds, tab, *ins.values(), *flat)
    return dict(zip(out_names, results))


def shape(rows, columns, kind):
    return jax.ShapeDtypeStruct((rows, columns), kind)


WIDE = shape(512, 512, F32)
NARROW = shape(512, 512, BF16)
TRIPLE = shape(512, 1536, BF16)
FOUR = shape(512, 2048, BF16)
STATE = shape(272, 128, BF16)
SMALL = shape(8, 2048, F32)
CARRY = {"state": jax.ShapeDtypeStruct((2, QUAD, QUAD), F32), "total": jax.ShapeDtypeStruct((2, 8, QUAD), F32)}


def enter(bounds, tab, x, w):
    def body(e, wait, done, bounds, tab):
        wait("x", "in")
        f1_body(e["x"], tab.at[0:8], e["in"], e["low_a"], e["qkv"], e["st"], bounds)
        done("low_a", "qkv", "st")

    return call(body, bounds, tab, {"x": x}, {"in": w["in"]}, {"low_a": NARROW, "qkv": TRIPLE, "st": STATE}, {}, 3e9, 8e6)


def inner(bounds, tab, x, qkv, prior, w, w_next):
    def body(e, wait, done, bounds, tab):
        here, there = tab.at[0:8], tab.at[8:16]
        wait("qkv", "prior", "x")
        f2_body(e["x"], e["qkv"], e["prior"], here, e["out"], e["up"], e["down"], e["state"], e["total"], e["att"], e["inv"], e["middle"], e["low_b"], e["act"], e["slope"], e["x1"], bounds, wait)
        done("att", "inv", "middle", "low_b", "act", "slope", "x1")
        wait("in")
        f1_body(e["x1"], there, e["in"], e["low_a"], e["qkv1"], e["st"], bounds)
        done("low_a", "qkv1", "st")

    outs = {"att": NARROW, "inv": WIDE, "middle": WIDE, "low_b": NARROW, "act": FOUR, "slope": FOUR, "x1": WIDE, "low_a": NARROW, "qkv1": TRIPLE, "st": STATE}
    return call(body, bounds, tab, {"qkv": qkv, "prior": prior, "x": x}, {"out": w["out"], "up": w["up"], "down": w["down"], "in": w_next["in"]}, outs, CARRY, 25e9, 32e6)


def turn(bounds, tab, x, qkv, prior, g, w):
    def body(e, wait, done, bounds, tab):
        tab = tab.at[8:16]
        wait("qkv", "prior", "x")
        f2_body(e["x"], e["qkv"], e["prior"], tab, e["out"], e["up"], e["down"], e["state"], e["total"], e["att"], e["inv"], e["middle"], e["low_b"], e["act"], e["slope"], e["y"], bounds, wait)
        done("y", "att", "low_b", "act")
        wait("g")
        b1_body(e["g"], tab, e["out"], e["up"], e["down"], e["qkv"], e["att"], e["inv"], e["middle"], e["slope"], e["bb"], e["hid"], e["ba"], e["dm"], e["dnum"], e["dden"], e["st"], e["small"], bounds)
        done("bb", "hid", "ba", "dm", "dnum", "dden", "st", "small")

    outs = {"y": WIDE, "att": NARROW, "low_b": NARROW, "act": FOUR, "bb": NARROW, "hid": FOUR, "ba": NARROW, "dm": WIDE, "dnum": NARROW, "dden": WIDE, "st": STATE, "small": SMALL}
    scratch = {"inv": WIDE, "middle": WIDE, "slope": FOUR, **CARRY}
    return call(body, bounds, tab, {"qkv": qkv, "prior": prior, "x": x, "g": g}, {"out": w["out"], "up": w["up"], "down": w["down"]}, outs, scratch, 30e9, 36e6)


def between(bounds, tab, x, dm, qkv, dnum, dden, prior, later, w_in, qkv_low, att, inv, middle, slope, w):
    def body(e, wait, done, bounds, tab):
        here, there = tab.at[8:16], tab.at[0:8]
        wait("qkv", "dnum", "dden", "prior", "later", "dm", "x")
        b2_body(e["x"], e["dm"], e["qkv"], e["dnum"], e["dden"], e["prior"], e["later"], here, e["in"], e["state"], e["total"], e["dpre"], e["dx"], e["small2"], bounds, wait)
        done("dpre", "small2")
        wait("slope", "middle", "inv", "att", "low_qkv", "out", "up", "down")
        b1_body(e["dx"], there, e["out"], e["up"], e["down"], e["low_qkv"], e["att"], e["inv"], e["middle"], e["slope"], e["bb"], e["hid"], e["ba"], e["dm1"], e["dnum1"], e["dden1"], e["st"], e["small"], bounds)
        done("bb", "hid", "ba", "dm1", "dnum1", "dden1", "st", "small")

    ins = {"qkv": qkv, "dnum": dnum, "dden": dden, "prior": prior, "later": later, "dm": dm, "x": x, "slope": slope, "middle": middle, "inv": inv, "att": att, "low_qkv": qkv_low}
    outs = {"dpre": TRIPLE, "small2": SMALL, "bb": NARROW, "hid": FOUR, "ba": NARROW, "dm1": WIDE, "dnum1": NARROW, "dden1": WIDE, "st": STATE, "small": SMALL}
    return call(body, bounds, tab, ins, {"in": w_in["in"], "out": w["out"], "up": w["up"], "down": w["down"]}, outs, {"dx": WIDE, **CARRY}, 30e9, 42e6)


def leave(bounds, tab, x, dm, qkv, dnum, dden, prior, later, w):
    def body(e, wait, done, bounds, tab):
        wait("qkv", "dnum", "dden", "prior", "later", "dm", "x")
        b2_body(e["x"], e["dm"], e["qkv"], e["dnum"], e["dden"], e["prior"], e["later"], tab.at[0:8], e["in"], e["state"], e["total"], e["dpre"], e["dx"], e["small2"], bounds, wait)
        done("dpre", "dx", "small2")

    ins = {"qkv": qkv, "dnum": dnum, "dden": dden, "prior": prior, "later": later, "dm": dm, "x": x}
    return call(body, bounds, tab, ins, {"in": w["in"]}, {"dpre": TRIPLE, "dx": WIDE, "small2": SMALL}, CARRY, 15e9, 20e6)


PACKED = {"in": 1536, "out": 512, "up": 2048, "down": 2048}
SMALL_ROWS = 32


def small_lines(smalls, owner):
    lines = []
    for layer in range(2):
        first, second = smalls[2 * layer], smalls[2 * layer + 1]
        for ref, row, width in ((second, 0, 384), (first, 0, 128), (first, 1, 512), (first, 2, 128), (second, 1, 128), (first, 3, 128), (second, 2, 128), (first, 4, 128)):
            for i in range(width // 128):
                at = pl.ds(pl.multiple_of(owner * width + i * 128, 128), 128)
                lines.append(ref[0, row : row + 1, at] + ref[1, row : row + 1, at])
    return jnp.concatenate(lines + [jnp.zeros((SMALL_ROWS - len(lines), 128), F32)], 0)


def weight_grads(parts, smalls, got):
    keep = got is not None
    n = len(parts)
    extra = [128 if smalls is not None and i == n - 1 else 0 for i in range(n)]
    columns = [PACKED[name] + extra[i] for i, (name, _, _) in enumerate(parts)]
    n_small = len(smalls) if smalls is not None else 0

    def kernel(*refs):
        refs = list(refs)
        take = lambda k: [refs.pop(0) for _ in range(k)]
        a_src, b_src, got_src = take(n), take(n), take(n if keep else 0)
        small_refs = take(n_small)
        out_near = take(n)
        out_far = take(n if keep else 0)
        a_buf, b_buf, got_buf = take(n), take(n), take(n if keep else 0)
        near_buf = take(n)
        far_buf = take(n if keep else 0)
        sems = refs.pop(0)
        dp = lax.axis_index("dp")
        owners = [flip(dp, j) for j in ((0, 2) if keep else (1, 3))]
        used = 0
        pending = []
        for i, (name, _, _) in enumerate(parts):
            part = 512 if name == "down" else 128
            copies = [(b_src[i], b_buf[i])]
            if keep:
                copies.append((got_src[i], got_buf[i]))
            for e, owner in enumerate(owners):
                copies.append((a_src[i].at[:, :, pl.ds(pl.multiple_of(owner * part, 128), part)], a_buf[i].at[e]))
            pending.append([])
            for s, d in copies:
                copy = pltpu.make_async_copy(s, d, sems.at[used])
                copy.start()
                pending[-1].append(copy)
                used += 1
        leaving = []
        for i, (name, _, _) in enumerate(parts):
            for copy in pending[i]:
                copy.wait()
            width = PACKED[name]
            for e in range(2):

                def put(cols, value):
                    if keep:
                        value = value + got_buf[i][e, :, cols].astype(F32)
                        if e == 0:
                            near_buf[i][:, cols] = value
                        else:
                            far_buf[i][:, cols] = value.astype(BF16)
                    else:
                        near_buf[i][e, :, cols] = value.astype(BF16)

                if name == "down":
                    for b in range(4):
                        cols = slice(b * 128, (b + 1) * 128)
                        value = tn(a_buf[i][e, 0, :, cols], b_buf[i][0]) + tn(a_buf[i][e, 1, :, cols], b_buf[i][1])
                        put(slice(b * 512, (b + 1) * 512), value)
                else:
                    for c in range(width // 512):
                        cols = slice(c * 512, (c + 1) * 512)
                        put(cols, tn(a_buf[i][e, 0], b_buf[i][0, :, cols]) + tn(a_buf[i][e, 1], b_buf[i][1, :, cols]))
                if extra[i]:
                    lines = small_lines(small_refs, owners[e])
                    put(slice(width, width + 128), jnp.concatenate([lines, jnp.zeros((128 - SMALL_ROWS, 128), F32)], 0))
            for buf, out in [(near_buf[i], out_near[i])] + ([(far_buf[i], out_far[i])] if keep else []):
                copy = pltpu.make_async_copy(buf, out, sems.at[used])
                copy.start()
                leaving.append(copy)
                used += 1
        for copy in leaving:
            copy.wait()

    hbm = pl.BlockSpec(memory_space=pl.ANY)
    vmem = pl.BlockSpec(memory_space=pltpu.VMEM)
    if keep:
        outs = [jax.ShapeDtypeStruct((128, c), F32) for c in columns] + [jax.ShapeDtypeStruct((128, c), BF16) for c in columns]
    else:
        outs = [jax.ShapeDtypeStruct((2, 128, c), BF16) for c in columns]
    a_parts = [(2, 2, 512, 512 if name == "down" else 128) for name, _, _ in parts]
    scratch = [pltpu.VMEM(s, BF16) for s in a_parts] + [pltpu.VMEM(b.shape, BF16) for _, _, b in parts]
    if keep:
        scratch += [pltpu.VMEM(g.shape, BF16) for g in got]
    scratch += [pltpu.VMEM(o.shape, o.dtype) for o in outs]
    scratch.append(pltpu.SemaphoreType.DMA((8 * n,)))
    flops = sum(2 * 1024 * 256 * c for c in columns)
    results = pl.pallas_call(
        kernel,
        out_shape=outs,
        in_specs=[hbm] * (2 * n + (n if keep else 0)) + [vmem] * n_small,
        out_specs=[hbm] * len(outs),
        scratch_shapes=scratch,
        compiler_params=pltpu.CompilerParams(vmem_limit_bytes=VMEM_LIMIT),
        cost_estimate=pl.CostEstimate(flops=4 * flops, bytes_accessed=sum(6 * 128 * c for c in columns), transcendentals=0),
    )(*[a for _, a, _ in parts], *[b for _, _, b in parts], *(got or []), *(smalls or []))
    return results if not keep else (results[:n], results[n:])


def swap(x, axis, bit):
    n = lax.axis_size(axis)
    return lax.ppermute(x, axis, [(i, i ^ bit) for i in range(n)])


def tied(x, *after):
    return lax.optimization_barrier((x,) + after)[0]


def absolute(pieces, dp):
    stacked = jnp.stack(pieces)
    return jnp.stack([lax.dynamic_index_in_dim(stacked, dp ^ j, 0, False) for j in range(4)])


def prefix_sums(x, forward):
    n = lax.axis_size("seq")
    place = lax.axis_index("seq")
    total, result, bit = x, 0.0, 1
    while bit < n:
        got = swap(total, "seq", bit).astype(F32)
        high = (place // bit) % 2 == 1
        result = result + jnp.where(high if forward else ~high, got, 0.0)
        total = (total.astype(F32) + got).astype(BF16)
        bit *= 2
    return result


def reduce_start(near, far):
    y = lax.axis_index("seq") % 2
    near = near + swap(far, "dp", 2).astype(F32)
    half = near.shape[0] // 2
    mine = lax.dynamic_slice_in_dim(near, y * half, half, 0)
    other = lax.dynamic_slice_in_dim(near, (1 - y) * half, half, 0).astype(BF16)
    return (mine + swap(other, "seq", 1).astype(F32)).astype(BF16)


def reduce_end(part):
    n = lax.axis_size("seq")
    bit = 2
    while bit < n:
        part = (part.astype(F32) + swap(part, "seq", bit).astype(F32)).astype(BF16)
        bit *= 2
    other = swap(part, "seq", 1)
    y = lax.axis_index("seq") % 2
    return jnp.where(y == 0, jnp.concatenate([part, other]), jnp.concatenate([other, part])).astype(F32)


def wide(v):
    return jnp.pad(v, (0, 2048 - v.shape[0]))


def per_device(tokens, cotangent, segments, input_weight, input_bias, output_weight, output_bias, up_weight, up_bias, down_weight, down_bias, norm_gain, norm_shift):
    dp = lax.axis_index("dp")
    middle_id = 3 * dp + 1
    bounds = jnp.stack([jnp.sum((segments < middle_id).astype(jnp.int32), 1), jnp.sum((segments <= middle_id).astype(jnp.int32), 1)], 1)
    flat = jnp.concatenate([input_bias[0], input_bias[1], up_bias[0], output_bias[0], output_bias[1], up_bias[1], down_bias[0], down_bias[1], norm_gain.reshape(-1), jnp.zeros((256,), BF16), norm_shift.reshape(-1), jnp.zeros((1024,), BF16)])
    blocks = lambda l: [down_weight[l][i * 128 : (i + 1) * 128] for i in range(4)]
    first = jnp.concatenate([input_weight[0], flat.reshape(3, 1536), jnp.zeros((13, 1536), BF16)])
    rest = jnp.concatenate([output_weight[0], up_weight[0]] + blocks(0), 1)
    last = jnp.concatenate([output_weight[1], up_weight[1]] + blocks(1), 1)
    across = []
    shards = [first, rest, input_weight[1], last]
    for i, s in enumerate(shards):
        if across:
            s = shards[i] = tied(s, across[-1])
        across.append(swap(s, "dp", 2))
    pieces = []
    for s, a in zip(shards, across):
        pieces.append([s, swap(s, "dp", 1), a, swap(a, "dp", 1)])
    ws = [
        {"in": (pieces[0], 0), "out": (pieces[1], 0), "up": (pieces[1], 512), "down": (pieces[1], 2560)},
        {"in": (pieces[2], 0), "out": (pieces[3], 0), "up": (pieces[3], 512), "down": (pieces[3], 2560)},
    ]
    sm = absolute([p[128:131] for p in pieces[0]], dp).astype(F32)
    g = lambda r, a, b: sm[:, r, a:b].reshape(-1)
    gains = sm[:, 1, 768:1280].reshape(4, 4, 128).transpose(1, 0, 2).reshape(4, 512)
    shifts = sm[:, 2, 0:512].reshape(4, 4, 128).transpose(1, 0, 2).reshape(4, 512)
    tab = jnp.stack(
        [wide(g(0, 0, 384)), wide(g(0, 1280, 1408)), wide(g(0, 768, 1280)), wide(g(1, 512, 640)), wide(gains[0]), wide(gains[1]), wide(shifts[0]), wide(shifts[1])]
        + [wide(g(0, 384, 768)), wide(g(0, 1408, 1536)), wide(g(1, 0, 512)), wide(g(1, 640, 768)), wide(gains[2]), wide(gains[3]), wide(shifts[2]), wide(shifts[3])]
    )
    e = enter(bounds, tab, tokens, ws[0])
    prior0 = prefix_sums(e["st"], True)
    i = inner(bounds, tab, tokens, e["qkv"], prior0, ws[0], ws[1])
    prior1 = prefix_sums(i["st"], True)
    t = turn(bounds, tab, i["x1"], i["qkv1"], prior1, cotangent, ws[1])
    later1 = prefix_sums(t["st"], False)

    def cores(parts, smalls=None):
        sent = weight_grads(parts, smalls, None)
        return weight_grads(parts, smalls, [swap(s, "dp", 1) for s in sent])

    near_a, far_a = cores([("down", t["act"], t["bb"]), ("up", t["low_b"], t["hid"]), ("out", t["att"], t["ba"])])
    b = between(bounds, tab, i["x1"], t["dm"], i["qkv1"], t["dnum"], t["dden"], prior1, later1, ws[1], e["qkv"], i["att"], i["inv"], i["middle"], i["slope"], ws[0])
    later0 = prefix_sums(b["st"], False)
    near_b, far_b = cores([("in", i["low_a"], b["dpre"]), ("down", i["act"], b["bb"]), ("up", i["low_b"], b["hid"]), ("out", i["att"], b["ba"])])
    v = leave(bounds, tab, tokens, b["dm1"], e["qkv"], b["dnum1"], b["dden1"], prior0, later0, ws[0])
    near_c, far_c = cores([("in", e["low_a"], v["dpre"])], [b["small"], v["small2"], t["small"], b["small2"]])
    down1, up1, out1 = [reduce_end(reduce_start(*p)) for p in zip(near_a, far_a)]
    in1, down0, up0, out0 = [reduce_end(reduce_start(*p)) for p in zip(near_b, far_b)]
    (in0,) = [reduce_end(reduce_start(*p)) for p in zip(near_c, far_c)]
    lines = in0[:SMALL_ROWS, 1536:].reshape(-1)
    layers = []
    for l in range(2):
        at, got = l * 1664, []
        for width in (384, 128, 512, 128, 128, 128, 128, 128):
            got.append(lines[at : at + width])
            at += width
        layers.append(got)
    small = lambda k: jnp.stack([layers[l][k] for l in range(2)])
    stacked = lambda d: jnp.concatenate([d[:, c * 512 : (c + 1) * 512] for c in range(4)])
    return (
        t["y"],
        v["dx"],
        jnp.stack([in0[:, :1536], in1]),
        small(0),
        jnp.stack([out0, out1]),
        small(1),
        jnp.stack([up0, up1]),
        small(2),
        jnp.stack([stacked(down0), stacked(down1)]),
        small(3),
        jnp.stack([small(4), small(5)], 1),
        jnp.stack([small(6), small(7)], 1),
    )


def solution(mesh):
    rows = P(None, ("dp", "seq"), None)
    split = P(None, "dp", None)
    flat = P(None, "dp")
    last = P(None, None, "dp")
    params = (split, flat, split, flat, split, flat, split, flat, last, last)
    return jax.shard_map(
        per_device,
        mesh=mesh,
        in_specs=(rows, rows, P(None, ("dp", "seq"))) + params,
        out_specs=(rows, rows) + params,
        check_vma=False,
    )
```

```python
import jax
import jax.numpy as jnp
from jax import lax
from jax.experimental import pallas as pl
from jax.experimental.pallas import tpu as pltpu
from jax.sharding import PartitionSpec as P

HEAD = 64
EPSILON = 1e-05
F32 = jnp.float32
BF16 = jnp.bfloat16
ROWS = 512
TILE = 128
QUAD = 256
NT = (((1,), (1,)), ((), ()))
TN = (((0,), (0,)), ((), ()))
GELU = 0.7978845608028654
CUBE = 0.044715


def nn(a, b):
    return jnp.dot(a, b, preferred_element_type=F32)


def nt(a, b):
    return lax.dot_general(a, b, NT, preferred_element_type=F32)


def tn(a, b):
    return lax.dot_general(a, b, TN, preferred_element_type=F32)


def norm(x):
    mean = jnp.mean(x, -1, keepdims=True)
    c = x - mean
    r = lax.rsqrt(jnp.mean(c * c, -1, keepdims=True) + EPSILON)
    return c * r, r


def norm_back(u, n, r, gain):
    s = u * gain
    return r * (s - jnp.mean(s, -1, keepdims=True) - n * jnp.mean(s * n, -1, keepdims=True))


def iota(shape, dim):
    return lax.broadcasted_iota(jnp.int32, shape, dim)


def class_of(row, bounds):
    one = jnp.int32(1)
    zero = jnp.int32(0)
    return jnp.where(row >= bounds[0], one, zero) + jnp.where(row >= bounds[1], one, zero)


def head_masks():
    lane = iota((1, QUAD), 1) // HEAD
    return [jnp.where(lane == h, 1.0, 0.0).astype(BF16) for h in range(4)]


def spread(a, masks):
    return jnp.concatenate([a * m for m in masks], 0)


def block_mask():
    return jnp.where(iota((QUAD, QUAD), 0) // HEAD == iota((QUAD, QUAD), 1) // HEAD, 1.0, 0.0).astype(F32)


def same_mask(j, bounds, row_dim):
    t = iota((TILE, TILE), row_dim) + j * TILE
    s = iota((TILE, TILE), 1 - row_dim) + j * TILE
    keep = (s <= t) & (class_of(s, bounds) == class_of(t, bounds))
    return jnp.where(keep, 1.0, 0.0).astype(F32)


def rows_of_class(j, bounds, which, width=QUAD):
    return jnp.where(class_of(iota((TILE, width), 0) + j * TILE, bounds) == which, 1.0, 0.0).astype(F32)


def unpack_state(packed, state, total):
    lane = iota((HEAD, TILE), 1)
    left = jnp.where(lane < HEAD, 1.0, 0.0).astype(F32)
    state[...] = jnp.zeros_like(state)
    for pair in range(4):
        at = pl.ds(pair % 2 * TILE, TILE)
        c = packed[pair * HEAD : (pair + 1) * HEAD, :]
        state[pair // 2, at, at] = jnp.concatenate([c * left, c * (1.0 - left)], 0)
        total[pair // 2, :, at] = jnp.broadcast_to(packed[256 + pair : 257 + pair, :], (8, TILE))


def pack_state(quads, totals, packed):
    lane = iota((HEAD, TILE), 1)
    left = jnp.where(lane < HEAD, 1.0, 0.0).astype(F32)
    for pair in range(4):
        at = pair % 2 * TILE
        block = quads[pair // 2][at : at + TILE, at : at + TILE]
        c = block[:HEAD] * left + block[HEAD:] * (1.0 - left)
        packed[pair * HEAD : (pair + 1) * HEAD, :] = c.astype(BF16)
    lines = [totals[p // 2][:1, p % 2 * TILE : (p % 2 + 1) * TILE] for p in range(4)]
    packed[256:272, :] = jnp.concatenate(lines + [jnp.zeros((12, TILE), F32)], 0).astype(BF16)


def f1_body(x, tab, win, low_a, qkv, st, bounds):
    half = ROWS // 2

    @pl.loop(0, 2, unroll=True)
    def _(i):
        at = pl.ds(pl.multiple_of(i * half, half), half)
        n, _ = norm(x[at, :])
        low = (n * tab[4:5, :512] + tab[6:7, :512]).astype(BF16)
        low_a[at, :] = low
        for c in range(3):
            cols = slice(c * 512, (c + 1) * 512)
            pre = nn(low, win[:, cols]) + tab[0:1, cols]
            if c < 2:
                pre = jnp.where(pre > 0, pre + 1.0, jnp.exp(jnp.minimum(pre, 0.0)))
            qkv[at, cols] = pre.astype(BF16)

    mid = jnp.where(class_of(iota((ROWS, QUAD), 0), bounds) == 1, 1.0, 0.0).astype(BF16)
    ones = jnp.ones((8, ROWS), BF16)
    quads, totals = [], []
    for h in range(2):
        k = qkv[:, 512 + h * QUAD : 512 + (h + 1) * QUAD] * mid
        quads.append(tn(k, qkv[:, 1024 + h * QUAD : 1024 + (h + 1) * QUAD]))
        totals.append(nn(ones, k))
    pack_state(quads, totals, st)


def forward_masks(j, bounds):
    first = j * TILE
    carried = jnp.where(j == 0, jnp.int32(1), class_of(first - 1, bounds))
    last = class_of(first + TILE - 1, bounds)
    go_on = jnp.where(carried == last, 1.0, 0.0).astype(F32)
    return rows_of_class(j, bounds, carried), rows_of_class(j, bounds, last).astype(BF16), go_on


def backward_masks(j, bounds):
    first = j * TILE
    carried = jnp.where(j == ROWS // TILE - 1, jnp.int32(1), class_of(first + TILE, bounds))
    here = class_of(first, bounds)
    go_on = jnp.where(carried == here, 1.0, 0.0).astype(F32)
    return rows_of_class(j, bounds, carried), rows_of_class(j, bounds, here).astype(BF16), go_on


def f2_body(x, qkv, prior, tab, wout, wup, wdn, state, total, att, inv, middle, low_b, act, slope, out, bounds, wait):
    unpack_state(prior, state, total)
    half = ROWS // 2

    @pl.loop(0, ROWS // TILE, unroll=True)
    def _(j):
        at = pl.ds(pl.multiple_of(j * TILE, TILE), TILE)
        masks = head_masks()
        blocks = block_mask()
        ones_block = blocks.astype(BF16)
        same = same_mask(j, bounds, 0)
        same4 = jnp.concatenate([same] * 4, 1)
        reads, keep, go_on = forward_masks(j, bounds)
        ones = jnp.ones((8, TILE), BF16)
        for h in range(2):
            q, k, v = (qkv[at, i * 512 + h * QUAD : i * 512 + (h + 1) * QUAD] for i in range(3))
            s = state[h]
            p = (nt(q, spread(k, masks)) * same4).astype(BF16)
            num = nn(p, spread(v, masks)) + reads * nn(q, s.astype(BF16))
            ksum = nn(same.astype(BF16), k) + reads * total[h, 0:1, :]
            den = nn((q.astype(F32) * ksum).astype(BF16), ones_block)
            r = 1.0 / den
            att[at, h * QUAD : (h + 1) * QUAD] = (num * r).astype(BF16)
            inv[at, h * QUAD : (h + 1) * QUAD] = r
            km = k * keep
            state[h] = go_on * s + tn(km, v) * blocks
            total[h] = go_on * total[h] + nn(ones, km)

    wait("out")

    @pl.loop(0, 2, unroll=True)
    def _(i):
        at = pl.ds(pl.multiple_of(i * half, half), half)
        m = x[at, :] + nn(att[at, :], wout[...]) + tab[1:2, :512]
        middle[at, :] = m
        n, _ = norm(m)
        low_b[at, :] = (n * tab[5:6, :512] + tab[7:8, :512]).astype(BF16)

    wait("up")
    wait("down")

    @pl.loop(0, 2, unroll=True)
    def _(i):
        at = pl.ds(pl.multiple_of(i * half, half), half)
        low = low_b[at, :]
        for c in range(4):
            cols = slice(c * 512, (c + 1) * 512)
            h = nn(low, wup[:, cols]) + tab[2:3, cols]
            h2 = h * h
            t = jnp.tanh(h * (GELU + GELU * CUBE * h2))
            up = 0.5 + 0.5 * t
            act[at, cols] = (h * up).astype(BF16)
            slope[at, cols] = (up + up * (1.0 - t) * h * (GELU + 3.0 * GELU * CUBE * h2)).astype(BF16)
        o = middle[at, :] + tab[3:4, :512]
        for c in range(4):
            o = o + nn(act[at, c * 512 : (c + 1) * 512], down_block(wdn, c))
        out[at, :] = o


def down_block(wdn, c):
    return jnp.concatenate([wdn[c, :, i * 512 : (i + 1) * 512] for i in range(4)], 0)


def b1_body(g, tab, wout, wup, wdn, qkv, att, inv, middle, slope, branch_b, hid, branch_a, dm, dnum, dden, st, small, bounds):
    half = ROWS // 2
    small[...] = jnp.zeros_like(small)

    @pl.loop(0, 2, unroll=True)
    def _(i):
        at = pl.ds(pl.multiple_of(i * half, half), half)
        gi = g[at, :]
        bb = gi.astype(BF16)
        branch_b[at, :] = bb
        for c in range(4):
            cols = slice(c * 512, (c + 1) * 512)
            dh = nt(bb, down_block(wdn, c)) * slope[at, cols].astype(F32)
            hid[at, cols] = dh.astype(BF16)
            small[1:2, cols] += jnp.sum(dh, 0, keepdims=True)
        u = nt(hid[at, :], wup[...])
        n, r = norm(middle[at, :])
        d = gi + norm_back(u, n, r, tab[5:6, :512])
        dm[at, :] = d
        ba = d.astype(BF16)
        branch_a[at, :] = ba
        small[0:1, :512] += jnp.sum(d, 0, keepdims=True)
        small[2:3, :512] += jnp.sum(gi, 0, keepdims=True)
        small[3:4, :512] += jnp.sum(u * n, 0, keepdims=True)
        small[4:5, :512] += jnp.sum(u, 0, keepdims=True)
        da = nt(ba, wout[...])
        ones_block = block_mask().astype(BF16)
        for h in range(2):
            cols = slice(h * QUAD, (h + 1) * QUAD)
            r = inv[at, cols]
            a = da[:, cols]
            dnum[at, cols] = (a * r).astype(BF16)
            dden[at, cols] = -r * nn((a * att[at, cols].astype(F32)).astype(BF16), ones_block)

    mid = jnp.where(class_of(iota((ROWS, QUAD), 0), bounds) == 1, 1.0, 0.0).astype(BF16)
    quads, totals = [], []
    for h in range(2):
        cols = slice(h * QUAD, (h + 1) * QUAD)
        q = qkv[:, cols] * mid
        quads.append(tn(q, dnum[:, cols]))
        totals.append(jnp.sum(q.astype(F32) * dden[:, cols], 0, keepdims=True))
    pack_state(quads, totals, st)


def b2_body(x, dm, qkv, dnum, dden, prior, later, tab, win, state, total, dpre, dx, small, bounds, wait):
    half = ROWS // 2
    count = ROWS // TILE
    small[...] = jnp.zeros_like(small)
    unpack_state(prior, state, total)

    @pl.loop(0, count, unroll=True)
    def _(j):
        at = pl.ds(pl.multiple_of(j * TILE, TILE), TILE)
        masks = head_masks()
        blocks = block_mask()
        same = same_mask(j, bounds, 0)
        same4 = jnp.concatenate([same] * 4, 1)
        reads, keep, go_on = forward_masks(j, bounds)
        ones = jnp.ones((8, TILE), BF16)
        for h in range(2):
            cols = slice(h * QUAD, (h + 1) * QUAD)
            q, k, v = (qkv[at, i * 512 + h * QUAD : i * 512 + (h + 1) * QUAD] for i in range(3))
            dn = dnum[at, cols]
            s = state[h]
            ds = (nt(dn, spread(v, masks)) * same4).astype(BF16)
            ksum = nn(same.astype(BF16), k) + reads * total[h, 0:1, :]
            dq = nn(ds, spread(k, masks)) + reads * nt(dn, s.astype(BF16)) + dden[at, cols] * ksum
            dq = dq * jnp.minimum(q.astype(F32), 1.0)
            dpre[at, cols] = dq.astype(BF16)
            small[0:1, cols] += jnp.sum(dq, 0, keepdims=True)
            km = k * keep
            state[h] = go_on * s + tn(km, v) * blocks
            total[h] = go_on * total[h] + nn(ones, km)

    unpack_state(later, state, total)

    @pl.loop(0, count, unroll=True)
    def _(back):
        j = count - 1 - back
        at = pl.ds(pl.multiple_of(j * TILE, TILE), TILE)
        masks = head_masks()
        blocks = block_mask()
        same = same_mask(j, bounds, 1)
        same4 = jnp.concatenate([same] * 4, 1)
        reads, keep, go_on = backward_masks(j, bounds)
        ones = jnp.ones((8, TILE), BF16)
        for h in range(2):
            cols = slice(h * QUAD, (h + 1) * QUAD)
            q, k, v = (qkv[at, i * 512 + h * QUAD : i * 512 + (h + 1) * QUAD] for i in range(3))
            dn = dnum[at, cols]
            s = state[h]
            low = s.astype(BF16)
            qx = spread(q, masks)
            dx_ = spread(dn, masks)
            sc = (nt(k, qx) * same4).astype(BF16)
            ds = (nt(v, dx_) * same4).astype(BF16)
            dv = nn(sc, dx_) + reads * nn(k, low)
            dd = (dden[at, cols] * q.astype(F32)).astype(BF16)
            dk = nn(ds, qx) + reads * (nt(v, low) + total[h, 0:1, :]) + nn(same.astype(BF16), dd)
            dk = dk * jnp.minimum(k.astype(F32), 1.0)
            kc = slice(512 + h * QUAD, 512 + (h + 1) * QUAD)
            vc = slice(1024 + h * QUAD, 1024 + (h + 1) * QUAD)
            dpre[at, kc] = dk.astype(BF16)
            dpre[at, vc] = dv.astype(BF16)
            small[0:1, kc] += jnp.sum(dk, 0, keepdims=True)
            small[0:1, vc] += jnp.sum(dv, 0, keepdims=True)
            state[h] = go_on * s + tn(q * keep, dn) * blocks
            total[h] = go_on * total[h] + nn(ones, dd * keep)

    wait("in")

    @pl.loop(0, 2, unroll=True)
    def _(i):
        at = pl.ds(pl.multiple_of(i * half, half), half)
        u = nt(dpre[at, :], win[...])
        n, r = norm(x[at, :])
        dx[at, :] = dm[at, :] + norm_back(u, n, r, tab[4:5, :512])
        small[1:2, :512] += jnp.sum(u * n, 0, keepdims=True)
        small[2:3, :512] += jnp.sum(u, 0, keepdims=True)


WEIGHT_SHAPES = {"in": (512, 1536), "out": (512, 512), "up": (512, 2048), "down": (4, 128, 2048)}
VMEM_LIMIT = 56 * 1024 * 1024


def flip(dp, j):
    if j % 2:
        dp = dp + 1 - 2 * (dp % 2)
    if j // 2:
        dp = (dp + 2) % 4
    return dp


LINES = (("in", 3), ("out", 1), ("up", 4), ("down", 1), ("gain_a", 1), ("gain_b", 1), ("shift_a", 1), ("shift_b", 1))


def lay_out(lines, tab, dp):
    for d in range(4):
        j = dp ^ d
        at = 0
        for layer in range(2):
            for row, (_, count) in enumerate(LINES):
                for i in range(count):
                    to = (d * count + i) * 128
                    tab[layer * 8 + row : layer * 8 + row + 1, to : to + 128] = lines[j, at : at + 1, :]
                    at += 1


def call(body, bounds, tab, ins, weights, outs, scratch, flops, moved, kept=None, after=None, once=None, extra=None, which=(0, 1)):
    kept, once, extra = kept or {}, once or {}, extra or {}
    in_names, weight_names, out_names, once_names, extra_names = list(ins), list(weights), list(outs), list(once), list(extra)
    chunks = []
    for chunk, _ in weights.values():
        if not any(chunk is c for c in chunks):
            chunks.append(chunk)
    flat = [a for c in chunks for a in c]
    slots = {n: 2 * i for i, n in enumerate(in_names + out_names + once_names + extra_names)}
    first_weight = 2 * len(slots)
    micros = len(which)

    def kernel(bounds_ref, tab_ref, *refs):
        refs = list(refs)
        take = lambda n: [refs.pop(0) for _ in range(n)]
        src = dict(zip(in_names, take(len(ins))))
        src.update(zip(extra_names, take(len(extra))))
        pieces = take(len(flat))
        dst = dict(zip(out_names + once_names, take(len(outs) + len(once))))
        full = dict(zip(in_names, take(len(ins))))
        whole = dict(zip(extra_names, take(len(extra))))
        held = dict(zip(weight_names, take(len(weights))))
        full.update(zip(out_names, take(len(outs))))
        whole.update(zip(once_names, take(len(once))))
        full.update(zip(kept, take(len(kept))))
        held.update(zip(scratch, take(len(scratch))))
        sems = refs.pop(0)
        dp = lax.axis_index("dp")
        tab = refs.pop(0)

        def arriving(name, m):
            return pltpu.make_async_copy(src[name].at[which[0] + m], full[name].at[m], sems.at[slots[name] + m])

        def fetching(name):
            return pltpu.make_async_copy(src[name], whole[name], sems.at[slots[name]])

        def leaving(name, m):
            return pltpu.make_async_copy(full[name].at[m], dst[name].at[m], sems.at[slots[name] + m])

        pending = {}
        for m in range(micros):
            for name in in_names:
                arriving(name, m).start()
            if m:
                continue
            for w, name in enumerate(weight_names):
                chunk, column = weights[name]
                base = 0
                for c in chunks:
                    if c is chunk:
                        break
                    base += len(c)
                width = 2048 if name == "down" else WEIGHT_SHAPES[name][1]
                for j in range(4):
                    owner = flip(dp, j)
                    piece = pieces[base + j].at[pl.ds(0, 128), pl.ds(column, width)]
                    target = held[name].at[owner] if name == "down" else held[name].at[pl.ds(pl.multiple_of(owner * 128, 128), 128), :]
                    copy = pltpu.make_async_copy(piece, target, sems.at[first_weight + 4 * w + j])
                    copy.start()
                    pending.setdefault(name, []).append(copy)
        for name in extra_names:
            fetching(name).start()
        lay_out(tab_ref, tab, dp)

        @pl.loop(0, micros)
        def _(m):
            env = {n: r.at[m] for n, r in full.items()}
            env.update(held)

            def wait(*names):
                for name in names:
                    if name in pending:

                        @pl.when(m == 0)
                        def _():
                            for copy in pending[name]:
                                copy.wait()

                    else:
                        arriving(name, m).wait()

            def done(*names):
                for name in names:
                    leaving(name, m).start()

            body(env, wait, done, (bounds_ref[which[0] + m, 0], bounds_ref[which[0] + m, 1]), tab)

        if after is not None:
            finished = []

            def finish(name):
                copy = pltpu.make_async_copy(whole[name], dst[name], sems.at[slots[name]])
                copy.start()
                finished.append(copy)

            after({**full, **whole}, lambda name: fetching(name).wait(), finish, dp)
            for copy in finished:
                copy.wait()
        for m in range(micros):
            for name in out_names:
                leaving(name, m).wait()

    hbm = pl.BlockSpec(memory_space=pl.ANY)
    shapes = [pltpu.VMEM((micros,) + a.shape[1:], a.dtype) for a in ins.values()]
    shapes += [pltpu.VMEM(a.shape, a.dtype) for a in extra.values()]
    shapes += [pltpu.VMEM(WEIGHT_SHAPES[w], BF16) for w in weight_names]
    per_micro = lambda s: (micros,) + s.shape
    shapes += [pltpu.VMEM(per_micro(s), s.dtype) for s in outs.values()]
    shapes += [pltpu.VMEM(s.shape, s.dtype) for s in once.values()]
    shapes += [pltpu.VMEM(per_micro(s), s.dtype) for s in kept.values()]
    shapes += [pltpu.VMEM(s.shape, s.dtype) for s in scratch.values()]
    shapes.append(pltpu.SemaphoreType.DMA((first_weight + 4 * len(weights),)))
    shapes.append(pltpu.VMEM((16, 2048), F32))
    results = pl.pallas_call(
        kernel,
        out_shape=[jax.ShapeDtypeStruct(per_micro(s), s.dtype) for s in outs.values()] + list(once.values()),
        in_specs=[pl.BlockSpec(memory_space=pltpu.SMEM), pl.BlockSpec(memory_space=pltpu.VMEM)] + [hbm] * (len(ins) + len(extra) + len(flat)),
        out_specs=[hbm] * (len(outs) + len(once)),
        scratch_shapes=shapes,
        compiler_params=pltpu.CompilerParams(vmem_limit_bytes=VMEM_LIMIT),
        cost_estimate=pl.CostEstimate(flops=int(flops), bytes_accessed=int(moved), transcendentals=0),
    )(bounds, tab, *ins.values(), *extra.values(), *flat)
    return dict(zip(out_names + once_names, results))


def shape(rows, columns, kind):
    return jax.ShapeDtypeStruct((rows, columns), kind)


WIDE = shape(512, 512, F32)
NARROW = shape(512, 512, BF16)
TRIPLE = shape(512, 1536, BF16)
FOUR = shape(512, 2048, BF16)
STATE = shape(272, 128, BF16)
SMALL = shape(8, 2048, F32)
CARRY = {"state": jax.ShapeDtypeStruct((2, QUAD, QUAD), F32), "total": jax.ShapeDtypeStruct((2, 8, QUAD), F32)}

PACKED = {"in": 1536, "out": 512, "up": 2048, "down": 2048}
SMALL_ROWS = 32


def parts_of(columns):
    return {"send": jax.ShapeDtypeStruct((2, 128, columns), BF16), "keep": jax.ShapeDtypeStruct((2, 128, columns), F32)}


def weight_grads(full, names, dp):
    owners = [flip(dp, j) for j in (1, 3, 0, 2)]
    at = 0

    def put(k, cols, value):
        if k < 2:
            full["send"][k, :, cols] = value.astype(BF16)
        else:
            full["keep"][k - 2, :, cols] = value

    for name, a, b in names:
        both = lambda refs, cols: jnp.concatenate([r[m, :, cols] for r, m in refs], 0)
        a, b = (n if isinstance(n, list) else [(full[n], 0), (full[n], 1)] for n in (a, b))
        if name == "down":
            b_all = both(b, slice(None))
            for k in range(4):
                for c in range(2):
                    cols = pl.ds(pl.multiple_of(owners[k] * 512 + c * 256, 128), 256)
                    value = tn(both(a, cols), b_all)
                    for half in range(2):
                        start = at + (2 * c + half) * 512
                        put(k, slice(start, start + 512), value[half * 128 : (half + 1) * 128])
        else:
            a_all = jnp.concatenate([both(a, pl.ds(pl.multiple_of(o * 128, 128), 128)) for o in owners], 1)
            for c in range(PACKED[name] // 512):
                value = tn(a_all, both(b, slice(c * 512, (c + 1) * 512)))
                for k in range(4):
                    put(k, slice(at + c * 512, at + (c + 1) * 512), value[k * 128 : (k + 1) * 128])
        at += PACKED[name]
    return at


def enter(bounds, tab, x, w):
    def body(e, wait, done, bounds, tab):
        wait("x", "in")
        f1_body(e["x"], tab.at[0:8], e["in"], e["low_a"], e["qkv"], e["st"], bounds)
        done("low_a", "qkv", "st")

    return call(body, bounds, tab, {"x": x}, {"in": w["in"]}, {"low_a": NARROW, "qkv": TRIPLE, "st": STATE}, {}, 6e9, 8e6)


def inner(bounds, tab, x, qkv, prior, w, w_next):
    def body(e, wait, done, bounds, tab):
        here, there = tab.at[0:8], tab.at[8:16]
        wait("qkv", "prior", "x")
        f2_body(e["x"], e["qkv"], e["prior"], here, e["out"], e["up"], e["down"], e["state"], e["total"], e["att"], e["inv"], e["middle"], e["low_b"], e["act"], e["slope"], e["x1"], bounds, wait)
        done("att", "inv", "middle", "low_b", "act", "slope", "x1")
        wait("in")
        f1_body(e["x1"], there, e["in"], e["low_a"], e["qkv1"], e["st"], bounds)
        done("low_a", "qkv1", "st")

    outs = {"att": NARROW, "inv": WIDE, "middle": WIDE, "low_b": NARROW, "act": FOUR, "slope": FOUR, "x1": WIDE, "low_a": NARROW, "qkv1": TRIPLE, "st": STATE}
    return call(body, bounds, tab, {"qkv": qkv, "prior": prior, "x": x}, {"out": w["out"], "up": w["up"], "down": w["down"], "in": w_next["in"]}, outs, CARRY, 25e9, 32e6)


BRANCHES = [("down", "act", "bb"), ("out", "att", "ba"), ("up", "low_b", "hid")]


def turn(bounds, tab, x, qkv, prior, g, w):
    def body(e, wait, done, bounds, tab):
        tab = tab.at[8:16]
        wait("qkv", "prior", "x")
        f2_body(e["x"], e["qkv"], e["prior"], tab, e["out"], e["up"], e["down"], e["state"], e["total"], e["att"], e["inv"], e["middle"], e["low_b"], e["act"], e["slope"], e["y"], bounds, wait)
        done("y")
        wait("g")
        b1_body(e["g"], tab, e["out"], e["up"], e["down"], e["qkv"], e["att"], e["inv"], e["middle"], e["slope"], e["bb"], e["hid"], e["ba"], e["dm"], e["dnum"], e["dden"], e["st"], e["small"], bounds)
        done("dm", "dnum", "dden", "st", "small")

    def after(full, wait, finish, dp):
        weight_grads(full, BRANCHES, dp)
        finish("send")
        finish("keep")

    outs = {"y": WIDE, "dm": WIDE, "dnum": NARROW, "dden": WIDE, "st": STATE, "small": SMALL}
    kept = {"att": NARROW, "low_b": NARROW, "act": FOUR, "bb": NARROW, "hid": FOUR, "ba": NARROW}
    scratch = {"inv": WIDE, "middle": WIDE, "slope": FOUR, **CARRY}
    return call(body, bounds, tab, {"qkv": qkv, "prior": prior, "x": x, "g": g}, {"out": w["out"], "up": w["up"], "down": w["down"]}, outs, scratch, 34e9, 36e6, kept, after, parts_of(4608))


def back(bounds, tab, layer, x, dm, qkv, dnum, dden, prior, later, w, which, low_a=None, first=None, smalls=None):
    def body(e, wait, done, bounds, tab):
        wait("qkv", "dnum", "dden", "prior", "later", "dm", "x")
        b2_body(e["x"], e["dm"], e["qkv"], e["dnum"], e["dden"], e["prior"], e["later"], tab.at[8 * layer : 8 * layer + 8], e["in"], e["state"], e["total"], e["dpre"], e["dx"], e["small2"], bounds, wait)
        done("dx", "small2")
        if low_a is None:
            done("dpre")

    def after(full, wait, finish, dp):
        for name in extra:
            wait(name)
        pre = "dpre" if first is None else [(full["dpre0"], 0), (full["dpre"], 0)]
        at = weight_grads(full, [("in", "low_a", pre)], dp)
        if smalls:
            for k, j in enumerate((1, 3, 0, 2)):
                second = [(full["first2"], 0), (full["small2"], 0)] if first is not None else [(full["small2"], 0), (full["small2"], 1)]
                two = lambda n: [(full[n], 0), (full[n], 1)]
                lines = small_lines([two("small0"), second, two("small1"), two("other2")], flip(dp, j))
                lines = jnp.concatenate([lines, jnp.zeros((128 - SMALL_ROWS, 128), F32)], 0)
                if k < 2:
                    full["send"][k, :, at : at + 128] = lines.astype(BF16)
                else:
                    full["keep"][k - 2, :, at : at + 128] = lines
        finish("send")
        finish("keep")

    ins = {"qkv": qkv, "dnum": dnum, "dden": dden, "prior": prior, "later": later, "dm": dm, "x": x}
    outs = {"dx": WIDE, "small2": SMALL}
    if low_a is None:
        return call(body, bounds, tab, ins, {"in": w["in"]}, {**outs, "dpre": TRIPLE}, CARRY, 10e9, 10e6, which=which)
    extra = {"low_a": low_a, **(smalls or {})}
    if first is not None:
        extra.update({"dpre0": first["dpre"], "first2": first["small2"]})
    return call(body, bounds, tab, ins, {"in": w["in"]}, outs, CARRY, 20e9, 20e6, {"dpre": TRIPLE}, after, parts_of(1664 if smalls else 1536), extra, which)


def descend(bounds, tab, g, qkv, att, inv, middle, slope, act, low_b, w):
    def body(e, wait, done, bounds, tab):
        wait("g", "slope", "middle", "inv", "att", "qkv", "out", "up", "down")
        b1_body(e["g"], tab.at[0:8], e["out"], e["up"], e["down"], e["qkv"], e["att"], e["inv"], e["middle"], e["slope"], e["bb"], e["hid"], e["ba"], e["dm"], e["dnum"], e["dden"], e["st"], e["small"], bounds)
        done("dm", "dnum", "dden", "st", "small")

    def after(full, wait, finish, dp):
        wait("act")
        wait("low_b")
        weight_grads(full, BRANCHES, dp)
        finish("send")
        finish("keep")

    ins = {"g": g, "slope": slope, "middle": middle, "inv": inv, "att": att, "qkv": qkv}
    outs = {"dm": WIDE, "dnum": NARROW, "dden": WIDE, "st": STATE, "small": SMALL}
    kept = {"bb": NARROW, "hid": FOUR, "ba": NARROW}
    return call(body, bounds, tab, ins, {"down": w["down"], "up": w["up"], "out": w["out"]}, outs, {}, 16e9, 30e6, kept, after, parts_of(4608), {"act": act, "low_b": low_b})


def prepare(segments, params):
    def kernel(seg, *refs):
        *small, lines, bounds = refs
        at = 0
        for layer in range(2):
            for ref, row in zip(small, (0, 0, 0, 0, 0, 1, 0, 1)):
                line = ref[layer, row : row + 1, :] if len(ref.shape) == 3 else ref[layer : layer + 1, :]
                line = line.astype(F32)
                for i in range(line.shape[1] // 128):
                    lines[at : at + 1, :] = line[:, i * 128 : (i + 1) * 128]
                    at += 1
        lines[at:, :] = jnp.zeros((SMALL_ROWS - at, 128), F32)
        middle_id = 3 * lax.axis_index("dp") + 1
        for m in range(2):
            row = seg[m : m + 1, :]
            for i, below in enumerate((row < middle_id, row <= middle_id)):
                bounds[m, i] = jnp.sum(jnp.where(below, 1.0, 0.0)).astype(jnp.int32)

    vmem = pl.BlockSpec(memory_space=pltpu.VMEM)
    return pl.pallas_call(
        kernel,
        out_shape=[jax.ShapeDtypeStruct((SMALL_ROWS, 128), F32), jax.ShapeDtypeStruct((2, 2), jnp.int32)],
        in_specs=[vmem] * (1 + len(params)),
        out_specs=[vmem, pl.BlockSpec(memory_space=pltpu.SMEM)],
    )(segments, *params)


def small_lines(smalls, owner):
    lines = []
    for layer in range(2):
        first, second = smalls[2 * layer], smalls[2 * layer + 1]
        for ref, row, width in ((second, 0, 384), (first, 0, 128), (first, 1, 512), (first, 2, 128), (second, 1, 128), (first, 3, 128), (second, 2, 128), (first, 4, 128)):
            for i in range(width // 128):
                at = pl.ds(pl.multiple_of(owner * width + i * 128, 128), 128)
                lines.append(sum(r[m, row : row + 1, at] for r, m in ref))
    return jnp.concatenate(lines + [jnp.zeros((SMALL_ROWS - len(lines), 128), F32)], 0)


def swap(x, axis, bit):
    n = lax.axis_size(axis)
    return lax.ppermute(x, axis, [(i, i ^ bit) for i in range(n)])


def tied(x, *after):
    return lax.optimization_barrier((x,) + after)[0]


def absolute(pieces, dp):
    stacked = jnp.stack(pieces)
    return jnp.stack([lax.dynamic_index_in_dim(stacked, dp ^ j, 0, False) for j in range(4)])


def prefix_sums(x, forward, gate=None):
    n = lax.axis_size("seq")
    place = lax.axis_index("seq")
    total, result, bit = x, 0.0, 1
    while bit < n:
        if gate is not None and bit == 4:
            total = tied(total, gate)
        got = swap(total, "seq", bit).astype(F32)
        high = (place // bit) % 2 == 1
        result = result + jnp.where(high if forward else ~high, got, 0.0)
        total = (total.astype(F32) + got).astype(BF16)
        if bit == 1:
            pair = total
        bit *= 2
    return result, pair


def add_x(near, far, gate):
    return (near + tied(swap(far, "dp", 2), gate).astype(F32)).astype(BF16)


def reduce_x(near, far, gate=None):
    y = lax.axis_index("seq") % 2
    got = swap(far, "dp", 2)
    if gate is not None:
        got = tied(got, gate)
    near = near + got.astype(F32)
    half = near.shape[0] // 2
    mine = lax.dynamic_slice_in_dim(near, y * half, half, 0)
    return mine, lax.dynamic_slice_in_dim(near, (1 - y) * half, half, 0).astype(BF16)


def reduce_y(mine, other, gate=None):
    got = swap(other, "seq", 1)
    if gate is not None:
        got = tied(got, gate)
    return (mine + got.astype(F32)).astype(BF16)


def scatter_z(part, bit, gate=None):
    if bit >= lax.axis_size("seq"):
        return part
    high = (lax.axis_index("seq") // bit) % 2
    half = part.shape[0] // 2
    mine = lax.dynamic_slice_in_dim(part, high * half, half, 0).astype(F32)
    got = swap(lax.dynamic_slice_in_dim(part, (1 - high) * half, half, 0), "seq", bit)
    if gate is not None:
        got = tied(got, gate)
    return (mine + got.astype(F32)).astype(BF16)


def add_z(part, bit):
    while bit < lax.axis_size("seq"):
        part = (part.astype(F32) + swap(part, "seq", bit).astype(F32)).astype(BF16)
        bit *= 2
    return part


def gather_z(part, bit):
    if bit >= lax.axis_size("seq"):
        return part
    other = swap(part, "seq", bit)
    return jnp.where((lax.axis_index("seq") // bit) % 2 == 0, jnp.concatenate([part, other]), jnp.concatenate([other, part]))


def both_halves(part):
    other = swap(part, "seq", 1)
    y = lax.axis_index("seq") % 2
    return jnp.where(y == 0, jnp.concatenate([part, other]), jnp.concatenate([other, part])).astype(F32)


def per_device(tokens, cotangent, segments, input_weight, input_bias, output_weight, output_bias, up_weight, up_bias, down_weight, down_bias, norm_gain, norm_shift):
    lines, bounds = prepare(segments, (input_bias, output_bias, up_bias, down_bias, norm_gain, norm_gain, norm_shift, norm_shift))

    def fetch(shard, gate=None):
        across = swap(shard, "dp", 2)
        last = across if gate is None else tied(across, gate)
        return [shard, swap(shard, "dp", 1), across, swap(last, "dp", 1)]

    def packed(l):
        return [output_weight[l], up_weight[l]] + [down_weight[l][i * 128 : (i + 1) * 128] for i in range(4)]

    first = fetch(input_weight[0])
    tab = jnp.stack(fetch(lines))
    e = enter(bounds, tab, tokens, {"in": (first, 0)})
    prior0, _ = prefix_sums(e["st"], True)
    second = fetch(tied(jnp.concatenate(packed(0) + [input_weight[1]], 1), tab), prior0)
    ws = [{"in": (first, 0), "out": (second, 0), "up": (second, 512), "down": (second, 2560)}, {"in": (second, 4608)}]
    i = inner(bounds, tab, tokens, e["qkv"], prior0, ws[0], ws[1])
    third = fetch(tied(jnp.concatenate(packed(1), 1), prior0), i["st"])
    ws[1].update({"out": (third, 0), "up": (third, 512), "down": (third, 2560)})
    prior1, _ = prefix_sums(i["st"], True)
    t = turn(bounds, tab, i["x1"], i["qkv1"], prior1, cotangent, ws[1])

    def cores(parts, *after):
        both = parts["keep"] + swap(tied(parts["send"], *after), "dp", 1).astype(F32)
        return both[0], both[1].astype(BF16)

    near_a, far_a = cores(t)
    later1, _ = prefix_sums(t["st"], False, far_a)
    b = back(bounds, tab, 1, i["x1"], tied(t["dm"], far_a), i["qkv1"], t["dnum"], t["dden"], prior1, later1, ws[1], (0, 1), i["low_a"])
    ready_1 = add_x(near_a[:, :2560], far_a[:, :2560], b["small2"])
    near_b, far_b = cores(b, ready_1)
    near_2, far_2 = jnp.concatenate([near_a[:, 2560:], near_b], 1), jnp.concatenate([far_a[:, 2560:], far_b], 1)
    d = descend(bounds, tab, tied(b["dx"], far_2, ready_1), e["qkv"], i["att"], i["inv"], i["middle"], i["slope"], i["act"], i["low_b"], ws[0])
    ready_2 = reduce_x(near_2, far_2, d["small"])
    near_d, far_d = cores(d)
    later0, pair = prefix_sums(tied(d["st"], *ready_2), False, far_d)
    part_2 = reduce_y(ready_2[0], tied(ready_2[1], pair), far_d)
    lower = lambda which, dm, **more: back(bounds, tab, 0, tokens, dm, e["qkv"], d["dnum"], d["dden"], prior0, later0, ws[0], which, **more)
    v0 = lower((0,), tied(d["dm"], far_d, part_2))
    part_2 = scatter_z(part_2, 2, v0["small2"])
    ready_d1 = reduce_x(near_d[:, :2048], far_d[:, :2048], v0["small2"])
    v = lower((1,), tied(d["dm"], part_2, *ready_d1), low_a=e["low_a"], first=v0, smalls={"small0": d["small"], "small1": t["small"], "other2": b["small2"]})
    part_2 = add_z(scatter_z(part_2, 4, v["small2"]), 8)
    ready_d2 = reduce_x(near_d[:, 2048:], far_d[:, 2048:], v["small2"])
    near_c, far_c = cores(v, *ready_d2)
    sum_1 = lax.psum(ready_1, "seq")
    ready_c = reduce_x(near_c, far_c)
    part_d = jnp.concatenate([reduce_y(*ready_d1, v["small2"]), reduce_y(ready_d2[0], tied(ready_d2[1], far_c))], 1)
    part_d = scatter_z(tied(part_d, ready_c[1]), 2)
    part_2 = gather_z(tied(part_2, far_c), 4)
    part_c = reduce_y(*ready_c)
    part_d = scatter_z(tied(part_d, part_c), 4)
    part_2 = gather_z(tied(part_2, part_c), 2)
    part_c = add_z(part_c, 2)
    part_d = gather_z(gather_z(add_z(part_d, 8), 4), 2)
    in0, sum_2, sum_d = both_halves(part_c), both_halves(part_2), both_halves(part_d)
    sum_1 = tied(sum_1, part_c).astype(F32)
    down1, out1, up1, in1 = sum_1[:, :2048], sum_1[:, 2048:], sum_2[:, :2048], sum_2[:, 2048:]
    down0, out0, up0 = sum_d[:, :2048], sum_d[:, 2048:2560], sum_d[:, 2560:]
    lines = in0[:SMALL_ROWS, 1536:].reshape(-1)
    layers = []
    for l in range(2):
        at, got = l * 1664, []
        for width in (384, 128, 512, 128, 128, 128, 128, 128):
            got.append(lines[at : at + width])
            at += width
        layers.append(got)
    small = lambda k: jnp.stack([layers[l][k] for l in range(2)])
    stacked = lambda d: jnp.concatenate([d[:, c * 512 : (c + 1) * 512] for c in range(4)])
    return (
        t["y"],
        jnp.concatenate([v0["dx"], v["dx"]]),
        jnp.stack([in0[:, :1536], in1]),
        small(0),
        jnp.stack([out0, out1]),
        small(1),
        jnp.stack([up0, up1]),
        small(2),
        jnp.stack([stacked(down0), stacked(down1)]),
        small(3),
        jnp.stack([small(4), small(5)], 1),
        jnp.stack([small(6), small(7)], 1),
    )


def solution(mesh):
    rows = P(None, ("dp", "seq"), None)
    split = P(None, "dp", None)
    flat = P(None, "dp")
    last = P(None, None, "dp")
    params = (split, flat, split, flat, split, flat, split, flat, last, last)
    return jax.shard_map(
        per_device,
        mesh=mesh,
        in_specs=(rows, rows, P(None, ("dp", "seq"))) + params,
        out_specs=(rows, rows) + params,
        check_vma=False,
    )
```

```python
import jax
import jax.numpy as jnp
from jax import lax
from jax.experimental import pallas as pl
from jax.experimental.pallas import tpu as pltpu
from jax.sharding import PartitionSpec as P

HEAD = 64
EPSILON = 1e-05
F32 = jnp.float32
BF16 = jnp.bfloat16
ROWS = 512
TILE = 128
QUAD = 256
NT = (((1,), (1,)), ((), ()))
TN = (((0,), (0,)), ((), ()))
GELU = 0.7978845608028654
CUBE = 0.044715


def nn(a, b):
    return jnp.dot(a, b, preferred_element_type=F32)


def nt(a, b):
    return lax.dot_general(a, b, NT, preferred_element_type=F32)


def tn(a, b):
    return lax.dot_general(a, b, TN, preferred_element_type=F32)


def norm(x):
    mean = jnp.mean(x, -1, keepdims=True)
    c = x - mean
    r = lax.rsqrt(jnp.mean(c * c, -1, keepdims=True) + EPSILON)
    return c * r, r


def norm_back(u, n, r, gain):
    s = u * gain
    return r * (s - jnp.mean(s, -1, keepdims=True) - n * jnp.mean(s * n, -1, keepdims=True))


def iota(shape, dim):
    return lax.broadcasted_iota(jnp.int32, shape, dim)


def class_of(row, bounds):
    one = jnp.int32(1)
    zero = jnp.int32(0)
    return jnp.where(row >= bounds[0], one, zero) + jnp.where(row >= bounds[1], one, zero)


def head_masks():
    lane = iota((1, QUAD), 1) // HEAD
    return [jnp.where(lane == h, 1.0, 0.0).astype(BF16) for h in range(4)]


def spread(a, masks):
    return jnp.concatenate([a * m for m in masks], 0)


def block_mask():
    return jnp.where(iota((QUAD, QUAD), 0) // HEAD == iota((QUAD, QUAD), 1) // HEAD, 1.0, 0.0).astype(F32)


def same_mask(j, bounds, row_dim):
    t = iota((TILE, TILE), row_dim) + j * TILE
    s = iota((TILE, TILE), 1 - row_dim) + j * TILE
    keep = (s <= t) & (class_of(s, bounds) == class_of(t, bounds))
    return jnp.where(keep, 1.0, 0.0).astype(F32)


def rows_of_class(j, bounds, which, width=QUAD):
    return jnp.where(class_of(iota((TILE, width), 0) + j * TILE, bounds) == which, 1.0, 0.0).astype(F32)


def unpack_state(packed, state, total):
    lane = iota((HEAD, TILE), 1)
    left = jnp.where(lane < HEAD, 1.0, 0.0).astype(F32)
    state[...] = jnp.zeros_like(state)
    for pair in range(4):
        at = pl.ds(pair % 2 * TILE, TILE)
        c = packed[pair * HEAD : (pair + 1) * HEAD, :]
        state[pair // 2, at, at] = jnp.concatenate([c * left, c * (1.0 - left)], 0)
        total[pair // 2, :, at] = jnp.broadcast_to(packed[256 + pair : 257 + pair, :], (8, TILE))


def pack_state(quads, totals, packed):
    lane = iota((HEAD, TILE), 1)
    left = jnp.where(lane < HEAD, 1.0, 0.0).astype(F32)
    for pair in range(4):
        at = pair % 2 * TILE
        block = quads[pair // 2][at : at + TILE, at : at + TILE]
        c = block[:HEAD] * left + block[HEAD:] * (1.0 - left)
        packed[pair * HEAD : (pair + 1) * HEAD, :] = c.astype(BF16)
    lines = [totals[p // 2][:1, p % 2 * TILE : (p % 2 + 1) * TILE] for p in range(4)]
    packed[256:272, :] = jnp.concatenate(lines + [jnp.zeros((12, TILE), F32)], 0).astype(BF16)


def f1_body(x, tab, win, low_a, qkv, st, bounds):
    half = ROWS // 2

    @pl.loop(0, 2, unroll=True)
    def _(i):
        at = pl.ds(pl.multiple_of(i * half, half), half)
        n, _ = norm(x[at, :])
        low = (n * tab[4:5, :512] + tab[6:7, :512]).astype(BF16)
        low_a[at, :] = low
        for c in range(3):
            cols = slice(c * 512, (c + 1) * 512)
            pre = nn(low, win[:, cols]) + tab[0:1, cols]
            if c < 2:
                pre = jnp.where(pre > 0, pre + 1.0, jnp.exp(jnp.minimum(pre, 0.0)))
            qkv[at, cols] = pre.astype(BF16)

    mid = jnp.where(class_of(iota((ROWS, QUAD), 0), bounds) == 1, 1.0, 0.0).astype(BF16)
    ones = jnp.ones((8, ROWS), BF16)
    quads, totals = [], []
    for h in range(2):
        k = qkv[:, 512 + h * QUAD : 512 + (h + 1) * QUAD] * mid
        quads.append(tn(k, qkv[:, 1024 + h * QUAD : 1024 + (h + 1) * QUAD]))
        totals.append(nn(ones, k))
    pack_state(quads, totals, st)


def forward_masks(j, bounds):
    first = j * TILE
    carried = jnp.where(j == 0, jnp.int32(1), class_of(first - 1, bounds))
    last = class_of(first + TILE - 1, bounds)
    go_on = jnp.where(carried == last, 1.0, 0.0).astype(F32)
    return rows_of_class(j, bounds, carried), rows_of_class(j, bounds, last).astype(BF16), go_on


def backward_masks(j, bounds):
    first = j * TILE
    carried = jnp.where(j == ROWS // TILE - 1, jnp.int32(1), class_of(first + TILE, bounds))
    here = class_of(first, bounds)
    go_on = jnp.where(carried == here, 1.0, 0.0).astype(F32)
    return rows_of_class(j, bounds, carried), rows_of_class(j, bounds, here).astype(BF16), go_on


def f2_body(x, qkv, prior, tab, wout, wup, wdn, state, total, att, inv, middle, low_b, act, slope, out, bounds, wait):
    unpack_state(prior, state, total)
    half = ROWS // 2

    @pl.loop(0, ROWS // TILE, unroll=True)
    def _(j):
        at = pl.ds(pl.multiple_of(j * TILE, TILE), TILE)
        masks = head_masks()
        blocks = block_mask()
        ones_block = blocks.astype(BF16)
        same = same_mask(j, bounds, 0)
        same4 = jnp.concatenate([same] * 4, 1)
        reads, keep, go_on = forward_masks(j, bounds)
        ones = jnp.ones((8, TILE), BF16)
        for h in range(2):
            q, k, v = (qkv[at, i * 512 + h * QUAD : i * 512 + (h + 1) * QUAD] for i in range(3))
            s = state[h]
            p = (nt(q, spread(k, masks)) * same4).astype(BF16)
            num = nn(p, spread(v, masks)) + reads * nn(q, s.astype(BF16))
            ksum = nn(same.astype(BF16), k) + reads * total[h, 0:1, :]
            den = nn((q.astype(F32) * ksum).astype(BF16), ones_block)
            r = 1.0 / den
            att[at, h * QUAD : (h + 1) * QUAD] = (num * r).astype(BF16)
            inv[at, h * QUAD : (h + 1) * QUAD] = r
            km = k * keep
            state[h] = go_on * s + tn(km, v) * blocks
            total[h] = go_on * total[h] + nn(ones, km)

    wait("out")

    @pl.loop(0, 2, unroll=True)
    def _(i):
        at = pl.ds(pl.multiple_of(i * half, half), half)
        m = x[at, :] + nn(att[at, :], wout[...]) + tab[1:2, :512]
        middle[at, :] = m
        n, _ = norm(m)
        low_b[at, :] = (n * tab[5:6, :512] + tab[7:8, :512]).astype(BF16)

    wait("up")
    wait("down")

    @pl.loop(0, 2, unroll=True)
    def _(i):
        at = pl.ds(pl.multiple_of(i * half, half), half)
        low = low_b[at, :]
        for c in range(4):
            cols = slice(c * 512, (c + 1) * 512)
            h = nn(low, wup[:, cols]) + tab[2:3, cols]
            h2 = h * h
            t = jnp.tanh(h * (GELU + GELU * CUBE * h2))
            up = 0.5 + 0.5 * t
            act[at, cols] = (h * up).astype(BF16)
            slope[at, cols] = (up + up * (1.0 - t) * h * (GELU + 3.0 * GELU * CUBE * h2)).astype(BF16)
        o = middle[at, :] + tab[3:4, :512]
        for c in range(4):
            o = o + nn(act[at, c * 512 : (c + 1) * 512], down_block(wdn, c))
        out[at, :] = o


def down_block(wdn, c):
    return jnp.concatenate([wdn[c, :, i * 512 : (i + 1) * 512] for i in range(4)], 0)


def b1_body(g, tab, wout, wup, wdn, qkv, att, inv, middle, slope, branch_b, hid, branch_a, dm, dnum, dden, st, small, bounds):
    half = ROWS // 2
    small[...] = jnp.zeros_like(small)

    @pl.loop(0, 2, unroll=True)
    def _(i):
        at = pl.ds(pl.multiple_of(i * half, half), half)
        gi = g[at, :]
        bb = gi.astype(BF16)
        branch_b[at, :] = bb
        for c in range(4):
            cols = slice(c * 512, (c + 1) * 512)
            dh = nt(bb, down_block(wdn, c)) * slope[at, cols].astype(F32)
            hid[at, cols] = dh.astype(BF16)
            small[1:2, cols] += jnp.sum(dh, 0, keepdims=True)
        u = nt(hid[at, :], wup[...])
        n, r = norm(middle[at, :])
        d = gi + norm_back(u, n, r, tab[5:6, :512])
        dm[at, :] = d
        ba = d.astype(BF16)
        branch_a[at, :] = ba
        small[0:1, :512] += jnp.sum(d, 0, keepdims=True)
        small[2:3, :512] += jnp.sum(gi, 0, keepdims=True)
        small[3:4, :512] += jnp.sum(u * n, 0, keepdims=True)
        small[4:5, :512] += jnp.sum(u, 0, keepdims=True)
        da = nt(ba, wout[...])
        ones_block = block_mask().astype(BF16)
        for h in range(2):
            cols = slice(h * QUAD, (h + 1) * QUAD)
            r = inv[at, cols]
            a = da[:, cols]
            dnum[at, cols] = (a * r).astype(BF16)
            dden[at, cols] = -r * nn((a * att[at, cols].astype(F32)).astype(BF16), ones_block)

    mid = jnp.where(class_of(iota((ROWS, QUAD), 0), bounds) == 1, 1.0, 0.0).astype(BF16)
    quads, totals = [], []
    for h in range(2):
        cols = slice(h * QUAD, (h + 1) * QUAD)
        q = qkv[:, cols] * mid
        quads.append(tn(q, dnum[:, cols]))
        totals.append(jnp.sum(q.astype(F32) * dden[:, cols], 0, keepdims=True))
    pack_state(quads, totals, st)


def b2_body(x, dm, qkv, dnum, dden, prior, later, tab, win, state, total, dpre, dx, small, bounds, wait):
    half = ROWS // 2
    count = ROWS // TILE
    small[...] = jnp.zeros_like(small)
    unpack_state(prior, state, total)

    @pl.loop(0, count, unroll=True)
    def _(j):
        at = pl.ds(pl.multiple_of(j * TILE, TILE), TILE)
        masks = head_masks()
        blocks = block_mask()
        same = same_mask(j, bounds, 0)
        same4 = jnp.concatenate([same] * 4, 1)
        reads, keep, go_on = forward_masks(j, bounds)
        ones = jnp.ones((8, TILE), BF16)
        for h in range(2):
            cols = slice(h * QUAD, (h + 1) * QUAD)
            q, k, v = (qkv[at, i * 512 + h * QUAD : i * 512 + (h + 1) * QUAD] for i in range(3))
            dn = dnum[at, cols]
            s = state[h]
            ds = (nt(dn, spread(v, masks)) * same4).astype(BF16)
            ksum = nn(same.astype(BF16), k) + reads * total[h, 0:1, :]
            dq = nn(ds, spread(k, masks)) + reads * nt(dn, s.astype(BF16)) + dden[at, cols] * ksum
            dq = dq * jnp.minimum(q.astype(F32), 1.0)
            dpre[at, cols] = dq.astype(BF16)
            small[0:1, cols] += jnp.sum(dq, 0, keepdims=True)
            km = k * keep
            state[h] = go_on * s + tn(km, v) * blocks
            total[h] = go_on * total[h] + nn(ones, km)

    unpack_state(later, state, total)

    @pl.loop(0, count, unroll=True)
    def _(back):
        j = count - 1 - back
        at = pl.ds(pl.multiple_of(j * TILE, TILE), TILE)
        masks = head_masks()
        blocks = block_mask()
        same = same_mask(j, bounds, 1)
        same4 = jnp.concatenate([same] * 4, 1)
        reads, keep, go_on = backward_masks(j, bounds)
        ones = jnp.ones((8, TILE), BF16)
        for h in range(2):
            cols = slice(h * QUAD, (h + 1) * QUAD)
            q, k, v = (qkv[at, i * 512 + h * QUAD : i * 512 + (h + 1) * QUAD] for i in range(3))
            dn = dnum[at, cols]
            s = state[h]
            low = s.astype(BF16)
            qx = spread(q, masks)
            dx_ = spread(dn, masks)
            sc = (nt(k, qx) * same4).astype(BF16)
            ds = (nt(v, dx_) * same4).astype(BF16)
            dv = nn(sc, dx_) + reads * nn(k, low)
            dd = (dden[at, cols] * q.astype(F32)).astype(BF16)
            dk = nn(ds, qx) + reads * (nt(v, low) + total[h, 0:1, :]) + nn(same.astype(BF16), dd)
            dk = dk * jnp.minimum(k.astype(F32), 1.0)
            kc = slice(512 + h * QUAD, 512 + (h + 1) * QUAD)
            vc = slice(1024 + h * QUAD, 1024 + (h + 1) * QUAD)
            dpre[at, kc] = dk.astype(BF16)
            dpre[at, vc] = dv.astype(BF16)
            small[0:1, kc] += jnp.sum(dk, 0, keepdims=True)
            small[0:1, vc] += jnp.sum(dv, 0, keepdims=True)
            state[h] = go_on * s + tn(q * keep, dn) * blocks
            total[h] = go_on * total[h] + nn(ones, dd * keep)

    wait("in")

    @pl.loop(0, 2, unroll=True)
    def _(i):
        at = pl.ds(pl.multiple_of(i * half, half), half)
        u = nt(dpre[at, :], win[...])
        n, r = norm(x[at, :])
        dx[at, :] = dm[at, :] + norm_back(u, n, r, tab[4:5, :512])
        small[1:2, :512] += jnp.sum(u * n, 0, keepdims=True)
        small[2:3, :512] += jnp.sum(u, 0, keepdims=True)


WEIGHT_SHAPES = {"in": (512, 1536), "out": (512, 512), "up": (512, 2048), "down": (4, 128, 2048)}
VMEM_LIMIT = 56 * 1024 * 1024


def flip(dp, j):
    if j % 2:
        dp = dp + 1 - 2 * (dp % 2)
    if j // 2:
        dp = (dp + 2) % 4
    return dp


LINES = (("in", 3), ("out", 1), ("up", 4), ("down", 1), ("gain_a", 1), ("gain_b", 1), ("shift_a", 1), ("shift_b", 1))


def lay_out(lines, tab, dp):
    for d in range(4):
        j = dp ^ d
        at = 0
        for layer in range(2):
            for row, (_, count) in enumerate(LINES):
                for i in range(count):
                    to = (d * count + i) * 128
                    tab[layer * 8 + row : layer * 8 + row + 1, to : to + 128] = lines[j, at // 12 : at // 12 + 1, at % 12 * 128 : at % 12 * 128 + 128]
                    at += 1


def call(body, bounds, tab, ins, weights, outs, scratch, flops, moved, kept=None, after=None, once=None, extra=None, which=(0, 1)):
    kept, once, extra = kept or {}, once or {}, extra or {}
    in_names, weight_names, out_names, once_names, extra_names = list(ins), list(weights), list(outs), list(once), list(extra)
    chunks = []
    for chunk, _ in weights.values():
        if not any(chunk is c for c in chunks):
            chunks.append(chunk)
    flat = [a for c in chunks for a in c]
    slots = {n: 2 * i for i, n in enumerate(in_names + out_names + once_names + extra_names)}
    first_weight = 2 * len(slots)
    micros = len(which)

    def kernel(bounds_ref, tab_ref, *refs):
        refs = list(refs)
        take = lambda n: [refs.pop(0) for _ in range(n)]
        src = dict(zip(in_names, take(len(ins))))
        src.update(zip(extra_names, take(len(extra))))
        pieces = take(len(flat))
        dst = dict(zip(out_names + once_names, take(len(outs) + len(once))))
        full = dict(zip(in_names, take(len(ins))))
        whole = dict(zip(extra_names, take(len(extra))))
        held = dict(zip(weight_names, take(len(weights))))
        full.update(zip(out_names, take(len(outs))))
        whole.update(zip(once_names, take(len(once))))
        full.update(zip(kept, take(len(kept))))
        held.update(zip(scratch, take(len(scratch))))
        sems = refs.pop(0)
        dp = lax.axis_index("dp")
        tab = refs.pop(0)

        def arriving(name, m):
            return pltpu.make_async_copy(src[name].at[which[0] + m], full[name].at[m], sems.at[slots[name] + m])

        def fetching(name):
            return pltpu.make_async_copy(src[name], whole[name], sems.at[slots[name]])

        def leaving(name, m):
            return pltpu.make_async_copy(full[name].at[m], dst[name].at[m], sems.at[slots[name] + m])

        pending = {}
        for m in range(micros):
            for name in in_names:
                arriving(name, m).start()
            if m:
                continue
            for w, name in enumerate(weight_names):
                chunk, column = weights[name]
                base = 0
                for c in chunks:
                    if c is chunk:
                        break
                    base += len(c)
                width = 2048 if name == "down" else WEIGHT_SHAPES[name][1]
                for j in range(4):
                    owner = flip(dp, j)
                    piece = pieces[base + j].at[pl.ds(0, 128), pl.ds(column, width)]
                    target = held[name].at[owner] if name == "down" else held[name].at[pl.ds(pl.multiple_of(owner * 128, 128), 128), :]
                    copy = pltpu.make_async_copy(piece, target, sems.at[first_weight + 4 * w + j])
                    copy.start()
                    pending.setdefault(name, []).append(copy)
        for name in extra_names:
            fetching(name).start()
        lay_out(tab_ref, tab, dp)

        @pl.loop(0, micros)
        def _(m):
            env = {n: r.at[m] for n, r in full.items()}
            env.update(held)

            def wait(*names):
                for name in names:
                    if name in pending:

                        @pl.when(m == 0)
                        def _():
                            for copy in pending[name]:
                                copy.wait()

                    else:
                        arriving(name, m).wait()

            def done(*names):
                for name in names:
                    leaving(name, m).start()

            body(env, wait, done, (bounds_ref[which[0] + m, 0], bounds_ref[which[0] + m, 1]), tab)

        if after is not None:
            finished = []

            def finish(name):
                copy = pltpu.make_async_copy(whole[name], dst[name], sems.at[slots[name]])
                copy.start()
                finished.append(copy)

            after({**full, **whole}, lambda name: fetching(name).wait(), finish, dp)
            for copy in finished:
                copy.wait()
        for m in range(micros):
            for name in out_names:
                leaving(name, m).wait()

    hbm = pl.BlockSpec(memory_space=pl.ANY)
    shapes = [pltpu.VMEM((micros,) + a.shape[1:], a.dtype) for a in ins.values()]
    shapes += [pltpu.VMEM(a.shape, a.dtype) for a in extra.values()]
    shapes += [pltpu.VMEM(WEIGHT_SHAPES[w], BF16) for w in weight_names]
    per_micro = lambda s: (micros,) + s.shape
    shapes += [pltpu.VMEM(per_micro(s), s.dtype) for s in outs.values()]
    shapes += [pltpu.VMEM(s.shape, s.dtype) for s in once.values()]
    shapes += [pltpu.VMEM(per_micro(s), s.dtype) for s in kept.values()]
    shapes += [pltpu.VMEM(s.shape, s.dtype) for s in scratch.values()]
    shapes.append(pltpu.SemaphoreType.DMA((first_weight + 4 * len(weights),)))
    shapes.append(pltpu.VMEM((16, 2048), F32))
    results = pl.pallas_call(
        kernel,
        out_shape=[jax.ShapeDtypeStruct(per_micro(s), s.dtype) for s in outs.values()] + list(once.values()),
        in_specs=[pl.BlockSpec(memory_space=pltpu.SMEM), pl.BlockSpec(memory_space=pltpu.VMEM)] + [hbm] * (len(ins) + len(extra) + len(flat)),
        out_specs=[hbm] * (len(outs) + len(once)),
        scratch_shapes=shapes,
        compiler_params=pltpu.CompilerParams(vmem_limit_bytes=VMEM_LIMIT),
        cost_estimate=pl.CostEstimate(flops=int(flops), bytes_accessed=int(moved), transcendentals=0),
    )(bounds, tab, *ins.values(), *extra.values(), *flat)
    return dict(zip(out_names + once_names, results))


def shape(rows, columns, kind):
    return jax.ShapeDtypeStruct((rows, columns), kind)


WIDE = shape(512, 512, F32)
NARROW = shape(512, 512, BF16)
TRIPLE = shape(512, 1536, BF16)
FOUR = shape(512, 2048, BF16)
STATE = shape(272, 128, BF16)
SMALL = shape(8, 2048, F32)
CARRY = {"state": jax.ShapeDtypeStruct((2, QUAD, QUAD), F32), "total": jax.ShapeDtypeStruct((2, 8, QUAD), F32)}

PACKED = {"in": 1536, "out": 512, "up": 2048, "down": 2048}
SMALL_ROWS = 32


def parts_of(columns):
    return {"send": jax.ShapeDtypeStruct((2, 128, columns), BF16), "keep": jax.ShapeDtypeStruct((2, 128, columns), F32)}


def weight_grads(full, names, dp):
    owners = [flip(dp, j) for j in (1, 3, 0, 2)]
    at = 0

    def put(k, cols, value):
        if k < 2:
            full["send"][k, :, cols] = value.astype(BF16)
        else:
            full["keep"][k - 2, :, cols] = value

    for name, a, b in names:
        both = lambda refs, cols: jnp.concatenate([r[m, :, cols] for r, m in refs], 0)
        a, b = (n if isinstance(n, list) else [(full[n], 0), (full[n], 1)] for n in (a, b))
        if name == "down":
            b_all = both(b, slice(None))
            for k in range(4):
                for c in range(2):
                    cols = pl.ds(pl.multiple_of(owners[k] * 512 + c * 256, 128), 256)
                    value = tn(both(a, cols), b_all)
                    for half in range(2):
                        start = at + (2 * c + half) * 512
                        put(k, slice(start, start + 512), value[half * 128 : (half + 1) * 128])
        else:
            a_all = jnp.concatenate([both(a, pl.ds(pl.multiple_of(o * 128, 128), 128)) for o in owners], 1)
            for c in range(PACKED[name] // 512):
                value = tn(a_all, both(b, slice(c * 512, (c + 1) * 512)))
                for k in range(4):
                    put(k, slice(at + c * 512, at + (c + 1) * 512), value[k * 128 : (k + 1) * 128])
        at += PACKED[name]
    return at


def enter(bounds, tab, x, w):
    def body(e, wait, done, bounds, tab):
        wait("x", "in")
        f1_body(e["x"], tab.at[0:8], e["in"], e["low_a"], e["qkv"], e["st"], bounds)
        done("low_a", "qkv", "st")

    return call(body, bounds, tab, {"x": x}, {"in": w["in"]}, {"low_a": NARROW, "qkv": TRIPLE, "st": STATE}, {}, 6e9, 8e6)


def inner(bounds, tab, x, qkv, prior, w, w_next):
    def body(e, wait, done, bounds, tab):
        here, there = tab.at[0:8], tab.at[8:16]
        wait("qkv", "prior", "x")
        f2_body(e["x"], e["qkv"], e["prior"], here, e["out"], e["up"], e["down"], e["state"], e["total"], e["att"], e["inv"], e["middle"], e["low_b"], e["act"], e["slope"], e["x1"], bounds, wait)
        done("att", "inv", "middle", "low_b", "act", "slope", "x1")
        wait("in")
        f1_body(e["x1"], there, e["in"], e["low_a"], e["qkv1"], e["st"], bounds)
        done("low_a", "qkv1", "st")

    outs = {"att": NARROW, "inv": WIDE, "middle": WIDE, "low_b": NARROW, "act": FOUR, "slope": FOUR, "x1": WIDE, "low_a": NARROW, "qkv1": TRIPLE, "st": STATE}
    return call(body, bounds, tab, {"qkv": qkv, "prior": prior, "x": x}, {"out": w["out"], "up": w["up"], "down": w["down"], "in": w_next["in"]}, outs, CARRY, 25e9, 32e6)


BRANCHES = [("down", "act", "bb"), ("out", "att", "ba"), ("up", "low_b", "hid")]


def turn(bounds, tab, x, qkv, prior, g, w):
    def body(e, wait, done, bounds, tab):
        tab = tab.at[8:16]
        wait("qkv", "prior", "x")
        f2_body(e["x"], e["qkv"], e["prior"], tab, e["out"], e["up"], e["down"], e["state"], e["total"], e["att"], e["inv"], e["middle"], e["low_b"], e["act"], e["slope"], e["y"], bounds, wait)
        done("y")
        wait("g")
        b1_body(e["g"], tab, e["out"], e["up"], e["down"], e["qkv"], e["att"], e["inv"], e["middle"], e["slope"], e["bb"], e["hid"], e["ba"], e["dm"], e["dnum"], e["dden"], e["st"], e["small"], bounds)
        done("dm", "dnum", "dden", "st", "small")

    def after(full, wait, finish, dp):
        weight_grads(full, BRANCHES, dp)
        finish("send")
        finish("keep")

    outs = {"y": WIDE, "dm": WIDE, "dnum": NARROW, "dden": WIDE, "st": STATE, "small": SMALL}
    kept = {"att": NARROW, "low_b": NARROW, "act": FOUR, "bb": NARROW, "hid": FOUR, "ba": NARROW}
    scratch = {"inv": WIDE, "middle": WIDE, "slope": FOUR, **CARRY}
    return call(body, bounds, tab, {"qkv": qkv, "prior": prior, "x": x, "g": g}, {"out": w["out"], "up": w["up"], "down": w["down"]}, outs, scratch, 34e9, 36e6, kept, after, parts_of(4608))


def back(bounds, tab, layer, x, dm, qkv, dnum, dden, prior, later, w, which, low_a=None, first=None, smalls=None):
    def body(e, wait, done, bounds, tab):
        wait("qkv", "dnum", "dden", "prior", "later", "dm", "x")
        b2_body(e["x"], e["dm"], e["qkv"], e["dnum"], e["dden"], e["prior"], e["later"], tab.at[8 * layer : 8 * layer + 8], e["in"], e["state"], e["total"], e["dpre"], e["dx"], e["small2"], bounds, wait)
        done("dx", "small2")
        if low_a is None:
            done("dpre")

    def after(full, wait, finish, dp):
        for name in extra:
            wait(name)
        pre = "dpre" if first is None else [(full["dpre0"], 0), (full["dpre"], 0)]
        at = weight_grads(full, [("in", "low_a", pre)], dp)
        if smalls:
            for k, j in enumerate((1, 3, 0, 2)):
                second = [(full["first2"], 0), (full["small2"], 0)] if first is not None else [(full["small2"], 0), (full["small2"], 1)]
                two = lambda n: [(full[n], 0), (full[n], 1)]
                lines = small_lines([two("small0"), second, two("small1"), two("other2")], flip(dp, j))
                lines = jnp.concatenate([lines, jnp.zeros((128 - SMALL_ROWS, 128), F32)], 0)
                if k < 2:
                    full["send"][k, :, at : at + 128] = lines.astype(BF16)
                else:
                    full["keep"][k - 2, :, at : at + 128] = lines
        finish("send")
        finish("keep")

    ins = {"qkv": qkv, "dnum": dnum, "dden": dden, "prior": prior, "later": later, "dm": dm, "x": x}
    outs = {"dx": WIDE, "small2": SMALL}
    if low_a is None:
        return call(body, bounds, tab, ins, {"in": w["in"]}, {**outs, "dpre": TRIPLE}, CARRY, 10e9, 10e6, which=which)
    extra = {"low_a": low_a, **(smalls or {})}
    if first is not None:
        extra.update({"dpre0": first["dpre"], "first2": first["small2"]})
    return call(body, bounds, tab, ins, {"in": w["in"]}, outs, CARRY, 20e9, 20e6, {"dpre": TRIPLE}, after, parts_of(1664 if smalls else 1536), extra, which)


def descend(bounds, tab, g, qkv, att, inv, middle, slope, act, low_b, w):
    def body(e, wait, done, bounds, tab):
        wait("g", "slope", "middle", "inv", "att", "qkv", "out", "up", "down")
        b1_body(e["g"], tab.at[0:8], e["out"], e["up"], e["down"], e["qkv"], e["att"], e["inv"], e["middle"], e["slope"], e["bb"], e["hid"], e["ba"], e["dm"], e["dnum"], e["dden"], e["st"], e["small"], bounds)
        done("dm", "dnum", "dden", "st", "small")

    def after(full, wait, finish, dp):
        wait("act")
        wait("low_b")
        weight_grads(full, BRANCHES, dp)
        finish("send")
        finish("keep")

    ins = {"g": g, "slope": slope, "middle": middle, "inv": inv, "att": att, "qkv": qkv}
    outs = {"dm": WIDE, "dnum": NARROW, "dden": WIDE, "st": STATE, "small": SMALL}
    kept = {"bb": NARROW, "hid": FOUR, "ba": NARROW}
    return call(body, bounds, tab, ins, {"down": w["down"], "up": w["up"], "out": w["out"]}, outs, {}, 16e9, 30e6, kept, after, parts_of(4608), {"act": act, "low_b": low_b})


def small_lines(smalls, owner):
    lines = []
    for layer in range(2):
        first, second = smalls[2 * layer], smalls[2 * layer + 1]
        for ref, row, width in ((second, 0, 384), (first, 0, 128), (first, 1, 512), (first, 2, 128), (second, 1, 128), (first, 3, 128), (second, 2, 128), (first, 4, 128)):
            for i in range(width // 128):
                at = pl.ds(pl.multiple_of(owner * width + i * 128, 128), 128)
                lines.append(sum(r[m, row : row + 1, at] for r, m in ref))
    return jnp.concatenate(lines + [jnp.zeros((SMALL_ROWS - len(lines), 128), F32)], 0)


def prepare(segments, weight, params):
    def kernel(seg, weight, *refs):
        *small, out, bounds, lines = refs
        out[:128, :] = weight[0]
        lines[...] = jnp.zeros_like(lines)
        at = 0
        for layer in range(2):
            for ref, row in zip(small, (0, 0, 0, 0, 0, 1, 0, 1)):
                line = ref[layer, row : row + 1, :] if len(ref.shape) == 3 else ref[layer : layer + 1, :]
                line = line.astype(F32)
                for i in range(line.shape[1] // 128):
                    lines[at // 12 : at // 12 + 1, at % 12 * 128 : at % 12 * 128 + 128] = line[:, i * 128 : (i + 1) * 128]
                    at += 1
        out[128:, :] = lines[...].astype(BF16)
        middle_id = 3 * lax.axis_index("dp") + 1
        for m in range(2):
            row = seg[m : m + 1, :]
            for i, inside in enumerate((row < middle_id, row <= middle_id)):
                bounds[m, i] = jnp.sum(jnp.where(inside, 1.0, 0.0)).astype(jnp.int32)

    vmem = pl.BlockSpec(memory_space=pltpu.VMEM)
    return pl.pallas_call(
        kernel,
        out_shape=[jax.ShapeDtypeStruct((144, 1536), BF16), jax.ShapeDtypeStruct((2, 2), jnp.int32)],
        in_specs=[vmem] * (2 + len(params)),
        out_specs=[vmem, pl.BlockSpec(memory_space=pltpu.SMEM)],
        scratch_shapes=[pltpu.VMEM((16, 1536), F32)],
    )(segments, weight, *params)


def swap(x, axis, bit):
    n = lax.axis_size(axis)
    return lax.ppermute(x, axis, [(i, i ^ bit) for i in range(n)])


def tied(x, *after):
    return lax.optimization_barrier((x,) + after)[0]


def absolute(pieces, dp):
    stacked = jnp.stack(pieces)
    return jnp.stack([lax.dynamic_index_in_dim(stacked, dp ^ j, 0, False) for j in range(4)])


def prefix_sums(x, forward, gate=None):
    n = lax.axis_size("seq")
    place = lax.axis_index("seq")
    total, result, bit = x, 0.0, 1
    while bit < n:
        got = swap(total, "seq", bit)
        if gate is not None and bit == 4:
            got = tied(got, gate)
        got = got.astype(F32)
        high = (place // bit) % 2 == 1
        result = result + jnp.where(high if forward else ~high, got, 0.0)
        total = (total.astype(F32) + got).astype(BF16)
        if bit == 1:
            pair = total
        bit *= 2
    return result, pair


def reduce_x(near, far, gate=None):
    y = lax.axis_index("seq") % 2
    got = swap(far, "dp", 2)
    if gate is not None:
        got = tied(got, gate)
    near = near + got.astype(F32)
    half = near.shape[0] // 2
    mine = lax.dynamic_slice_in_dim(near, y * half, half, 0)
    return mine, lax.dynamic_slice_in_dim(near, (1 - y) * half, half, 0).astype(BF16)


def reduce_y(mine, other, gate=None):
    got = swap(other, "seq", 1)
    if gate is not None:
        got = tied(got, gate)
    return (mine + got.astype(F32)).astype(BF16)


def scatter_z(part, bit, gate=None):
    if bit >= lax.axis_size("seq"):
        return part
    high = (lax.axis_index("seq") // bit) % 2
    half = part.shape[0] // 2
    mine = lax.dynamic_slice_in_dim(part, high * half, half, 0).astype(F32)
    got = swap(lax.dynamic_slice_in_dim(part, (1 - high) * half, half, 0), "seq", bit)
    if gate is not None:
        got = tied(got, gate)
    return (mine + got.astype(F32)).astype(BF16)


def add_z(part, bit):
    while bit < lax.axis_size("seq"):
        part = (part.astype(F32) + swap(part, "seq", bit).astype(F32)).astype(BF16)
        bit *= 2
    return part


def gather_z(part, bit):
    if bit >= lax.axis_size("seq"):
        return part
    other = swap(part, "seq", bit)
    return jnp.where((lax.axis_index("seq") // bit) % 2 == 0, jnp.concatenate([part, other]), jnp.concatenate([other, part]))


def both_halves(part):
    other = swap(part, "seq", 1)
    y = lax.axis_index("seq") % 2
    return jnp.where(y == 0, jnp.concatenate([part, other]), jnp.concatenate([other, part])).astype(F32)


def per_device(tokens, cotangent, segments, input_weight, input_bias, output_weight, output_bias, up_weight, up_bias, down_weight, down_bias, norm_gain, norm_shift):
    shard, bounds = prepare(segments, input_weight, (input_bias, output_bias, up_bias, down_bias, norm_gain, norm_gain, norm_shift, norm_shift))

    def fetch(shard, gate=None):
        across = swap(shard, "dp", 2)
        last = across if gate is None else tied(across, gate)
        return [shard, swap(shard, "dp", 1), across, swap(last, "dp", 1)]

    def packed(l):
        return [output_weight[l], up_weight[l]] + [down_weight[l][i * 128 : (i + 1) * 128] for i in range(4)]

    first = fetch(shard)
    tab = jnp.stack([p[128:144] for p in first]).astype(F32)
    second = tied(jnp.concatenate(packed(0) + [input_weight[1]], 1), first[1])
    e = enter(bounds, tab, tokens, {"in": (first, 0)})
    prior0, _ = prefix_sums(e["st"], True)
    second = fetch(second, prior0)
    ws = [{"in": (first, 0), "out": (second, 0), "up": (second, 512), "down": (second, 2560)}, {"in": (second, 4608)}]
    i = inner(bounds, tab, tokens, e["qkv"], prior0, ws[0], ws[1])
    third = fetch(tied(jnp.concatenate(packed(1), 1), prior0), i["st"])
    ws[1].update({"out": (third, 0), "up": (third, 512), "down": (third, 2560)})
    prior1, _ = prefix_sums(i["st"], True)
    t = turn(bounds, tab, i["x1"], i["qkv1"], prior1, cotangent, ws[1])

    def cores(parts, *after):
        both = parts["keep"] + swap(tied(parts["send"], *after), "dp", 1).astype(F32)
        return both[0], both[1].astype(BF16)

    near_a, far_a = cores(t)
    later1, _ = prefix_sums(t["st"], False, far_a)
    b = back(bounds, tab, 1, i["x1"], tied(t["dm"], far_a), i["qkv1"], t["dnum"], t["dden"], prior1, later1, ws[1], (0, 1), i["low_a"])
    ready_1 = reduce_x(near_a[:, :2560], far_a[:, :2560], b["small2"])
    near_b, far_b = cores(b, *ready_1)
    near_2, far_2 = jnp.concatenate([near_a[:, 2560:], near_b], 1), jnp.concatenate([far_a[:, 2560:], far_b], 1)
    d = descend(bounds, tab, tied(b["dx"], far_2, *ready_1), e["qkv"], i["att"], i["inv"], i["middle"], i["slope"], i["act"], i["low_b"], ws[0])
    ready_2 = reduce_x(near_2, far_2, d["small"])
    near_d, far_d = cores(d)
    later0, pair = prefix_sums(tied(d["st"], *ready_2), False, far_d)
    part_2 = jnp.concatenate([reduce_y(*ready_1, d["small"]), reduce_y(ready_2[0], tied(ready_2[1], pair), far_d)], 1)
    lower = lambda which, dm, **more: back(bounds, tab, 0, tokens, dm, e["qkv"], d["dnum"], d["dden"], prior0, later0, ws[0], which, **more)
    v0 = lower((0,), tied(d["dm"], far_d, part_2))
    part_2 = scatter_z(part_2, 2, v0["small2"])
    ready_d1 = reduce_x(near_d[:, :2048], far_d[:, :2048], v0["small2"])
    v = lower((1,), tied(d["dm"], part_2, *ready_d1), low_a=e["low_a"], first=v0, smalls={"small0": d["small"], "small1": t["small"], "other2": b["small2"]})
    part_2 = add_z(scatter_z(part_2, 4, v["small2"]), 8)
    ready_d2 = reduce_x(near_d[:, 2048:], far_d[:, 2048:], v["small2"])
    near_c, far_c = cores(v, *ready_d2)
    ready_c = reduce_x(near_c, far_c)
    part_d = jnp.concatenate([reduce_y(*ready_d1, v["small2"]), reduce_y(ready_d2[0], tied(ready_d2[1], far_c))], 1)
    part_2 = gather_z(tied(part_2, far_c), 4)
    part_d = scatter_z(tied(part_d, ready_c[1], part_2), 2)
    part_c = reduce_y(*ready_c)
    part_d = scatter_z(tied(part_d, part_c), 4)
    part_2 = gather_z(part_2, 2)
    part_c = add_z(part_c, 2)
    part_d = gather_z(gather_z(tied(add_z(part_d, 8), part_2), 4), 2)
    in0, sum_2, sum_d = both_halves(part_c), both_halves(part_2), both_halves(part_d)
    down1, out1, up1, in1 = sum_2[:, :2048], sum_2[:, 2048:2560], sum_2[:, 2560:4608], sum_2[:, 4608:]
    down0, out0, up0 = sum_d[:, :2048], sum_d[:, 2048:2560], sum_d[:, 2560:]
    lines = in0[:SMALL_ROWS, 1536:].reshape(-1)
    layers = []
    for l in range(2):
        at, got = l * 1664, []
        for width in (384, 128, 512, 128, 128, 128, 128, 128):
            got.append(lines[at : at + width])
            at += width
        layers.append(got)
    small = lambda k: jnp.stack([layers[l][k] for l in range(2)])
    stacked = lambda d: jnp.concatenate([d[:, c * 512 : (c + 1) * 512] for c in range(4)])
    return (
        t["y"],
        jnp.concatenate([v0["dx"], tied(v["dx"], far_c)]),
        jnp.stack([in0[:, :1536], in1]),
        small(0),
        jnp.stack([out0, out1]),
        small(1),
        jnp.stack([up0, up1]),
        small(2),
        jnp.stack([stacked(down0), stacked(down1)]),
        small(3),
        jnp.stack([small(4), small(5)], 1),
        jnp.stack([small(6), small(7)], 1),
    )


def solution(mesh):
    rows = P(None, ("dp", "seq"), None)
    split = P(None, "dp", None)
    flat = P(None, "dp")
    last = P(None, None, "dp")
    params = (split, flat, split, flat, split, flat, split, flat, last, last)
    return jax.shard_map(
        per_device,
        mesh=mesh,
        in_specs=(rows, rows, P(None, ("dp", "seq"))) + params,
        out_specs=(rows, rows) + params,
        check_vma=False,
    )
```

```python
import jax
import jax.numpy as jnp
from jax import lax
from jax.experimental import pallas as pl
from jax.experimental.pallas import tpu as pltpu
from jax.sharding import PartitionSpec as P

HEAD = 64
EPSILON = 1e-05
F32 = jnp.float32
BF16 = jnp.bfloat16
ROWS = 512
TILE = 128
QUAD = 256
NT = (((1,), (1,)), ((), ()))
TN = (((0,), (0,)), ((), ()))
GELU = 0.7978845608028654
CUBE = 0.044715


def nn(a, b):
    return jnp.dot(a, b, preferred_element_type=F32)


def nt(a, b):
    return lax.dot_general(a, b, NT, preferred_element_type=F32)


def tn(a, b):
    return lax.dot_general(a, b, TN, preferred_element_type=F32)


def norm(x):
    mean = jnp.mean(x, -1, keepdims=True)
    c = x - mean
    r = lax.rsqrt(jnp.mean(c * c, -1, keepdims=True) + EPSILON)
    return c * r, r


def norm_back(u, n, r, gain):
    s = u * gain
    return r * (s - jnp.mean(s, -1, keepdims=True) - n * jnp.mean(s * n, -1, keepdims=True))


def iota(shape, dim):
    return lax.broadcasted_iota(jnp.int32, shape, dim)


def class_of(row, bounds):
    one = jnp.int32(1)
    zero = jnp.int32(0)
    return jnp.where(row >= bounds[0], one, zero) + jnp.where(row >= bounds[1], one, zero)


def head_masks():
    lane = iota((1, QUAD), 1) // HEAD
    return [jnp.where(lane == h, 1.0, 0.0).astype(BF16) for h in range(4)]


def spread(a, masks):
    return jnp.concatenate([a * m for m in masks], 0)


def block_mask():
    return jnp.where(iota((QUAD, QUAD), 0) // HEAD == iota((QUAD, QUAD), 1) // HEAD, 1.0, 0.0).astype(F32)


def same_mask(j, bounds, row_dim):
    t = iota((TILE, TILE), row_dim) + j * TILE
    s = iota((TILE, TILE), 1 - row_dim) + j * TILE
    keep = (s <= t) & (class_of(s, bounds) == class_of(t, bounds))
    return jnp.where(keep, 1.0, 0.0).astype(F32)


def rows_of_class(j, bounds, which, width=QUAD):
    return jnp.where(class_of(iota((TILE, width), 0) + j * TILE, bounds) == which, 1.0, 0.0).astype(F32)


def unpack_state(packed, state, total):
    lane = iota((HEAD, TILE), 1)
    left = jnp.where(lane < HEAD, 1.0, 0.0).astype(F32)
    state[...] = jnp.zeros_like(state)
    for pair in range(4):
        at = pl.ds(pair % 2 * TILE, TILE)
        c = packed[pair * HEAD : (pair + 1) * HEAD, :]
        state[pair // 2, at, at] = jnp.concatenate([c * left, c * (1.0 - left)], 0)
        total[pair // 2, :, at] = jnp.broadcast_to(packed[256 + pair : 257 + pair, :], (8, TILE))


def pack_state(quads, totals, packed):
    lane = iota((HEAD, TILE), 1)
    left = jnp.where(lane < HEAD, 1.0, 0.0).astype(F32)
    for pair in range(4):
        at = pair % 2 * TILE
        block = quads[pair // 2][at : at + TILE, at : at + TILE]
        c = block[:HEAD] * left + block[HEAD:] * (1.0 - left)
        packed[pair * HEAD : (pair + 1) * HEAD, :] = c.astype(BF16)
    lines = [totals[p // 2][:1, p % 2 * TILE : (p % 2 + 1) * TILE] for p in range(4)]
    packed[256:272, :] = jnp.concatenate(lines + [jnp.zeros((12, TILE), F32)], 0).astype(BF16)


def f1_body(x, tab, win, low_a, qkv, st, bounds):
    half = ROWS // 2

    @pl.loop(0, 2, unroll=True)
    def _(i):
        at = pl.ds(pl.multiple_of(i * half, half), half)
        n, _ = norm(x[at, :])
        low = (n * tab[4:5, :512] + tab[6:7, :512]).astype(BF16)
        low_a[at, :] = low
        for c in range(3):
            cols = slice(c * 512, (c + 1) * 512)
            pre = nn(low, win[:, cols]) + tab[0:1, cols]
            if c < 2:
                pre = jnp.where(pre > 0, pre + 1.0, jnp.exp(jnp.minimum(pre, 0.0)))
            qkv[at, cols] = pre.astype(BF16)

    mid = jnp.where(class_of(iota((ROWS, QUAD), 0), bounds) == 1, 1.0, 0.0).astype(BF16)
    ones = jnp.ones((8, ROWS), BF16)
    quads, totals = [], []
    for h in range(2):
        k = qkv[:, 512 + h * QUAD : 512 + (h + 1) * QUAD] * mid
        quads.append(tn(k, qkv[:, 1024 + h * QUAD : 1024 + (h + 1) * QUAD]))
        totals.append(nn(ones, k))
    pack_state(quads, totals, st)


def forward_masks(j, bounds):
    first = j * TILE
    carried = jnp.where(j == 0, jnp.int32(1), class_of(first - 1, bounds))
    last = class_of(first + TILE - 1, bounds)
    go_on = jnp.where(carried == last, 1.0, 0.0).astype(F32)
    return rows_of_class(j, bounds, carried), rows_of_class(j, bounds, last).astype(BF16), go_on


def backward_masks(j, bounds):
    first = j * TILE
    carried = jnp.where(j == ROWS // TILE - 1, jnp.int32(1), class_of(first + TILE, bounds))
    here = class_of(first, bounds)
    go_on = jnp.where(carried == here, 1.0, 0.0).astype(F32)
    return rows_of_class(j, bounds, carried), rows_of_class(j, bounds, here).astype(BF16), go_on


def f2_body(x, qkv, prior, tab, wout, wup, wdn, state, total, att, inv, middle, low_b, act, slope, out, bounds, wait, done=lambda *names: None):
    unpack_state(prior, state, total)
    half = ROWS // 2

    @pl.loop(0, ROWS // TILE, unroll=True)
    def _(j):
        at = pl.ds(pl.multiple_of(j * TILE, TILE), TILE)
        masks = head_masks()
        blocks = block_mask()
        ones_block = blocks.astype(BF16)
        same = same_mask(j, bounds, 0)
        same4 = jnp.concatenate([same] * 4, 1)
        reads, keep, go_on = forward_masks(j, bounds)
        ones = jnp.ones((8, TILE), BF16)
        for h in range(2):
            q, k, v = (qkv[at, i * 512 + h * QUAD : i * 512 + (h + 1) * QUAD] for i in range(3))
            s = state[h]
            p = (nt(q, spread(k, masks)) * same4).astype(BF16)
            num = nn(p, spread(v, masks)) + reads * nn(q, s.astype(BF16))
            ksum = nn(same.astype(BF16), k) + reads * total[h, 0:1, :]
            den = nn((q.astype(F32) * ksum).astype(BF16), ones_block)
            r = 1.0 / den
            att[at, h * QUAD : (h + 1) * QUAD] = (num * r).astype(BF16)
            inv[at, h * QUAD : (h + 1) * QUAD] = r
            km = k * keep
            state[h] = go_on * s + tn(km, v) * blocks
            total[h] = go_on * total[h] + nn(ones, km)

    done("att", "inv")
    wait("out")

    @pl.loop(0, 2, unroll=True)
    def _(i):
        at = pl.ds(pl.multiple_of(i * half, half), half)
        m = x[at, :] + nn(att[at, :], wout[...]) + tab[1:2, :512]
        middle[at, :] = m
        n, _ = norm(m)
        low_b[at, :] = (n * tab[5:6, :512] + tab[7:8, :512]).astype(BF16)

    done("middle", "low_b")
    wait("up")
    wait("down")

    @pl.loop(0, 2, unroll=True)
    def _(i):
        at = pl.ds(pl.multiple_of(i * half, half), half)
        low = low_b[at, :]
        for c in range(4):
            cols = slice(c * 512, (c + 1) * 512)
            h = nn(low, wup[:, cols]) + tab[2:3, cols]
            h2 = h * h
            t = jnp.tanh(h * (GELU + GELU * CUBE * h2))
            up = 0.5 + 0.5 * t
            act[at, cols] = (h * up).astype(BF16)
            slope[at, cols] = (up + up * (1.0 - t) * h * (GELU + 3.0 * GELU * CUBE * h2)).astype(BF16)
        o = middle[at, :] + tab[3:4, :512]
        for c in range(4):
            o = o + nn(act[at, c * 512 : (c + 1) * 512], down_block(wdn, c))
        out[at, :] = o


def down_block(wdn, c):
    return jnp.concatenate([wdn[c, :, i * 512 : (i + 1) * 512] for i in range(4)], 0)


def b1_body(g, tab, wout, wup, wdn, qkv, att, inv, middle, slope, branch_b, hid, branch_a, dm, dnum, dden, st, small, bounds):
    half = ROWS // 2
    small[...] = jnp.zeros_like(small)

    @pl.loop(0, 2, unroll=True)
    def _(i):
        at = pl.ds(pl.multiple_of(i * half, half), half)
        gi = g[at, :]
        bb = gi.astype(BF16)
        branch_b[at, :] = bb
        for c in range(4):
            cols = slice(c * 512, (c + 1) * 512)
            dh = nt(bb, down_block(wdn, c)) * slope[at, cols].astype(F32)
            hid[at, cols] = dh.astype(BF16)
            small[1:2, cols] += jnp.sum(dh, 0, keepdims=True)
        u = nt(hid[at, :], wup[...])
        n, r = norm(middle[at, :])
        d = gi + norm_back(u, n, r, tab[5:6, :512])
        dm[at, :] = d
        ba = d.astype(BF16)
        branch_a[at, :] = ba
        small[0:1, :512] += jnp.sum(d, 0, keepdims=True)
        small[2:3, :512] += jnp.sum(gi, 0, keepdims=True)
        small[3:4, :512] += jnp.sum(u * n, 0, keepdims=True)
        small[4:5, :512] += jnp.sum(u, 0, keepdims=True)
        da = nt(ba, wout[...])
        ones_block = block_mask().astype(BF16)
        for h in range(2):
            cols = slice(h * QUAD, (h + 1) * QUAD)
            r = inv[at, cols]
            a = da[:, cols]
            dnum[at, cols] = (a * r).astype(BF16)
            dden[at, cols] = -r * nn((a * att[at, cols].astype(F32)).astype(BF16), ones_block)

    mid = jnp.where(class_of(iota((ROWS, QUAD), 0), bounds) == 1, 1.0, 0.0).astype(BF16)
    quads, totals = [], []
    for h in range(2):
        cols = slice(h * QUAD, (h + 1) * QUAD)
        q = qkv[:, cols] * mid
        quads.append(tn(q, dnum[:, cols]))
        totals.append(jnp.sum(q.astype(F32) * dden[:, cols], 0, keepdims=True))
    pack_state(quads, totals, st)


def b2_body(x, dm, qkv, dnum, dden, prior, later, tab, win, state, total, dpre, dx, small, bounds, wait):
    half = ROWS // 2
    count = ROWS // TILE
    small[...] = jnp.zeros_like(small)
    unpack_state(prior, state, total)

    @pl.loop(0, count, unroll=True)
    def _(j):
        at = pl.ds(pl.multiple_of(j * TILE, TILE), TILE)
        masks = head_masks()
        blocks = block_mask()
        same = same_mask(j, bounds, 0)
        same4 = jnp.concatenate([same] * 4, 1)
        reads, keep, go_on = forward_masks(j, bounds)
        ones = jnp.ones((8, TILE), BF16)
        for h in range(2):
            cols = slice(h * QUAD, (h + 1) * QUAD)
            q, k, v = (qkv[at, i * 512 + h * QUAD : i * 512 + (h + 1) * QUAD] for i in range(3))
            dn = dnum[at, cols]
            s = state[h]
            ds = (nt(dn, spread(v, masks)) * same4).astype(BF16)
            ksum = nn(same.astype(BF16), k) + reads * total[h, 0:1, :]
            dq = nn(ds, spread(k, masks)) + reads * nt(dn, s.astype(BF16)) + dden[at, cols] * ksum
            dq = dq * jnp.minimum(q.astype(F32), 1.0)
            dpre[at, cols] = dq.astype(BF16)
            small[0:1, cols] += jnp.sum(dq, 0, keepdims=True)
            km = k * keep
            state[h] = go_on * s + tn(km, v) * blocks
            total[h] = go_on * total[h] + nn(ones, km)

    unpack_state(later, state, total)

    @pl.loop(0, count, unroll=True)
    def _(back):
        j = count - 1 - back
        at = pl.ds(pl.multiple_of(j * TILE, TILE), TILE)
        masks = head_masks()
        blocks = block_mask()
        same = same_mask(j, bounds, 1)
        same4 = jnp.concatenate([same] * 4, 1)
        reads, keep, go_on = backward_masks(j, bounds)
        ones = jnp.ones((8, TILE), BF16)
        for h in range(2):
            cols = slice(h * QUAD, (h + 1) * QUAD)
            q, k, v = (qkv[at, i * 512 + h * QUAD : i * 512 + (h + 1) * QUAD] for i in range(3))
            dn = dnum[at, cols]
            s = state[h]
            low = s.astype(BF16)
            qx = spread(q, masks)
            dx_ = spread(dn, masks)
            sc = (nt(k, qx) * same4).astype(BF16)
            ds = (nt(v, dx_) * same4).astype(BF16)
            dv = nn(sc, dx_) + reads * nn(k, low)
            dd = (dden[at, cols] * q.astype(F32)).astype(BF16)
            dk = nn(ds, qx) + reads * (nt(v, low) + total[h, 0:1, :]) + nn(same.astype(BF16), dd)
            dk = dk * jnp.minimum(k.astype(F32), 1.0)
            kc = slice(512 + h * QUAD, 512 + (h + 1) * QUAD)
            vc = slice(1024 + h * QUAD, 1024 + (h + 1) * QUAD)
            dpre[at, kc] = dk.astype(BF16)
            dpre[at, vc] = dv.astype(BF16)
            small[0:1, kc] += jnp.sum(dk, 0, keepdims=True)
            small[0:1, vc] += jnp.sum(dv, 0, keepdims=True)
            state[h] = go_on * s + tn(q * keep, dn) * blocks
            total[h] = go_on * total[h] + nn(ones, dd * keep)

    wait("in")

    @pl.loop(0, 2, unroll=True)
    def _(i):
        at = pl.ds(pl.multiple_of(i * half, half), half)
        u = nt(dpre[at, :], win[...])
        n, r = norm(x[at, :])
        dx[at, :] = dm[at, :] + norm_back(u, n, r, tab[4:5, :512])
        small[1:2, :512] += jnp.sum(u * n, 0, keepdims=True)
        small[2:3, :512] += jnp.sum(u, 0, keepdims=True)


WEIGHT_SHAPES = {"in": (512, 1536), "out": (512, 512), "up": (512, 2048), "down": (4, 128, 2048)}
VMEM_LIMIT = 56 * 1024 * 1024


def flip(dp, j):
    if j % 2:
        dp = dp + 1 - 2 * (dp % 2)
    if j // 2:
        dp = (dp + 2) % 4
    return dp


LINES = (("in", 3), ("out", 1), ("up", 4), ("down", 1), ("gain_a", 1), ("gain_b", 1), ("shift_a", 1), ("shift_b", 1))


def lay_out(lines, tab, dp):
    for d in range(4):
        j = dp ^ d
        at = 0
        for layer in range(2):
            for row, (_, count) in enumerate(LINES):
                for i in range(count):
                    to = (d * count + i) * 128
                    tab[layer * 8 + row : layer * 8 + row + 1, to : to + 128] = lines[j, at // 12 : at // 12 + 1, at % 12 * 128 : at % 12 * 128 + 128]
                    at += 1


def call(body, bounds, tab, ins, weights, outs, scratch, flops, moved, kept=None, after=None, once=None, extra=None, which=(0, 1)):
    kept, once, extra = kept or {}, once or {}, extra or {}
    in_names, weight_names, out_names, once_names, extra_names = list(ins), list(weights), list(outs), list(once), list(extra)
    chunks = []
    for chunk, _ in weights.values():
        if not any(chunk is c for c in chunks):
            chunks.append(chunk)
    flat = [a for c in chunks for a in c]
    slots = {n: 2 * i for i, n in enumerate(in_names + out_names + once_names + extra_names)}
    first_weight = 2 * len(slots)
    last_slot = first_weight + 4 * len(weights)
    micros = len(which)

    def kernel(bounds_ref, tab_ref, *refs):
        refs = list(refs)
        take = lambda n: [refs.pop(0) for _ in range(n)]
        src = dict(zip(in_names, take(len(ins))))
        src.update(zip(extra_names, take(len(extra))))
        pieces = take(len(flat))
        dst = dict(zip(out_names + once_names, take(len(outs) + len(once))))
        full = dict(zip(in_names, take(len(ins))))
        whole = dict(zip(extra_names, take(len(extra))))
        held = dict(zip(weight_names, take(len(weights))))
        full.update(zip(out_names, take(len(outs))))
        whole.update(zip(once_names, take(len(once))))
        full.update(zip(kept, take(len(kept))))
        held.update(zip(scratch, take(len(scratch))))
        sems = refs.pop(0)
        dp = lax.axis_index("dp")
        tab = refs.pop(0)

        def arriving(name, m):
            return pltpu.make_async_copy(src[name].at[which[0] + m], full[name].at[m], sems.at[slots[name] + m])

        def fetching(name):
            return pltpu.make_async_copy(src[name], whole[name], sems.at[slots[name]])

        def leaving(name, m):
            return pltpu.make_async_copy(full[name].at[m], dst[name].at[m], sems.at[slots[name] + m])

        pending = {}
        for m in range(micros):
            for name in in_names:
                arriving(name, m).start()
            if m:
                continue
            for w, name in enumerate(weight_names):
                chunk, column = weights[name]
                base = 0
                for c in chunks:
                    if c is chunk:
                        break
                    base += len(c)
                width = 2048 if name == "down" else WEIGHT_SHAPES[name][1]
                for j in range(4):
                    owner = flip(dp, j)
                    piece = pieces[base + j].at[pl.ds(0, 128), pl.ds(column, width)]
                    target = held[name].at[owner] if name == "down" else held[name].at[pl.ds(pl.multiple_of(owner * 128, 128), 128), :]
                    copy = pltpu.make_async_copy(piece, target, sems.at[first_weight + 4 * w + j])
                    copy.start()
                    pending.setdefault(name, []).append(copy)
        for name in extra_names:
            fetching(name).start()
        lay_out(tab_ref, tab, dp)

        @pl.loop(0, micros)
        def _(m):
            env = {n: r.at[m] for n, r in full.items()}
            env.update(held)

            def wait(*names):
                for name in names:
                    if name in pending:

                        @pl.when(m == 0)
                        def _():
                            for copy in pending[name]:
                                copy.wait()

                    else:
                        arriving(name, m).wait()

            def done(*names):
                for name in names:
                    leaving(name, m).start()

            body(env, wait, done, (bounds_ref[which[0] + m, 0], bounds_ref[which[0] + m, 1]), tab)

        if after is not None:
            finished = []

            def finish(start, stop):
                cols = pl.ds(start, stop - start)
                for name in once_names:
                    copy = pltpu.make_async_copy(whole[name].at[:, :, cols], dst[name].at[:, :, cols], sems.at[last_slot + len(finished)])
                    copy.start()
                    finished.append(copy)

            after({**full, **whole}, lambda name: fetching(name).wait(), finish, dp)
            for copy in finished:
                copy.wait()
        for m in range(micros):
            for name in out_names:
                leaving(name, m).wait()

    hbm = pl.BlockSpec(memory_space=pltpu.HBM)
    shapes = [pltpu.VMEM((micros,) + a.shape[1:], a.dtype) for a in ins.values()]
    shapes += [pltpu.VMEM(a.shape, a.dtype) for a in extra.values()]
    shapes += [pltpu.VMEM(WEIGHT_SHAPES[w], BF16) for w in weight_names]
    per_micro = lambda s: (micros,) + s.shape
    shapes += [pltpu.VMEM(per_micro(s), s.dtype) for s in outs.values()]
    shapes += [pltpu.VMEM(s.shape, s.dtype) for s in once.values()]
    shapes += [pltpu.VMEM(per_micro(s), s.dtype) for s in kept.values()]
    shapes += [pltpu.VMEM(s.shape, s.dtype) for s in scratch.values()]
    shapes.append(pltpu.SemaphoreType.DMA((last_slot + 8,)))
    shapes.append(pltpu.VMEM((16, 2048), F32))
    results = pl.pallas_call(
        kernel,
        out_shape=[jax.ShapeDtypeStruct(per_micro(s), s.dtype) for s in outs.values()] + list(once.values()),
        in_specs=[pl.BlockSpec(memory_space=pltpu.SMEM), pl.BlockSpec(memory_space=pltpu.VMEM)] + [hbm] * (len(ins) + len(extra) + len(flat)),
        out_specs=[hbm] * (len(outs) + len(once)),
        scratch_shapes=shapes,
        compiler_params=pltpu.CompilerParams(vmem_limit_bytes=VMEM_LIMIT),
        cost_estimate=pl.CostEstimate(flops=int(flops), bytes_accessed=int(moved), transcendentals=0),
    )(bounds, tab, *ins.values(), *extra.values(), *flat)
    return dict(zip(out_names + once_names, results))


def shape(rows, columns, kind):
    return jax.ShapeDtypeStruct((rows, columns), kind)


WIDE = shape(512, 512, F32)
NARROW = shape(512, 512, BF16)
TRIPLE = shape(512, 1536, BF16)
FOUR = shape(512, 2048, BF16)
STATE = shape(272, 128, BF16)
SMALL = shape(8, 2048, F32)
CARRY = {"state": jax.ShapeDtypeStruct((2, QUAD, QUAD), F32), "total": jax.ShapeDtypeStruct((2, 8, QUAD), F32)}

PACKED = {"in": 1536, "out": 512, "up": 2048, "down": 2048}
SMALL_ROWS = 32


def parts_of(columns):
    return {"send": jax.ShapeDtypeStruct((2, 128, columns), BF16), "keep": jax.ShapeDtypeStruct((2, 128, columns), BF16)}


def weight_grads(full, names, dp, finish):
    owners = [flip(dp, j) for j in (1, 3, 0, 2)]
    at = 0

    def put(k, cols, value):
        if k < 2:
            full["send"][k, :, cols] = value.astype(BF16)
        else:
            full["keep"][k - 2, :, cols] = value.astype(BF16)

    for name, a, b in names:
        both = lambda refs, cols: jnp.concatenate([r[m, :, cols] for r, m in refs], 0)
        a, b = (n if isinstance(n, list) else [(full[n], 0), (full[n], 1)] for n in (a, b))
        if name == "down":
            b_all = both(b, slice(None))
            for k in range(4):
                for c in range(2):
                    cols = pl.ds(pl.multiple_of(owners[k] * 512 + c * 256, 128), 256)
                    value = tn(both(a, cols), b_all)
                    for half in range(2):
                        start = at + (2 * c + half) * 512
                        put(k, slice(start, start + 512), value[half * 128 : (half + 1) * 128])
        else:
            a_all = jnp.concatenate([both(a, pl.ds(pl.multiple_of(o * 128, 128), 128)) for o in owners], 1)
            for c in range(PACKED[name] // 512):
                value = tn(a_all, both(b, slice(c * 512, (c + 1) * 512)))
                for k in range(4):
                    put(k, slice(at + c * 512, at + (c + 1) * 512), value[k * 128 : (k + 1) * 128])
        finish(at, at + PACKED[name])
        at += PACKED[name]
    return at


def enter(bounds, tab, x, w):
    def body(e, wait, done, bounds, tab):
        wait("x", "in")
        f1_body(e["x"], tab.at[0:8], e["in"], e["low_a"], e["qkv"], e["st"], bounds)
        done("low_a", "qkv", "st")

    return call(body, bounds, tab, {"x": x}, {"in": w["in"]}, {"low_a": NARROW, "qkv": TRIPLE, "st": STATE}, {}, 6e9, 8e6)


def inner(bounds, tab, x, qkv, prior, w, w_next):
    def body(e, wait, done, bounds, tab):
        here, there = tab.at[0:8], tab.at[8:16]
        wait("qkv", "prior", "x")
        f2_body(e["x"], e["qkv"], e["prior"], here, e["out"], e["up"], e["down"], e["state"], e["total"], e["att"], e["inv"], e["middle"], e["low_b"], e["act"], e["slope"], e["x1"], bounds, wait, done)
        done("act", "slope", "x1")
        wait("in")
        f1_body(e["x1"], there, e["in"], e["low_a"], e["qkv1"], e["st"], bounds)
        done("low_a", "qkv1", "st")

    outs = {"att": NARROW, "inv": WIDE, "middle": WIDE, "low_b": NARROW, "act": FOUR, "slope": FOUR, "x1": WIDE, "low_a": NARROW, "qkv1": TRIPLE, "st": STATE}
    return call(body, bounds, tab, {"qkv": qkv, "prior": prior, "x": x}, {"out": w["out"], "up": w["up"], "down": w["down"], "in": w_next["in"]}, outs, CARRY, 25e9, 32e6)


BRANCHES = [("down", "act", "bb"), ("out", "att", "ba"), ("up", "low_b", "hid")]


def turn(bounds, tab, x, qkv, prior, g, w):
    def body(e, wait, done, bounds, tab):
        tab = tab.at[8:16]
        wait("qkv", "prior", "x")
        f2_body(e["x"], e["qkv"], e["prior"], tab, e["out"], e["up"], e["down"], e["state"], e["total"], e["att"], e["inv"], e["middle"], e["low_b"], e["act"], e["slope"], e["y"], bounds, wait)
        done("y")
        wait("g")
        b1_body(e["g"], tab, e["out"], e["up"], e["down"], e["qkv"], e["att"], e["inv"], e["middle"], e["slope"], e["bb"], e["hid"], e["ba"], e["dm"], e["dnum"], e["dden"], e["st"], e["small"], bounds)
        done("dm", "dnum", "dden", "st", "small")

    def after(full, wait, finish, dp):
        weight_grads(full, BRANCHES, dp, finish)

    outs = {"y": WIDE, "dm": WIDE, "dnum": NARROW, "dden": WIDE, "st": STATE, "small": SMALL}
    kept = {"att": NARROW, "low_b": NARROW, "act": FOUR, "bb": NARROW, "hid": FOUR, "ba": NARROW}
    scratch = {"inv": WIDE, "middle": WIDE, "slope": FOUR, **CARRY}
    return call(body, bounds, tab, {"qkv": qkv, "prior": prior, "x": x, "g": g}, {"out": w["out"], "up": w["up"], "down": w["down"]}, outs, scratch, 34e9, 36e6, kept, after, parts_of(4608))


def back(bounds, tab, layer, x, dm, qkv, dnum, dden, prior, later, w, which, low_a=None, first=None, smalls=None):
    def body(e, wait, done, bounds, tab):
        wait("qkv", "dnum", "dden", "prior", "later", "dm", "x")
        b2_body(e["x"], e["dm"], e["qkv"], e["dnum"], e["dden"], e["prior"], e["later"], tab.at[8 * layer : 8 * layer + 8], e["in"], e["state"], e["total"], e["dpre"], e["dx"], e["small2"], bounds, wait)
        done("dx", "small2")
        if low_a is None:
            done("dpre")

    def after(full, wait, finish, dp):
        for name in extra:
            wait(name)
        pre = "dpre" if first is None else [(full["dpre0"], 0), (full["dpre"], 0)]
        at = weight_grads(full, [("in", "low_a", pre)], dp, finish)
        if smalls:
            for k, j in enumerate((1, 3, 0, 2)):
                second = [(full["first2"], 0), (full["small2"], 0)] if first is not None else [(full["small2"], 0), (full["small2"], 1)]
                two = lambda n: [(full[n], 0), (full[n], 1)]
                lines = small_lines([two("small0"), second, two("small1"), two("other2")], flip(dp, j))
                lines = jnp.concatenate([lines, jnp.zeros((128 - SMALL_ROWS, 128), F32)], 0)
                if k < 2:
                    full["send"][k, :, at : at + 128] = lines.astype(BF16)
                else:
                    full["keep"][k - 2, :, at : at + 128] = lines.astype(BF16)
            finish(at, at + 128)

    ins = {"qkv": qkv, "dnum": dnum, "dden": dden, "prior": prior, "later": later, "dm": dm, "x": x}
    outs = {"dx": WIDE, "small2": SMALL}
    if low_a is None:
        return call(body, bounds, tab, ins, {"in": w["in"]}, {**outs, "dpre": TRIPLE}, CARRY, 10e9, 10e6, which=which)
    extra = {"low_a": low_a, **(smalls or {})}
    if first is not None:
        extra.update({"dpre0": first["dpre"], "first2": first["small2"]})
    return call(body, bounds, tab, ins, {"in": w["in"]}, outs, CARRY, 20e9, 20e6, {"dpre": TRIPLE}, after, parts_of(1664 if smalls else 1536), extra, which)


def descend(bounds, tab, g, qkv, att, inv, middle, slope, act, low_b, w):
    def body(e, wait, done, bounds, tab):
        wait("g", "slope", "middle", "inv", "att", "qkv", "out", "up", "down")
        b1_body(e["g"], tab.at[0:8], e["out"], e["up"], e["down"], e["qkv"], e["att"], e["inv"], e["middle"], e["slope"], e["bb"], e["hid"], e["ba"], e["dm"], e["dnum"], e["dden"], e["st"], e["small"], bounds)
        done("dm", "dnum", "dden", "st", "small")

    def after(full, wait, finish, dp):
        wait("act")
        wait("low_b")
        weight_grads(full, BRANCHES, dp, finish)

    ins = {"g": g, "slope": slope, "middle": middle, "inv": inv, "att": att, "qkv": qkv}
    outs = {"dm": WIDE, "dnum": NARROW, "dden": WIDE, "st": STATE, "small": SMALL}
    kept = {"bb": NARROW, "hid": FOUR, "ba": NARROW}
    return call(body, bounds, tab, ins, {"down": w["down"], "up": w["up"], "out": w["out"]}, outs, {}, 16e9, 30e6, kept, after, parts_of(4608), {"act": act, "low_b": low_b})


def small_lines(smalls, owner):
    lines = []
    for layer in range(2):
        first, second = smalls[2 * layer], smalls[2 * layer + 1]
        for ref, row, width in ((second, 0, 384), (first, 0, 128), (first, 1, 512), (first, 2, 128), (second, 1, 128), (first, 3, 128), (second, 2, 128), (first, 4, 128)):
            for i in range(width // 128):
                at = pl.ds(pl.multiple_of(owner * width + i * 128, 128), 128)
                lines.append(sum(r[m, row : row + 1, at] for r, m in ref))
    return jnp.concatenate(lines + [jnp.zeros((SMALL_ROWS - len(lines), 128), F32)], 0)


def prepare(segments, weight, params):
    def kernel(seg, weight, *refs):
        *small, out, bounds, lines = refs
        out[:128, :] = weight[0]
        lines[...] = jnp.zeros_like(lines)
        at = 0
        for layer in range(2):
            for ref, row in zip(small, (0, 0, 0, 0, 0, 1, 0, 1)):
                line = ref[layer, row : row + 1, :] if len(ref.shape) == 3 else ref[layer : layer + 1, :]
                line = line.astype(F32)
                for i in range(line.shape[1] // 128):
                    lines[at // 12 : at // 12 + 1, at % 12 * 128 : at % 12 * 128 + 128] = line[:, i * 128 : (i + 1) * 128]
                    at += 1
        out[128:, :] = lines[...].astype(BF16)
        middle_id = 3 * lax.axis_index("dp") + 1
        for m in range(2):
            row = seg[m : m + 1, :]
            for i, inside in enumerate((row < middle_id, row <= middle_id)):
                bounds[m, i] = jnp.sum(jnp.where(inside, 1.0, 0.0)).astype(jnp.int32)

    vmem = pl.BlockSpec(memory_space=pltpu.VMEM)
    return pl.pallas_call(
        kernel,
        out_shape=[jax.ShapeDtypeStruct((144, 1536), BF16), jax.ShapeDtypeStruct((2, 2), jnp.int32)],
        in_specs=[vmem] * (2 + len(params)),
        out_specs=[vmem, pl.BlockSpec(memory_space=pltpu.SMEM)],
        scratch_shapes=[pltpu.VMEM((16, 1536), F32)],
    )(segments, weight, *params)


def swap(x, axis, bit):
    n = lax.axis_size(axis)
    return lax.ppermute(x, axis, [(i, i ^ bit) for i in range(n)])


def tied(x, *after):
    return lax.optimization_barrier((x,) + after)[0]


def absolute(pieces, dp):
    stacked = jnp.stack(pieces)
    return jnp.stack([lax.dynamic_index_in_dim(stacked, dp ^ j, 0, False) for j in range(4)])


def prefix_sums(x, forward, gate=None):
    n = lax.axis_size("seq")
    place = lax.axis_index("seq")
    total, result, bit = x, 0.0, 1
    while bit < n:
        got = swap(total, "seq", bit)
        if gate is not None and bit == 4:
            got = tied(got, gate)
        got = got.astype(F32)
        high = (place // bit) % 2 == 1
        result = result + jnp.where(high if forward else ~high, got, 0.0)
        total = (total.astype(F32) + got).astype(BF16)
        if bit == 1:
            pair = total
        bit *= 2
    return result, pair


def reduce_x(near, far, gate=None):
    y = lax.axis_index("seq") % 2
    got = swap(far, "dp", 2)
    if gate is not None:
        got = tied(got, gate)
    near = near.astype(F32) + got.astype(F32)
    half = near.shape[0] // 2
    mine = lax.dynamic_slice_in_dim(near, y * half, half, 0)
    return mine, lax.dynamic_slice_in_dim(near, (1 - y) * half, half, 0).astype(BF16)


def reduce_y(mine, other, gate=None):
    got = swap(other, "seq", 1)
    if gate is not None:
        got = tied(got, gate)
    return (mine + got.astype(F32)).astype(BF16)


def scatter_z(part, bit, gate=None):
    if bit >= lax.axis_size("seq"):
        return part
    high = (lax.axis_index("seq") // bit) % 2
    half = part.shape[0] // 2
    mine = lax.dynamic_slice_in_dim(part, high * half, half, 0).astype(F32)
    got = swap(lax.dynamic_slice_in_dim(part, (1 - high) * half, half, 0), "seq", bit)
    if gate is not None:
        got = tied(got, gate)
    return (mine + got.astype(F32)).astype(BF16)


def add_z(part, bit):
    while bit < lax.axis_size("seq"):
        part = (part.astype(F32) + swap(part, "seq", bit).astype(F32)).astype(BF16)
        bit *= 2
    return part


def gather_z(part, bit):
    if bit >= lax.axis_size("seq"):
        return part
    other = swap(part, "seq", bit)
    return jnp.where((lax.axis_index("seq") // bit) % 2 == 0, jnp.concatenate([part, other]), jnp.concatenate([other, part]))


def both_halves(part):
    other = swap(part, "seq", 1)
    y = lax.axis_index("seq") % 2
    return jnp.where(y == 0, jnp.concatenate([part, other]), jnp.concatenate([other, part])).astype(F32)


def per_device(tokens, cotangent, segments, input_weight, input_bias, output_weight, output_bias, up_weight, up_bias, down_weight, down_bias, norm_gain, norm_shift):
    shard, bounds = prepare(segments, input_weight, (input_bias, output_bias, up_bias, down_bias, norm_gain, norm_gain, norm_shift, norm_shift))

    def fetch(shard, gate=None):
        across = swap(shard, "dp", 2)
        last = across if gate is None else tied(across, gate)
        return [shard, swap(shard, "dp", 1), across, swap(last, "dp", 1)]

    def packed(l):
        return [output_weight[l], up_weight[l]] + [down_weight[l][i * 128 : (i + 1) * 128] for i in range(4)]

    first = fetch(shard)
    tab = jnp.stack([p[128:144] for p in first]).astype(F32)
    second = tied(jnp.concatenate(packed(0) + [input_weight[1]], 1), first[1])
    e = enter(bounds, tab, tokens, {"in": (first, 0)})
    prior0, _ = prefix_sums(e["st"], True)
    second = fetch(second, prior0)
    ws = [{"in": (first, 0), "out": (second, 0), "up": (second, 512), "down": (second, 2560)}, {"in": (second, 4608)}]
    i = inner(bounds, tab, tokens, e["qkv"], prior0, ws[0], ws[1])
    third = fetch(tied(jnp.concatenate(packed(1), 1), prior0), i["st"])
    ws[1].update({"out": (third, 0), "up": (third, 512), "down": (third, 2560)})
    prior1, _ = prefix_sums(i["st"], True)
    t = turn(bounds, tab, i["x1"], i["qkv1"], prior1, cotangent, ws[1])

    def cores(parts, *after):
        both = parts["keep"].astype(F32) + swap(tied(parts["send"], *after), "dp", 1).astype(F32)
        both = both.astype(BF16)
        return both[0], both[1]

    near_a, far_a = cores(t)
    later1, _ = prefix_sums(t["st"], False, far_a)
    b = back(bounds, tab, 1, i["x1"], tied(t["dm"], far_a), i["qkv1"], t["dnum"], t["dden"], prior1, later1, ws[1], (0, 1), i["low_a"])
    ready_1 = reduce_x(near_a[:, :2560], far_a[:, :2560], b["small2"])
    near_b, far_b = cores(b, *ready_1)
    near_2, far_2 = jnp.concatenate([near_a[:, 2560:], near_b], 1), jnp.concatenate([far_a[:, 2560:], far_b], 1)
    d = descend(bounds, tab, tied(b["dx"], far_2, *ready_1), e["qkv"], i["att"], i["inv"], i["middle"], i["slope"], i["act"], i["low_b"], ws[0])
    ready_2 = reduce_x(near_2, far_2, d["small"])
    near_d, far_d = cores(d)
    later0, pair = prefix_sums(tied(d["st"], *ready_2), False, far_d)
    part_2 = jnp.concatenate([reduce_y(*ready_1, d["small"]), reduce_y(ready_2[0], tied(ready_2[1], pair), far_d)], 1)
    lower = lambda which, dm, **more: back(bounds, tab, 0, tokens, dm, e["qkv"], d["dnum"], d["dden"], prior0, later0, ws[0], which, **more)
    v0 = lower((0,), tied(d["dm"], far_d, part_2))
    part_2 = scatter_z(part_2, 2, v0["small2"])
    ready_d1 = reduce_x(near_d[:, :2048], far_d[:, :2048], v0["small2"])
    v = lower((1,), tied(d["dm"], part_2, *ready_d1), low_a=e["low_a"], first=v0, smalls={"small0": d["small"], "small1": t["small"], "other2": b["small2"]})
    part_2 = add_z(scatter_z(part_2, 4, v["small2"]), 8)
    ready_d2 = reduce_x(near_d[:, 2048:], far_d[:, 2048:], v["small2"])
    near_c, far_c = cores(v, *ready_d2)
    ready_c = reduce_x(near_c, far_c)
    part_d = jnp.concatenate([reduce_y(*ready_d1, v["small2"]), reduce_y(ready_d2[0], tied(ready_d2[1], far_c))], 1)
    part_2 = gather_z(tied(part_2, far_c), 4)
    part_d = scatter_z(tied(part_d, ready_c[1], part_2), 2)
    part_c = reduce_y(*ready_c)
    part_d = scatter_z(tied(part_d, part_c), 4)
    part_2 = gather_z(part_2, 2)
    part_c = add_z(part_c, 2)
    part_d = gather_z(gather_z(tied(add_z(part_d, 8), part_2), 4), 2)
    in0, sum_2, sum_d = both_halves(part_c), both_halves(part_2), both_halves(part_d)
    down1, out1, up1, in1 = sum_2[:, :2048], sum_2[:, 2048:2560], sum_2[:, 2560:4608], sum_2[:, 4608:]
    down0, out0, up0 = sum_d[:, :2048], sum_d[:, 2048:2560], sum_d[:, 2560:]
    lines = in0[:SMALL_ROWS, 1536:].reshape(-1)
    layers = []
    for l in range(2):
        at, got = l * 1664, []
        for width in (384, 128, 512, 128, 128, 128, 128, 128):
            got.append(lines[at : at + width])
            at += width
        layers.append(got)
    small = lambda k: jnp.stack([layers[l][k] for l in range(2)])
    stacked = lambda d: jnp.concatenate([d[:, c * 512 : (c + 1) * 512] for c in range(4)])
    return (
        t["y"],
        jnp.concatenate([v0["dx"], tied(v["dx"], far_c)]),
        jnp.stack([in0[:, :1536], in1]),
        small(0),
        jnp.stack([out0, out1]),
        small(1),
        jnp.stack([up0, up1]),
        small(2),
        jnp.stack([stacked(down0), stacked(down1)]),
        small(3),
        jnp.stack([small(4), small(5)], 1),
        jnp.stack([small(6), small(7)], 1),
    )


def solution(mesh):
    rows = P(None, ("dp", "seq"), None)
    split = P(None, "dp", None)
    flat = P(None, "dp")
    last = P(None, None, "dp")
    params = (split, flat, split, flat, split, flat, split, flat, last, last)
    return jax.shard_map(
        per_device,
        mesh=mesh,
        in_specs=(rows, rows, P(None, ("dp", "seq"))) + params,
        out_specs=(rows, rows) + params,
        check_vma=False,
    )
```

```python
import jax
import jax.numpy as jnp
from jax import lax
from jax.experimental import pallas as pl
from jax.experimental.pallas import tpu as pltpu
from jax.sharding import PartitionSpec as P

HEAD = 64
EPSILON = 1e-05
F32 = jnp.float32
BF16 = jnp.bfloat16
ROWS = 512
TILE = 128
QUAD = 256
NT = (((1,), (1,)), ((), ()))
TN = (((0,), (0,)), ((), ()))
GELU = 0.7978845608028654
CUBE = 0.044715


def nn(a, b):
    return jnp.dot(a, b, preferred_element_type=F32)


def nt(a, b):
    return lax.dot_general(a, b, NT, preferred_element_type=F32)


def tn(a, b):
    return lax.dot_general(a, b, TN, preferred_element_type=F32)


def norm(x):
    mean = jnp.mean(x, -1, keepdims=True)
    c = x - mean
    r = lax.rsqrt(jnp.mean(c * c, -1, keepdims=True) + EPSILON)
    return c * r, r


def norm_back(u, n, r, gain):
    s = u * gain
    return r * (s - jnp.mean(s, -1, keepdims=True) - n * jnp.mean(s * n, -1, keepdims=True))


def iota(shape, dim):
    return lax.broadcasted_iota(jnp.int32, shape, dim)


def class_of(row, bounds):
    one = jnp.int32(1)
    zero = jnp.int32(0)
    return jnp.where(row >= bounds[0], one, zero) + jnp.where(row >= bounds[1], one, zero)


def head_masks():
    lane = iota((1, QUAD), 1) // HEAD
    return [jnp.where(lane == h, 1.0, 0.0).astype(BF16) for h in range(4)]


def spread(a, masks):
    return jnp.concatenate([a * m for m in masks], 0)


def block_mask():
    return jnp.where(iota((QUAD, QUAD), 0) // HEAD == iota((QUAD, QUAD), 1) // HEAD, 1.0, 0.0).astype(F32)


def same_mask(j, bounds, row_dim):
    t = iota((TILE, TILE), row_dim) + j * TILE
    s = iota((TILE, TILE), 1 - row_dim) + j * TILE
    keep = (s <= t) & (class_of(s, bounds) == class_of(t, bounds))
    return jnp.where(keep, 1.0, 0.0).astype(F32)


def rows_of_class(j, bounds, which, width=QUAD):
    return jnp.where(class_of(iota((TILE, width), 0) + j * TILE, bounds) == which, 1.0, 0.0).astype(F32)


def unpack_state(packed, state, total):
    lane = iota((HEAD, TILE), 1)
    left = jnp.where(lane < HEAD, 1.0, 0.0).astype(F32)
    state[...] = jnp.zeros_like(state)
    for pair in range(4):
        at = pl.ds(pair % 2 * TILE, TILE)
        c = packed[pair * HEAD : (pair + 1) * HEAD, :]
        state[pair // 2, at, at] = jnp.concatenate([c * left, c * (1.0 - left)], 0)
        total[pair // 2, :, at] = jnp.broadcast_to(packed[256 + pair : 257 + pair, :], (8, TILE))


def pack_state(quads, totals, packed):
    lane = iota((HEAD, TILE), 1)
    left = jnp.where(lane < HEAD, 1.0, 0.0).astype(F32)
    for pair in range(4):
        at = pair % 2 * TILE
        block = quads[pair // 2][at : at + TILE, at : at + TILE]
        c = block[:HEAD] * left + block[HEAD:] * (1.0 - left)
        packed[pair * HEAD : (pair + 1) * HEAD, :] = c.astype(BF16)
    lines = [totals[p // 2][:1, p % 2 * TILE : (p % 2 + 1) * TILE] for p in range(4)]
    packed[256:272, :] = jnp.concatenate(lines + [jnp.zeros((12, TILE), F32)], 0).astype(BF16)


def f1_body(x, tab, win, low_a, qkv, st, bounds, wait):
    half = ROWS // 2

    for i in range(2):
        at = pl.ds(i * half, half)
        n, _ = norm(x[at, :])
        low = (n * tab[4:5, :512] + tab[6:7, :512]).astype(BF16)
        low_a[at, :] = low
        if i == 0:
            wait("in")
        for c in range(3):
            cols = slice(c * 512, (c + 1) * 512)
            pre = nn(low, win[:, cols]) + tab[0:1, cols]
            if c < 2:
                pre = jnp.where(pre > 0, pre + 1.0, jnp.exp(jnp.minimum(pre, 0.0)))
            qkv[at, cols] = pre.astype(BF16)

    mid = jnp.where(class_of(iota((ROWS, QUAD), 0), bounds) == 1, 1.0, 0.0).astype(BF16)
    ones = jnp.ones((8, ROWS), BF16)
    quads, totals = [], []
    for h in range(2):
        k = qkv[:, 512 + h * QUAD : 512 + (h + 1) * QUAD] * mid
        quads.append(tn(k, qkv[:, 1024 + h * QUAD : 1024 + (h + 1) * QUAD]))
        totals.append(nn(ones, k))
    pack_state(quads, totals, st)


def forward_masks(j, bounds):
    first = j * TILE
    carried = jnp.where(j == 0, jnp.int32(1), class_of(first - 1, bounds))
    last = class_of(first + TILE - 1, bounds)
    go_on = jnp.where(carried == last, 1.0, 0.0).astype(F32)
    return rows_of_class(j, bounds, carried), rows_of_class(j, bounds, last).astype(BF16), go_on


def backward_masks(j, bounds):
    first = j * TILE
    carried = jnp.where(j == ROWS // TILE - 1, jnp.int32(1), class_of(first + TILE, bounds))
    here = class_of(first, bounds)
    go_on = jnp.where(carried == here, 1.0, 0.0).astype(F32)
    return rows_of_class(j, bounds, carried), rows_of_class(j, bounds, here).astype(BF16), go_on


def f2_body(x, qkv, prior, tab, wout, wup, wdn, state, total, att, inv, middle, low_b, act, slope, out, bounds, wait, done=lambda *names: None):
    unpack_state(prior, state, total)
    half = ROWS // 2

    @pl.loop(0, ROWS // TILE, unroll=True)
    def _(j):
        at = pl.ds(pl.multiple_of(j * TILE, TILE), TILE)
        masks = head_masks()
        blocks = block_mask()
        ones_block = blocks.astype(BF16)
        same = same_mask(j, bounds, 0)
        same4 = jnp.concatenate([same] * 4, 1)
        reads, keep, go_on = forward_masks(j, bounds)
        ones = jnp.ones((8, TILE), BF16)
        for h in range(2):
            q, k, v = (qkv[at, i * 512 + h * QUAD : i * 512 + (h + 1) * QUAD] for i in range(3))
            s = state[h]
            p = (nt(q, spread(k, masks)) * same4).astype(BF16)
            num = nn(p, spread(v, masks)) + reads * nn(q, s.astype(BF16))
            ksum = nn(same.astype(BF16), k) + reads * total[h, 0:1, :]
            den = nn((q.astype(F32) * ksum).astype(BF16), ones_block)
            r = 1.0 / den
            att[at, h * QUAD : (h + 1) * QUAD] = (num * r).astype(BF16)
            inv[at, h * QUAD : (h + 1) * QUAD] = r
            km = k * keep
            state[h] = go_on * s + tn(km, v) * blocks
            total[h] = go_on * total[h] + nn(ones, km)

    done("att", "inv")
    wait("x", "out")

    @pl.loop(0, 2, unroll=True)
    def _(i):
        at = pl.ds(pl.multiple_of(i * half, half), half)
        m = x[at, :] + nn(att[at, :], wout[...]) + tab[1:2, :512]
        middle[at, :] = m
        n, _ = norm(m)
        low_b[at, :] = (n * tab[5:6, :512] + tab[7:8, :512]).astype(BF16)

    done("middle", "low_b")
    wait("up")
    wait("down")

    @pl.loop(0, 2, unroll=True)
    def _(i):
        at = pl.ds(pl.multiple_of(i * half, half), half)
        low = low_b[at, :]
        for c in range(4):
            cols = slice(c * 512, (c + 1) * 512)
            h = nn(low, wup[:, cols]) + tab[2:3, cols]
            h2 = h * h
            t = jnp.tanh(h * (GELU + GELU * CUBE * h2))
            up = 0.5 + 0.5 * t
            act[at, cols] = (h * up).astype(BF16)
            slope[at, cols] = (up + up * (1.0 - t) * h * (GELU + 3.0 * GELU * CUBE * h2)).astype(BF16)
        o = middle[at, :] + tab[3:4, :512]
        for c in range(4):
            o = o + nn(act[at, c * 512 : (c + 1) * 512], down_block(wdn, c))
        out[at, :] = o


def down_block(wdn, c):
    return jnp.concatenate([wdn[c, :, i * 512 : (i + 1) * 512] for i in range(4)], 0)


def b1_body(g, tab, wout, wup, wdn, qkv, att, inv, middle, slope, branch_b, hid, branch_a, dm, dnum, dden, st, small, bounds, wait=lambda *names: None):
    half = ROWS // 2
    small[...] = jnp.zeros_like(small)

    for i in range(2):
        at = pl.ds(i * half, half)
        if i == 0:
            wait("g", "down", "slope")
        gi = g[at, :]
        bb = gi.astype(BF16)
        branch_b[at, :] = bb
        for c in range(4):
            cols = slice(c * 512, (c + 1) * 512)
            dh = nt(bb, down_block(wdn, c)) * slope[at, cols].astype(F32)
            hid[at, cols] = dh.astype(BF16)
            small[1:2, cols] += jnp.sum(dh, 0, keepdims=True)
        if i == 0:
            wait("up", "middle")
        u = nt(hid[at, :], wup[...])
        n, r = norm(middle[at, :])
        d = gi + norm_back(u, n, r, tab[5:6, :512])
        dm[at, :] = d
        ba = d.astype(BF16)
        branch_a[at, :] = ba
        small[0:1, :512] += jnp.sum(d, 0, keepdims=True)
        small[2:3, :512] += jnp.sum(gi, 0, keepdims=True)
        small[3:4, :512] += jnp.sum(u * n, 0, keepdims=True)
        small[4:5, :512] += jnp.sum(u, 0, keepdims=True)
        if i == 0:
            wait("out", "inv", "att", "qkv")
        da = nt(ba, wout[...])
        ones_block = block_mask().astype(BF16)
        for h in range(2):
            cols = slice(h * QUAD, (h + 1) * QUAD)
            r = inv[at, cols]
            a = da[:, cols]
            dnum[at, cols] = (a * r).astype(BF16)
            dden[at, cols] = -r * nn((a * att[at, cols].astype(F32)).astype(BF16), ones_block)

    mid = jnp.where(class_of(iota((ROWS, QUAD), 0), bounds) == 1, 1.0, 0.0).astype(BF16)
    quads, totals = [], []
    for h in range(2):
        cols = slice(h * QUAD, (h + 1) * QUAD)
        q = qkv[:, cols] * mid
        quads.append(tn(q, dnum[:, cols]))
        totals.append(jnp.sum(q.astype(F32) * dden[:, cols], 0, keepdims=True))
    pack_state(quads, totals, st)


def b2_body(x, dm, qkv, dnum, dden, prior, later, tab, win, state, total, dpre, dx, small, bounds, wait, done):
    half = ROWS // 2
    count = ROWS // TILE
    small[...] = jnp.zeros_like(small)
    unpack_state(prior, state, total)

    @pl.loop(0, count, unroll=True)
    def _(j):
        at = pl.ds(pl.multiple_of(j * TILE, TILE), TILE)
        masks = head_masks()
        blocks = block_mask()
        same = same_mask(j, bounds, 0)
        same4 = jnp.concatenate([same] * 4, 1)
        reads, keep, go_on = forward_masks(j, bounds)
        ones = jnp.ones((8, TILE), BF16)
        for h in range(2):
            cols = slice(h * QUAD, (h + 1) * QUAD)
            q, k, v = (qkv[at, i * 512 + h * QUAD : i * 512 + (h + 1) * QUAD] for i in range(3))
            dn = dnum[at, cols]
            s = state[h]
            ds = (nt(dn, spread(v, masks)) * same4).astype(BF16)
            ksum = nn(same.astype(BF16), k) + reads * total[h, 0:1, :]
            dq = nn(ds, spread(k, masks)) + reads * nt(dn, s.astype(BF16)) + dden[at, cols] * ksum
            dq = dq * jnp.minimum(q.astype(F32), 1.0)
            dpre[at, cols] = dq.astype(BF16)
            small[0:1, cols] += jnp.sum(dq, 0, keepdims=True)
            km = k * keep
            state[h] = go_on * s + tn(km, v) * blocks
            total[h] = go_on * total[h] + nn(ones, km)

    wait("later")
    unpack_state(later, state, total)

    @pl.loop(0, count, unroll=True)
    def _(back):
        j = count - 1 - back
        at = pl.ds(pl.multiple_of(j * TILE, TILE), TILE)
        masks = head_masks()
        blocks = block_mask()
        same = same_mask(j, bounds, 1)
        same4 = jnp.concatenate([same] * 4, 1)
        reads, keep, go_on = backward_masks(j, bounds)
        ones = jnp.ones((8, TILE), BF16)
        for h in range(2):
            cols = slice(h * QUAD, (h + 1) * QUAD)
            q, k, v = (qkv[at, i * 512 + h * QUAD : i * 512 + (h + 1) * QUAD] for i in range(3))
            dn = dnum[at, cols]
            s = state[h]
            low = s.astype(BF16)
            qx = spread(q, masks)
            dx_ = spread(dn, masks)
            sc = (nt(k, qx) * same4).astype(BF16)
            ds = (nt(v, dx_) * same4).astype(BF16)
            dv = nn(sc, dx_) + reads * nn(k, low)
            dd = (dden[at, cols] * q.astype(F32)).astype(BF16)
            dk = nn(ds, qx) + reads * (nt(v, low) + total[h, 0:1, :]) + nn(same.astype(BF16), dd)
            dk = dk * jnp.minimum(k.astype(F32), 1.0)
            kc = slice(512 + h * QUAD, 512 + (h + 1) * QUAD)
            vc = slice(1024 + h * QUAD, 1024 + (h + 1) * QUAD)
            dpre[at, kc] = dk.astype(BF16)
            dpre[at, vc] = dv.astype(BF16)
            small[0:1, kc] += jnp.sum(dk, 0, keepdims=True)
            small[0:1, vc] += jnp.sum(dv, 0, keepdims=True)
            state[h] = go_on * s + tn(q * keep, dn) * blocks
            total[h] = go_on * total[h] + nn(ones, dd * keep)

    done("dpre")
    wait("in", "dm", "x")

    @pl.loop(0, 2, unroll=True)
    def _(i):
        at = pl.ds(pl.multiple_of(i * half, half), half)
        u = nt(dpre[at, :], win[...])
        n, r = norm(x[at, :])
        dx[at, :] = dm[at, :] + norm_back(u, n, r, tab[4:5, :512])
        small[1:2, :512] += jnp.sum(u * n, 0, keepdims=True)
        small[2:3, :512] += jnp.sum(u, 0, keepdims=True)


WEIGHT_SHAPES = {"in": (512, 1536), "out": (512, 512), "up": (512, 2048), "down": (4, 128, 2048)}
VMEM_LIMIT = 56 * 1024 * 1024


def flip(dp, j):
    if j % 2:
        dp = dp + 1 - 2 * (dp % 2)
    if j // 2:
        dp = (dp + 2) % 4
    return dp


LINES = (("in", 3), ("out", 1), ("up", 4), ("down", 1), ("gain_a", 1), ("gain_b", 1), ("shift_a", 1), ("shift_b", 1))


def lay_out(lines, tab, dp):
    for d in range(4):
        j = dp ^ d
        at = 0
        for layer in range(2):
            for row, (_, count) in enumerate(LINES):
                for i in range(count):
                    to = (d * count + i) * 128
                    tab[layer * 8 + row : layer * 8 + row + 1, to : to + 128] = lines[j, at // 12 : at // 12 + 1, at % 12 * 128 : at % 12 * 128 + 128]
                    at += 1


def call(body, bounds, tab, ins, weights, outs, scratch, flops, moved, kept=None, after=None, once=None, extra=None, which=(0, 1), order=None):
    kept, once, extra = kept or {}, once or {}, extra or {}
    in_names, weight_names, out_names, once_names, extra_names = list(ins), list(weights), list(outs), list(once), list(extra)
    chunks = []
    for chunk, _ in weights.values():
        if not any(chunk is c for c in chunks):
            chunks.append(chunk)
    flat = [a for c in chunks for a in c]
    slots = {n: 2 * i for i, n in enumerate(in_names + out_names + once_names + extra_names)}
    first_weight = 2 * len(slots)
    last_slot = first_weight + 4 * len(weights)
    micros = len(which)

    def kernel(bounds_ref, tab_ref, *refs):
        refs = list(refs)
        take = lambda n: [refs.pop(0) for _ in range(n)]
        src = dict(zip(in_names, take(len(ins))))
        src.update(zip(extra_names, take(len(extra))))
        pieces = take(len(flat))
        dst = dict(zip(out_names + once_names, take(len(outs) + len(once))))
        full = dict(zip(in_names, take(len(ins))))
        whole = dict(zip(extra_names, take(len(extra))))
        held = dict(zip(weight_names, take(len(weights))))
        full.update(zip(out_names, take(len(outs))))
        whole.update(zip(once_names, take(len(once))))
        full.update(zip(kept, take(len(kept))))
        held.update(zip(scratch, take(len(scratch))))
        sems = refs.pop(0)
        dp = lax.axis_index("dp")
        tab = refs.pop(0)

        def arriving(name, m):
            return pltpu.make_async_copy(src[name].at[which[0] + m], full[name].at[m], sems.at[slots[name] + m])

        def fetching(name):
            return pltpu.make_async_copy(src[name], whole[name], sems.at[slots[name]])

        def leaving(name, m):
            return pltpu.make_async_copy(full[name].at[m], dst[name].at[m], sems.at[slots[name] + m])

        pending = {}
        for m in range(micros):
            for name in order or in_names + weight_names:
                if name in in_names:
                    arriving(name, m).start()
                if m or name in in_names:
                    continue
                w = weight_names.index(name)
                chunk, column = weights[name]
                base = 0
                for c in chunks:
                    if c is chunk:
                        break
                    base += len(c)
                width = 2048 if name == "down" else WEIGHT_SHAPES[name][1]
                for j in range(4):
                    owner = flip(dp, j)
                    piece = pieces[base + j].at[pl.ds(0, 128), pl.ds(column, width)]
                    target = held[name].at[owner] if name == "down" else held[name].at[pl.ds(pl.multiple_of(owner * 128, 128), 128), :]
                    copy = pltpu.make_async_copy(piece, target, sems.at[first_weight + 4 * w + j])
                    copy.start()
                    pending.setdefault(name, []).append(copy)
        for name in extra_names:
            fetching(name).start()
        lay_out(tab_ref, tab, dp)

        @pl.loop(0, micros)
        def _(m):
            env = {n: r.at[m] for n, r in full.items()}
            env.update(held)

            def wait(*names):
                for name in names:
                    if name in pending:

                        @pl.when(m == 0)
                        def _():
                            for copy in pending[name]:
                                copy.wait()

                    else:
                        arriving(name, m).wait()

            def done(*names):
                for name in names:
                    leaving(name, m).start()

            body(env, wait, done, (bounds_ref[which[0] + m, 0], bounds_ref[which[0] + m, 1]), tab)

        if after is not None:
            finished = []

            def finish(start, stop):
                cols = pl.ds(start, stop - start)
                for name in once_names:
                    copy = pltpu.make_async_copy(whole[name].at[:, :, cols], dst[name].at[:, :, cols], sems.at[last_slot + len(finished)])
                    copy.start()
                    finished.append(copy)

            after({**full, **whole}, lambda name: fetching(name).wait(), finish, dp)
            for copy in finished:
                copy.wait()
        for m in range(micros):
            for name in out_names:
                leaving(name, m).wait()

    hbm = pl.BlockSpec(memory_space=pltpu.HBM)
    shapes = [pltpu.VMEM((micros,) + a.shape[1:], a.dtype) for a in ins.values()]
    shapes += [pltpu.VMEM(a.shape, a.dtype) for a in extra.values()]
    shapes += [pltpu.VMEM(WEIGHT_SHAPES[w], BF16) for w in weight_names]
    per_micro = lambda s: (micros,) + s.shape
    shapes += [pltpu.VMEM(per_micro(s), s.dtype) for s in outs.values()]
    shapes += [pltpu.VMEM(s.shape, s.dtype) for s in once.values()]
    shapes += [pltpu.VMEM(per_micro(s), s.dtype) for s in kept.values()]
    shapes += [pltpu.VMEM(s.shape, s.dtype) for s in scratch.values()]
    shapes.append(pltpu.SemaphoreType.DMA((last_slot + 8,)))
    shapes.append(pltpu.VMEM((16, 2048), F32))
    results = pl.pallas_call(
        kernel,
        out_shape=[jax.ShapeDtypeStruct(per_micro(s), s.dtype) for s in outs.values()] + list(once.values()),
        in_specs=[pl.BlockSpec(memory_space=pltpu.SMEM), pl.BlockSpec(memory_space=pltpu.VMEM)] + [hbm] * (len(ins) + len(extra) + len(flat)),
        out_specs=[hbm] * (len(outs) + len(once)),
        scratch_shapes=shapes,
        compiler_params=pltpu.CompilerParams(vmem_limit_bytes=VMEM_LIMIT),
        cost_estimate=pl.CostEstimate(flops=int(flops), bytes_accessed=int(moved), transcendentals=0),
    )(bounds, tab, *ins.values(), *extra.values(), *flat)
    return dict(zip(out_names + once_names, results))


def shape(rows, columns, kind):
    return jax.ShapeDtypeStruct((rows, columns), kind)


WIDE = shape(512, 512, F32)
NARROW = shape(512, 512, BF16)
TRIPLE = shape(512, 1536, BF16)
FOUR = shape(512, 2048, BF16)
STATE = shape(272, 128, BF16)
SMALL = shape(8, 2048, F32)
CARRY = {"state": jax.ShapeDtypeStruct((2, QUAD, QUAD), F32), "total": jax.ShapeDtypeStruct((2, 8, QUAD), F32)}

PACKED = {"in": 1536, "out": 512, "up": 2048, "down": 2048}
SMALL_ROWS = 32


def parts_of(columns):
    return {"send": jax.ShapeDtypeStruct((2, 128, columns), BF16), "keep": jax.ShapeDtypeStruct((2, 128, columns), BF16)}


def weight_grads(full, names, dp, finish):
    owners = [flip(dp, j) for j in (1, 3, 0, 2)]
    at = 0

    def put(k, cols, value):
        if k < 2:
            full["send"][k, :, cols] = value.astype(BF16)
        else:
            full["keep"][k - 2, :, cols] = value.astype(BF16)

    for name, a, b in names:
        both = lambda refs, cols: jnp.concatenate([r[m, :, cols] for r, m in refs], 0)
        a, b = (n if isinstance(n, list) else [(full[n], 0), (full[n], 1)] for n in (a, b))
        if name == "down":
            b_all = both(b, slice(None))
            for k in range(4):
                for c in range(2):
                    cols = pl.ds(pl.multiple_of(owners[k] * 512 + c * 256, 128), 256)
                    value = tn(both(a, cols), b_all)
                    for half in range(2):
                        start = at + (2 * c + half) * 512
                        put(k, slice(start, start + 512), value[half * 128 : (half + 1) * 128])
        else:
            a_all = jnp.concatenate([both(a, pl.ds(pl.multiple_of(o * 128, 128), 128)) for o in owners], 1)
            for c in range(PACKED[name] // 512):
                value = tn(a_all, both(b, slice(c * 512, (c + 1) * 512)))
                for k in range(4):
                    put(k, slice(at + c * 512, at + (c + 1) * 512), value[k * 128 : (k + 1) * 128])
        finish(at, at + PACKED[name])
        at += PACKED[name]
    return at


def enter(bounds, tab, x, w):
    def body(e, wait, done, bounds, tab):
        wait("x")
        f1_body(e["x"], tab.at[0:8], e["in"], e["low_a"], e["qkv"], e["st"], bounds, wait)
        done("low_a", "qkv", "st")

    return call(body, bounds, tab, {"x": x}, {"in": w["in"]}, {"low_a": NARROW, "qkv": TRIPLE, "st": STATE}, {}, 6e9, 8e6)


def inner(bounds, tab, x, qkv, prior, w, w_next):
    def body(e, wait, done, bounds, tab):
        here, there = tab.at[0:8], tab.at[8:16]
        wait("qkv", "prior")
        f2_body(e["x"], e["qkv"], e["prior"], here, e["out"], e["up"], e["down"], e["state"], e["total"], e["att"], e["inv"], e["middle"], e["low_b"], e["act"], e["slope"], e["x1"], bounds, wait, done)
        done("act", "slope", "x1")
        f1_body(e["x1"], there, e["in"], e["low_a"], e["qkv1"], e["st"], bounds, wait)
        done("low_a", "qkv1", "st")

    outs = {"att": NARROW, "inv": WIDE, "middle": WIDE, "low_b": NARROW, "act": FOUR, "slope": FOUR, "x1": WIDE, "low_a": NARROW, "qkv1": TRIPLE, "st": STATE}
    return call(body, bounds, tab, {"qkv": qkv, "prior": prior, "x": x}, {"out": w["out"], "up": w["up"], "down": w["down"], "in": w_next["in"]}, outs, CARRY, 25e9, 32e6)


BRANCHES = [("down", "act", "bb"), ("out", "att", "ba"), ("up", "low_b", "hid")]


def turn(bounds, tab, x, qkv, prior, g, w):
    def body(e, wait, done, bounds, tab):
        tab = tab.at[8:16]
        wait("qkv", "prior")
        f2_body(e["x"], e["qkv"], e["prior"], tab, e["out"], e["up"], e["down"], e["state"], e["total"], e["att"], e["inv"], e["middle"], e["low_b"], e["act"], e["slope"], e["y"], bounds, wait)
        done("y")
        wait("g")
        b1_body(e["g"], tab, e["out"], e["up"], e["down"], e["qkv"], e["att"], e["inv"], e["middle"], e["slope"], e["bb"], e["hid"], e["ba"], e["dm"], e["dnum"], e["dden"], e["st"], e["small"], bounds)
        done("dm", "dnum", "dden", "st", "small")

    def after(full, wait, finish, dp):
        weight_grads(full, BRANCHES, dp, finish)

    outs = {"y": WIDE, "dm": WIDE, "dnum": NARROW, "dden": WIDE, "st": STATE, "small": SMALL}
    kept = {"att": NARROW, "low_b": NARROW, "act": FOUR, "bb": NARROW, "hid": FOUR, "ba": NARROW}
    scratch = {"inv": WIDE, "middle": WIDE, "slope": FOUR, **CARRY}
    return call(body, bounds, tab, {"qkv": qkv, "prior": prior, "x": x, "g": g}, {"out": w["out"], "up": w["up"], "down": w["down"]}, outs, scratch, 34e9, 36e6, kept, after, parts_of(4608))


def back(bounds, tab, layer, x, dm, qkv, dnum, dden, prior, later, w, which, low_a=None, first=None, smalls=None):
    def body(e, wait, done, bounds, tab):
        wait("qkv", "dnum", "dden", "prior")
        b2_body(e["x"], e["dm"], e["qkv"], e["dnum"], e["dden"], e["prior"], e["later"], tab.at[8 * layer : 8 * layer + 8], e["in"], e["state"], e["total"], e["dpre"], e["dx"], e["small2"], bounds, wait, done if low_a is None else lambda name: None)
        done("dx", "small2")

    def after(full, wait, finish, dp):
        for name in extra:
            wait(name)
        pre = "dpre" if first is None else [(full["dpre0"], 0), (full["dpre"], 0)]
        at = weight_grads(full, [("in", "low_a", pre)], dp, finish)
        if smalls:
            for k, j in enumerate((1, 3, 0, 2)):
                second = [(full["first2"], 0), (full["small2"], 0)] if first is not None else [(full["small2"], 0), (full["small2"], 1)]
                two = lambda n: [(full[n], 0), (full[n], 1)]
                lines = small_lines([two("small0"), second, two("small1"), two("other2")], flip(dp, j))
                lines = jnp.concatenate([lines, jnp.zeros((128 - SMALL_ROWS, 128), F32)], 0)
                if k < 2:
                    full["send"][k, :, at : at + 128] = lines.astype(BF16)
                else:
                    full["keep"][k - 2, :, at : at + 128] = lines.astype(BF16)
            finish(at, at + 128)

    ins = {"qkv": qkv, "dnum": dnum, "dden": dden, "prior": prior, "later": later, "dm": dm, "x": x}
    outs = {"dx": WIDE, "small2": SMALL}
    if low_a is None:
        return call(body, bounds, tab, ins, {"in": w["in"]}, {**outs, "dpre": TRIPLE}, CARRY, 10e9, 10e6, which=which)
    extra = {"low_a": low_a, **(smalls or {})}
    if first is not None:
        extra.update({"dpre0": first["dpre"], "first2": first["small2"]})
    return call(body, bounds, tab, ins, {"in": w["in"]}, outs, CARRY, 20e9, 20e6, {"dpre": TRIPLE}, after, parts_of(1664 if smalls else 1536), extra, which)


def descend(bounds, tab, g, qkv, att, inv, middle, slope, act, low_b, w):
    def body(e, wait, done, bounds, tab):
        b1_body(e["g"], tab.at[0:8], e["out"], e["up"], e["down"], e["qkv"], e["att"], e["inv"], e["middle"], e["slope"], e["bb"], e["hid"], e["ba"], e["dm"], e["dnum"], e["dden"], e["st"], e["small"], bounds, wait)
        done("dm", "dnum", "dden", "st", "small")

    def after(full, wait, finish, dp):
        wait("act")
        wait("low_b")
        weight_grads(full, BRANCHES, dp, finish)

    ins = {"g": g, "slope": slope, "middle": middle, "inv": inv, "att": att, "qkv": qkv}
    outs = {"dm": WIDE, "dnum": NARROW, "dden": WIDE, "st": STATE, "small": SMALL}
    kept = {"bb": NARROW, "hid": FOUR, "ba": NARROW}
    return call(body, bounds, tab, ins, {"down": w["down"], "up": w["up"], "out": w["out"]}, outs, {}, 16e9, 30e6, kept, after, parts_of(4608), {"act": act, "low_b": low_b}, order=("g", "down", "slope", "up", "middle", "out", "inv", "att", "qkv"))


def small_lines(smalls, owner):
    lines = []
    for layer in range(2):
        first, second = smalls[2 * layer], smalls[2 * layer + 1]
        for ref, row, width in ((second, 0, 384), (first, 0, 128), (first, 1, 512), (first, 2, 128), (second, 1, 128), (first, 3, 128), (second, 2, 128), (first, 4, 128)):
            for i in range(width // 128):
                at = pl.ds(pl.multiple_of(owner * width + i * 128, 128), 128)
                lines.append(sum(r[m, row : row + 1, at] for r, m in ref))
    return jnp.concatenate(lines + [jnp.zeros((SMALL_ROWS - len(lines), 128), F32)], 0)


def prepare(segments, weight, params):
    def kernel(seg, weight, *refs):
        *small, out, bounds, lines = refs
        out[:128, :] = weight[0]
        lines[...] = jnp.zeros_like(lines)
        at = 0
        for layer in range(2):
            for ref, row in zip(small, (0, 0, 0, 0, 0, 1, 0, 1)):
                line = ref[layer, row : row + 1, :] if len(ref.shape) == 3 else ref[layer : layer + 1, :]
                line = line.astype(F32)
                for i in range(line.shape[1] // 128):
                    lines[at // 12 : at // 12 + 1, at % 12 * 128 : at % 12 * 128 + 128] = line[:, i * 128 : (i + 1) * 128]
                    at += 1
        out[128:, :] = lines[...].astype(BF16)
        middle_id = 3 * lax.axis_index("dp") + 1
        for m in range(2):
            row = seg[m : m + 1, :]
            for i, inside in enumerate((row < middle_id, row <= middle_id)):
                bounds[m, i] = jnp.sum(jnp.where(inside, 1.0, 0.0)).astype(jnp.int32)

    vmem = pl.BlockSpec(memory_space=pltpu.VMEM)
    return pl.pallas_call(
        kernel,
        out_shape=[jax.ShapeDtypeStruct((144, 1536), BF16), jax.ShapeDtypeStruct((2, 2), jnp.int32)],
        in_specs=[vmem] * (2 + len(params)),
        out_specs=[vmem, pl.BlockSpec(memory_space=pltpu.SMEM)],
        scratch_shapes=[pltpu.VMEM((16, 1536), F32)],
    )(segments, weight, *params)


def swap(x, axis, bit):
    n = lax.axis_size(axis)
    return lax.ppermute(x, axis, [(i, i ^ bit) for i in range(n)])


def tied(x, *after):
    return lax.optimization_barrier((x,) + after)[0]


def absolute(pieces, dp):
    stacked = jnp.stack(pieces)
    return jnp.stack([lax.dynamic_index_in_dim(stacked, dp ^ j, 0, False) for j in range(4)])


def prefix_sums(x, forward, gate=None):
    n = lax.axis_size("seq")
    place = lax.axis_index("seq")
    total, result, bit = x, 0.0, 1
    while bit < n:
        got = swap(total, "seq", bit)
        if gate is not None and bit == 4:
            got = tied(got, gate)
        got = got.astype(F32)
        high = (place // bit) % 2 == 1
        result = result + jnp.where(high if forward else ~high, got, 0.0)
        total = (total.astype(F32) + got).astype(BF16)
        if bit == 1:
            pair = total
        bit *= 2
    return result, pair


def reduce_x(near, far, gate=None):
    y = lax.axis_index("seq") % 2
    got = swap(far, "dp", 2)
    if gate is not None:
        got = tied(got, gate)
    near = near.astype(F32) + got.astype(F32)
    half = near.shape[0] // 2
    mine = lax.dynamic_slice_in_dim(near, y * half, half, 0)
    return mine, lax.dynamic_slice_in_dim(near, (1 - y) * half, half, 0).astype(BF16)


def reduce_y(mine, other, gate=None):
    got = swap(other, "seq", 1)
    if gate is not None:
        got = tied(got, gate)
    return (mine + got.astype(F32)).astype(BF16)


def scatter_z(part, bit, gate=None):
    if bit >= lax.axis_size("seq"):
        return part
    high = (lax.axis_index("seq") // bit) % 2
    half = part.shape[0] // 2
    mine = lax.dynamic_slice_in_dim(part, high * half, half, 0).astype(F32)
    got = swap(lax.dynamic_slice_in_dim(part, (1 - high) * half, half, 0), "seq", bit)
    if gate is not None:
        got = tied(got, gate)
    return (mine + got.astype(F32)).astype(BF16)


def add_z(part, bit):
    while bit < lax.axis_size("seq"):
        part = (part.astype(F32) + swap(part, "seq", bit).astype(F32)).astype(BF16)
        bit *= 2
    return part


def gather_z(part, bit):
    if bit >= lax.axis_size("seq"):
        return part
    other = swap(part, "seq", bit)
    return jnp.where((lax.axis_index("seq") // bit) % 2 == 0, jnp.concatenate([part, other]), jnp.concatenate([other, part]))


def both_halves(part):
    other = swap(part, "seq", 1)
    y = lax.axis_index("seq") % 2
    return jnp.where(y == 0, jnp.concatenate([part, other]), jnp.concatenate([other, part])).astype(F32)


def per_device(tokens, cotangent, segments, input_weight, input_bias, output_weight, output_bias, up_weight, up_bias, down_weight, down_bias, norm_gain, norm_shift):
    shard, bounds = prepare(segments, input_weight, (input_bias, output_bias, up_bias, down_bias, norm_gain, norm_gain, norm_shift, norm_shift))

    def fetch(shard, gate=None):
        across = swap(shard, "dp", 2)
        last = across if gate is None else tied(across, gate)
        return [shard, swap(shard, "dp", 1), across, swap(last, "dp", 1)]

    def packed(l):
        return [output_weight[l], up_weight[l]] + [down_weight[l][i * 128 : (i + 1) * 128] for i in range(4)]

    first = fetch(shard)
    tab = jnp.stack([p[128:144] for p in first]).astype(F32)
    second = tied(jnp.concatenate(packed(0) + [input_weight[1]], 1), first[1])
    e = enter(bounds, tab, tokens, {"in": (first, 0)})
    prior0, _ = prefix_sums(e["st"], True)
    second = fetch(second, prior0)
    ws = [{"in": (first, 0), "out": (second, 0), "up": (second, 512), "down": (second, 2560)}, {"in": (second, 4608)}]
    i = inner(bounds, tab, tokens, e["qkv"], prior0, ws[0], ws[1])
    third = fetch(tied(jnp.concatenate(packed(1), 1), prior0), i["st"])
    ws[1].update({"out": (third, 0), "up": (third, 512), "down": (third, 2560)})
    prior1, _ = prefix_sums(i["st"], True)
    t = turn(bounds, tab, i["x1"], i["qkv1"], prior1, cotangent, ws[1])

    def cores(parts, *after):
        both = parts["keep"].astype(F32) + swap(tied(parts["send"], *after), "dp", 1).astype(F32)
        both = both.astype(BF16)
        return both[0], both[1]

    near_a, far_a = cores(t)
    later1, _ = prefix_sums(t["st"], False, far_a)
    b = back(bounds, tab, 1, i["x1"], tied(t["dm"], far_a), i["qkv1"], t["dnum"], t["dden"], prior1, later1, ws[1], (0, 1), i["low_a"])
    ready_1 = reduce_x(near_a[:, :2560], far_a[:, :2560], b["small2"])
    near_b, far_b = cores(b, *ready_1)
    near_2, far_2 = jnp.concatenate([near_a[:, 2560:], near_b], 1), jnp.concatenate([far_a[:, 2560:], far_b], 1)
    d = descend(bounds, tab, tied(b["dx"], far_2, *ready_1), e["qkv"], i["att"], i["inv"], i["middle"], i["slope"], i["act"], i["low_b"], ws[0])
    ready_2 = reduce_x(near_2, far_2, d["small"])
    near_d, far_d = cores(d)
    later0, pair = prefix_sums(tied(d["st"], *ready_2), False, far_d)
    part_2 = jnp.concatenate([reduce_y(*ready_1, d["small"]), reduce_y(ready_2[0], tied(ready_2[1], pair), far_d)], 1)
    lower = lambda which, dm, **more: back(bounds, tab, 0, tokens, dm, e["qkv"], d["dnum"], d["dden"], prior0, later0, ws[0], which, **more)
    v0 = lower((0,), tied(d["dm"], far_d, part_2))
    part_2 = scatter_z(part_2, 2, v0["small2"])
    ready_d1 = reduce_x(near_d[:, :2048], far_d[:, :2048], v0["small2"])
    v = lower((1,), tied(d["dm"], part_2, *ready_d1), low_a=e["low_a"], first=v0, smalls={"small0": d["small"], "small1": t["small"], "other2": b["small2"]})
    part_2 = add_z(scatter_z(part_2, 4, v["small2"]), 8)
    ready_d2 = reduce_x(near_d[:, 2048:], far_d[:, 2048:], v["small2"])
    near_c, far_c = cores(v, *ready_d2)
    ready_c = reduce_x(near_c, far_c)
    part_d = jnp.concatenate([reduce_y(*ready_d1, v["small2"]), reduce_y(ready_d2[0], tied(ready_d2[1], far_c))], 1)
    part_2 = gather_z(tied(part_2, far_c), 4)
    part_d = scatter_z(tied(part_d, ready_c[1], part_2), 2)
    part_c = reduce_y(*ready_c)
    part_d = scatter_z(tied(part_d, part_c), 4)
    part_2 = gather_z(part_2, 2)
    part_c = add_z(part_c, 2)
    part_d = gather_z(gather_z(tied(add_z(part_d, 8), part_2), 4), 2)
    in0, sum_2, sum_d = both_halves(part_c), both_halves(part_2), both_halves(part_d)
    down1, out1, up1, in1 = sum_2[:, :2048], sum_2[:, 2048:2560], sum_2[:, 2560:4608], sum_2[:, 4608:]
    down0, out0, up0 = sum_d[:, :2048], sum_d[:, 2048:2560], sum_d[:, 2560:]
    lines = in0[:SMALL_ROWS, 1536:].reshape(-1)
    layers = []
    for l in range(2):
        at, got = l * 1664, []
        for width in (384, 128, 512, 128, 128, 128, 128, 128):
            got.append(lines[at : at + width])
            at += width
        layers.append(got)
    small = lambda k: jnp.stack([layers[l][k] for l in range(2)])
    stacked = lambda d: jnp.concatenate([d[:, c * 512 : (c + 1) * 512] for c in range(4)])
    return (
        t["y"],
        jnp.concatenate([v0["dx"], tied(v["dx"], far_c)]),
        jnp.stack([in0[:, :1536], in1]),
        small(0),
        jnp.stack([out0, out1]),
        small(1),
        jnp.stack([up0, up1]),
        small(2),
        jnp.stack([stacked(down0), stacked(down1)]),
        small(3),
        jnp.stack([small(4), small(5)], 1),
        jnp.stack([small(6), small(7)], 1),
    )


def solution(mesh):
    rows = P(None, ("dp", "seq"), None)
    split = P(None, "dp", None)
    flat = P(None, "dp")
    last = P(None, None, "dp")
    params = (split, flat, split, flat, split, flat, split, flat, last, last)
    return jax.shard_map(
        per_device,
        mesh=mesh,
        in_specs=(rows, rows, P(None, ("dp", "seq"))) + params,
        out_specs=(rows, rows) + params,
        check_vma=False,
    )
```

```python
import jax
import jax.numpy as jnp
from jax import lax
from jax.experimental import pallas as pl
from jax.experimental.pallas import tpu as pltpu
from jax.sharding import PartitionSpec as P

HEAD = 64
EPSILON = 1e-05
F32 = jnp.float32
BF16 = jnp.bfloat16
ROWS = 512
TILE = 128
QUAD = 256
NT = (((1,), (1,)), ((), ()))
TN = (((0,), (0,)), ((), ()))
GELU = 0.7978845608028654
CUBE = 0.044715


def nn(a, b):
    return jnp.dot(a, b, preferred_element_type=F32)


def nt(a, b):
    return lax.dot_general(a, b, NT, preferred_element_type=F32)


def tn(a, b):
    return lax.dot_general(a, b, TN, preferred_element_type=F32)


def norm(x):
    mean = jnp.mean(x, -1, keepdims=True)
    c = x - mean
    r = lax.rsqrt(jnp.mean(c * c, -1, keepdims=True) + EPSILON)
    return c * r, r


def norm_back(u, n, r, gain):
    s = u * gain
    return r * (s - jnp.mean(s, -1, keepdims=True) - n * jnp.mean(s * n, -1, keepdims=True))


def iota(shape, dim):
    return lax.broadcasted_iota(jnp.int32, shape, dim)


def class_of(row, bounds):
    one = jnp.int32(1)
    zero = jnp.int32(0)
    return jnp.where(row >= bounds[0], one, zero) + jnp.where(row >= bounds[1], one, zero)


def head_masks():
    lane = iota((1, QUAD), 1) // HEAD
    return [jnp.where(lane == h, 1.0, 0.0).astype(BF16) for h in range(4)]


def spread(a, masks):
    return jnp.concatenate([a * m for m in masks], 0)


def block_mask():
    return jnp.where(iota((QUAD, QUAD), 0) // HEAD == iota((QUAD, QUAD), 1) // HEAD, 1.0, 0.0).astype(F32)


def same_mask(j, bounds, row_dim):
    t = iota((TILE, TILE), row_dim) + j * TILE
    s = iota((TILE, TILE), 1 - row_dim) + j * TILE
    keep = (s <= t) & (class_of(s, bounds) == class_of(t, bounds))
    return jnp.where(keep, 1.0, 0.0).astype(F32)


def rows_of_class(j, bounds, which, width=QUAD):
    return jnp.where(class_of(iota((TILE, width), 0) + j * TILE, bounds) == which, 1.0, 0.0).astype(F32)


def unpack_state(packed, state, total):
    lane = iota((HEAD, TILE), 1)
    left = jnp.where(lane < HEAD, 1.0, 0.0).astype(F32)
    state[...] = jnp.zeros_like(state)
    for pair in range(4):
        at = pl.ds(pair % 2 * TILE, TILE)
        c = packed[pair * HEAD : (pair + 1) * HEAD, :]
        state[pair // 2, at, at] = jnp.concatenate([c * left, c * (1.0 - left)], 0)
        total[pair // 2, :, at] = jnp.broadcast_to(packed[256 + pair : 257 + pair, :], (8, TILE))


def pack_state(quads, totals, packed):
    lane = iota((HEAD, TILE), 1)
    left = jnp.where(lane < HEAD, 1.0, 0.0).astype(F32)
    for pair in range(4):
        at = pair % 2 * TILE
        block = quads[pair // 2][at : at + TILE, at : at + TILE]
        c = block[:HEAD] * left + block[HEAD:] * (1.0 - left)
        packed[pair * HEAD : (pair + 1) * HEAD, :] = c.astype(BF16)
    lines = [totals[p // 2][:1, p % 2 * TILE : (p % 2 + 1) * TILE] for p in range(4)]
    packed[256:272, :] = jnp.concatenate(lines + [jnp.zeros((12, TILE), F32)], 0).astype(BF16)


def f1_body(x, tab, win, low_a, qkv, st, bounds, wait):
    half = ROWS // 2

    for i in range(2):
        at = pl.ds(i * half, half)
        n, _ = norm(x[at, :])
        low = (n * tab[4:5, :512] + tab[6:7, :512]).astype(BF16)
        low_a[at, :] = low
        if i == 0:
            wait("in")
        for c in range(3):
            cols = slice(c * 512, (c + 1) * 512)
            pre = nn(low, win[:, cols]) + tab[0:1, cols]
            if c < 2:
                pre = jnp.where(pre > 0, pre + 1.0, jnp.exp(jnp.minimum(pre, 0.0)))
            qkv[at, cols] = pre.astype(BF16)

    mid = jnp.where(class_of(iota((ROWS, QUAD), 0), bounds) == 1, 1.0, 0.0).astype(BF16)
    ones = jnp.ones((8, ROWS), BF16)
    quads, totals = [], []
    for h in range(2):
        k = qkv[:, 512 + h * QUAD : 512 + (h + 1) * QUAD] * mid
        quads.append(tn(k, qkv[:, 1024 + h * QUAD : 1024 + (h + 1) * QUAD]))
        totals.append(nn(ones, k))
    pack_state(quads, totals, st)


def forward_masks(j, bounds):
    first = j * TILE
    carried = jnp.where(j == 0, jnp.int32(1), class_of(first - 1, bounds))
    last = class_of(first + TILE - 1, bounds)
    go_on = jnp.where(carried == last, 1.0, 0.0).astype(F32)
    return rows_of_class(j, bounds, carried), rows_of_class(j, bounds, last).astype(BF16), go_on


def backward_masks(j, bounds):
    first = j * TILE
    carried = jnp.where(j == ROWS // TILE - 1, jnp.int32(1), class_of(first + TILE, bounds))
    here = class_of(first, bounds)
    go_on = jnp.where(carried == here, 1.0, 0.0).astype(F32)
    return rows_of_class(j, bounds, carried), rows_of_class(j, bounds, here).astype(BF16), go_on


def f2_body(x, qkv, prior, tab, wout, wup, wdn, state, total, att, inv, middle, low_b, act, slope, out, bounds, wait, done=lambda *names: None):
    unpack_state(prior, state, total)
    half = ROWS // 2

    @pl.loop(0, ROWS // TILE, unroll=True)
    def _(j):
        at = pl.ds(pl.multiple_of(j * TILE, TILE), TILE)
        masks = head_masks()
        blocks = block_mask()
        ones_block = blocks.astype(BF16)
        same = same_mask(j, bounds, 0)
        same4 = jnp.concatenate([same] * 4, 1)
        reads, keep, go_on = forward_masks(j, bounds)
        ones = jnp.ones((8, TILE), BF16)
        for h in range(2):
            q, k, v = (qkv[at, i * 512 + h * QUAD : i * 512 + (h + 1) * QUAD] for i in range(3))
            s = state[h]
            p = (nt(q, spread(k, masks)) * same4).astype(BF16)
            num = nn(p, spread(v, masks)) + reads * nn(q, s.astype(BF16))
            ksum = nn(same.astype(BF16), k) + reads * total[h, 0:1, :]
            den = nn((q.astype(F32) * ksum).astype(BF16), ones_block)
            r = 1.0 / den
            att[at, h * QUAD : (h + 1) * QUAD] = (num * r).astype(BF16)
            inv[at, h * QUAD : (h + 1) * QUAD] = r
            km = k * keep
            state[h] = go_on * s + tn(km, v) * blocks
            total[h] = go_on * total[h] + nn(ones, km)

    done("att", "inv")
    wait("x", "out")

    @pl.loop(0, 2, unroll=True)
    def _(i):
        at = pl.ds(pl.multiple_of(i * half, half), half)
        m = x[at, :] + nn(att[at, :], wout[...]) + tab[1:2, :512]
        middle[at, :] = m
        n, _ = norm(m)
        low_b[at, :] = (n * tab[5:6, :512] + tab[7:8, :512]).astype(BF16)

    done("middle", "low_b")
    wait("up")
    wait("down")

    @pl.loop(0, 2, unroll=True)
    def _(i):
        at = pl.ds(pl.multiple_of(i * half, half), half)
        low = low_b[at, :]
        for c in range(4):
            cols = slice(c * 512, (c + 1) * 512)
            h = nn(low, wup[:, cols]) + tab[2:3, cols]
            h2 = h * h
            t = jnp.tanh(h * (GELU + GELU * CUBE * h2))
            up = 0.5 + 0.5 * t
            act[at, cols] = (h * up).astype(BF16)
            slope[at, cols] = (up + up * (1.0 - t) * h * (GELU + 3.0 * GELU * CUBE * h2)).astype(BF16)
        o = middle[at, :] + tab[3:4, :512]
        for c in range(4):
            o = o + nn(act[at, c * 512 : (c + 1) * 512], down_block(wdn, c))
        out[at, :] = o


def down_block(wdn, c):
    return jnp.concatenate([wdn[c, :, i * 512 : (i + 1) * 512] for i in range(4)], 0)


def b1_body(g, tab, wout, wup, wdn, qkv, att, inv, middle, slope, branch_b, hid, branch_a, dm, dnum, dden, st, small, bounds, wait=lambda *names: None):
    half = ROWS // 2
    small[...] = jnp.zeros_like(small)

    for i in range(2):
        at = pl.ds(i * half, half)
        if i == 0:
            wait("g", "down", "slope")
        gi = g[at, :]
        bb = gi.astype(BF16)
        branch_b[at, :] = bb
        for c in range(4):
            cols = slice(c * 512, (c + 1) * 512)
            dh = nt(bb, down_block(wdn, c)) * slope[at, cols].astype(F32)
            hid[at, cols] = dh.astype(BF16)
            small[1:2, cols] += jnp.sum(dh, 0, keepdims=True)
        if i == 0:
            wait("up", "middle")
        u = nt(hid[at, :], wup[...])
        n, r = norm(middle[at, :])
        d = gi + norm_back(u, n, r, tab[5:6, :512])
        dm[at, :] = d
        ba = d.astype(BF16)
        branch_a[at, :] = ba
        small[0:1, :512] += jnp.sum(d, 0, keepdims=True)
        small[2:3, :512] += jnp.sum(gi, 0, keepdims=True)
        small[3:4, :512] += jnp.sum(u * n, 0, keepdims=True)
        small[4:5, :512] += jnp.sum(u, 0, keepdims=True)
        if i == 0:
            wait("out", "inv", "att", "qkv")
        da = nt(ba, wout[...])
        ones_block = block_mask().astype(BF16)
        for h in range(2):
            cols = slice(h * QUAD, (h + 1) * QUAD)
            r = inv[at, cols]
            a = da[:, cols]
            dnum[at, cols] = (a * r).astype(BF16)
            dden[at, cols] = -r * nn((a * att[at, cols].astype(F32)).astype(BF16), ones_block)

    mid = jnp.where(class_of(iota((ROWS, QUAD), 0), bounds) == 1, 1.0, 0.0).astype(BF16)
    quads, totals = [], []
    for h in range(2):
        cols = slice(h * QUAD, (h + 1) * QUAD)
        q = qkv[:, cols] * mid
        quads.append(tn(q, dnum[:, cols]))
        totals.append(jnp.sum(q.astype(F32) * dden[:, cols], 0, keepdims=True))
    pack_state(quads, totals, st)


def b2_body(x, dm, qkv, dnum, dden, prior, later, tab, win, state, total, dpre, dx, small, bounds, wait, done):
    half = ROWS // 2
    count = ROWS // TILE
    small[...] = jnp.zeros_like(small)
    unpack_state(prior, state, total)

    @pl.loop(0, count, unroll=True)
    def _(j):
        at = pl.ds(pl.multiple_of(j * TILE, TILE), TILE)
        masks = head_masks()
        blocks = block_mask()
        same = same_mask(j, bounds, 0)
        same4 = jnp.concatenate([same] * 4, 1)
        reads, keep, go_on = forward_masks(j, bounds)
        ones = jnp.ones((8, TILE), BF16)
        for h in range(2):
            cols = slice(h * QUAD, (h + 1) * QUAD)
            q, k, v = (qkv[at, i * 512 + h * QUAD : i * 512 + (h + 1) * QUAD] for i in range(3))
            dn = dnum[at, cols]
            s = state[h]
            ds = (nt(dn, spread(v, masks)) * same4).astype(BF16)
            ksum = nn(same.astype(BF16), k) + reads * total[h, 0:1, :]
            dq = nn(ds, spread(k, masks)) + reads * nt(dn, s.astype(BF16)) + dden[at, cols] * ksum
            dq = dq * jnp.minimum(q.astype(F32), 1.0)
            dpre[at, cols] = dq.astype(BF16)
            small[0:1, cols] += jnp.sum(dq, 0, keepdims=True)
            km = k * keep
            state[h] = go_on * s + tn(km, v) * blocks
            total[h] = go_on * total[h] + nn(ones, km)

    wait("later")
    unpack_state(later, state, total)

    @pl.loop(0, count, unroll=True)
    def _(back):
        j = count - 1 - back
        at = pl.ds(pl.multiple_of(j * TILE, TILE), TILE)
        masks = head_masks()
        blocks = block_mask()
        same = same_mask(j, bounds, 1)
        same4 = jnp.concatenate([same] * 4, 1)
        reads, keep, go_on = backward_masks(j, bounds)
        ones = jnp.ones((8, TILE), BF16)
        for h in range(2):
            cols = slice(h * QUAD, (h + 1) * QUAD)
            q, k, v = (qkv[at, i * 512 + h * QUAD : i * 512 + (h + 1) * QUAD] for i in range(3))
            dn = dnum[at, cols]
            s = state[h]
            low = s.astype(BF16)
            qx = spread(q, masks)
            dx_ = spread(dn, masks)
            sc = (nt(k, qx) * same4).astype(BF16)
            ds = (nt(v, dx_) * same4).astype(BF16)
            dv = nn(sc, dx_) + reads * nn(k, low)
            dd = (dden[at, cols] * q.astype(F32)).astype(BF16)
            dk = nn(ds, qx) + reads * (nt(v, low) + total[h, 0:1, :]) + nn(same.astype(BF16), dd)
            dk = dk * jnp.minimum(k.astype(F32), 1.0)
            kc = slice(512 + h * QUAD, 512 + (h + 1) * QUAD)
            vc = slice(1024 + h * QUAD, 1024 + (h + 1) * QUAD)
            dpre[at, kc] = dk.astype(BF16)
            dpre[at, vc] = dv.astype(BF16)
            small[0:1, kc] += jnp.sum(dk, 0, keepdims=True)
            small[0:1, vc] += jnp.sum(dv, 0, keepdims=True)
            state[h] = go_on * s + tn(q * keep, dn) * blocks
            total[h] = go_on * total[h] + nn(ones, dd * keep)

    done("dpre")
    wait("in", "dm", "x")

    @pl.loop(0, 2, unroll=True)
    def _(i):
        at = pl.ds(pl.multiple_of(i * half, half), half)
        u = nt(dpre[at, :], win[...])
        n, r = norm(x[at, :])
        dx[at, :] = dm[at, :] + norm_back(u, n, r, tab[4:5, :512])
        small[1:2, :512] += jnp.sum(u * n, 0, keepdims=True)
        small[2:3, :512] += jnp.sum(u, 0, keepdims=True)


WEIGHT_SHAPES = {"in": (512, 1536), "out": (512, 512), "up": (512, 2048), "down": (4, 128, 2048)}
VMEM_LIMIT = 56 * 1024 * 1024


def flip(dp, j):
    if j % 2:
        dp = dp + 1 - 2 * (dp % 2)
    if j // 2:
        dp = (dp + 2) % 4
    return dp


LINES = (("in", 3), ("out", 1), ("up", 4), ("down", 1), ("gain_a", 1), ("gain_b", 1), ("shift_a", 1), ("shift_b", 1))


def lay_out(lines, tab, dp):
    for d in range(4):
        j = dp ^ d
        at = 0
        for layer in range(2):
            for row, (_, count) in enumerate(LINES):
                for i in range(count):
                    to = (d * count + i) * 128
                    tab[layer * 8 + row : layer * 8 + row + 1, to : to + 128] = lines[j, at // 12 : at // 12 + 1, at % 12 * 128 : at % 12 * 128 + 128]
                    at += 1


def call(body, bounds, tab, ins, weights, outs, scratch, flops, moved, kept=None, after=None, once=None, extra=None, which=(0, 1), order=None):
    kept, once, extra = kept or {}, once or {}, extra or {}
    in_names, weight_names, out_names, once_names, extra_names = list(ins), list(weights), list(outs), list(once), list(extra)
    chunks = []
    for chunk, _ in weights.values():
        if not any(chunk is c for c in chunks):
            chunks.append(chunk)
    flat = [a for c in chunks for a in c]
    slots = {n: 2 * i for i, n in enumerate(in_names + out_names + once_names + extra_names)}
    first_weight = 2 * len(slots)
    last_slot = first_weight + 4 * len(weights)
    micros = len(which)

    def kernel(bounds_ref, tab_ref, *refs):
        refs = list(refs)
        take = lambda n: [refs.pop(0) for _ in range(n)]
        src = dict(zip(in_names, take(len(ins))))
        src.update(zip(extra_names, take(len(extra))))
        pieces = take(len(flat))
        dst = dict(zip(out_names + once_names, take(len(outs) + len(once))))
        full = dict(zip(in_names, take(len(ins))))
        whole = dict(zip(extra_names, take(len(extra))))
        held = dict(zip(weight_names, take(len(weights))))
        full.update(zip(out_names, take(len(outs))))
        whole.update(zip(once_names, take(len(once))))
        full.update(zip(kept, take(len(kept))))
        held.update(zip(scratch, take(len(scratch))))
        sems = refs.pop(0)
        dp = lax.axis_index("dp")
        tab = refs.pop(0)

        def arriving(name, m):
            return pltpu.make_async_copy(src[name].at[which[0] + m], full[name].at[m], sems.at[slots[name] + m])

        def fetching(name):
            return pltpu.make_async_copy(src[name], whole[name], sems.at[slots[name]])

        def leaving(name, m):
            return pltpu.make_async_copy(full[name].at[m], dst[name].at[m], sems.at[slots[name] + m])

        pending = {}
        for m in range(micros):
            for name in order or in_names + weight_names:
                if name in in_names:
                    arriving(name, m).start()
                if m or name in in_names:
                    continue
                w = weight_names.index(name)
                chunk, column = weights[name]
                base = 0
                for c in chunks:
                    if c is chunk:
                        break
                    base += len(c)
                width = 2048 if name == "down" else WEIGHT_SHAPES[name][1]
                for j in range(4):
                    owner = flip(dp, j)
                    piece = pieces[base + j].at[pl.ds(0, 128), pl.ds(column, width)]
                    target = held[name].at[owner] if name == "down" else held[name].at[pl.ds(pl.multiple_of(owner * 128, 128), 128), :]
                    copy = pltpu.make_async_copy(piece, target, sems.at[first_weight + 4 * w + j])
                    copy.start()
                    pending.setdefault(name, []).append(copy)
        for name in extra_names:
            fetching(name).start()
        lay_out(tab_ref, tab, dp)

        @pl.loop(0, micros)
        def _(m):
            env = {n: r.at[m] for n, r in full.items()}
            env.update(held)

            def wait(*names):
                for name in names:
                    if name in pending:

                        @pl.when(m == 0)
                        def _():
                            for copy in pending[name]:
                                copy.wait()

                    else:
                        arriving(name, m).wait()

            def done(*names):
                for name in names:
                    leaving(name, m).start()

            body(env, wait, done, (bounds_ref[which[0] + m, 0], bounds_ref[which[0] + m, 1]), tab)

        if after is not None:
            finished = []

            def finish(start, stop):
                cols = pl.ds(start, stop - start)
                for name in once_names:
                    copy = pltpu.make_async_copy(whole[name].at[:, :, cols], dst[name].at[:, :, cols], sems.at[last_slot + len(finished)])
                    copy.start()
                    finished.append(copy)

            after({**full, **whole}, lambda name: fetching(name).wait(), finish, dp)
            for copy in finished:
                copy.wait()
        for m in range(micros):
            for name in out_names:
                leaving(name, m).wait()

    hbm = pl.BlockSpec(memory_space=pltpu.HBM)
    shapes = [pltpu.VMEM((micros,) + a.shape[1:], a.dtype) for a in ins.values()]
    shapes += [pltpu.VMEM(a.shape, a.dtype) for a in extra.values()]
    shapes += [pltpu.VMEM(WEIGHT_SHAPES[w], BF16) for w in weight_names]
    per_micro = lambda s: (micros,) + s.shape
    shapes += [pltpu.VMEM(per_micro(s), s.dtype) for s in outs.values()]
    shapes += [pltpu.VMEM(s.shape, s.dtype) for s in once.values()]
    shapes += [pltpu.VMEM(per_micro(s), s.dtype) for s in kept.values()]
    shapes += [pltpu.VMEM(s.shape, s.dtype) for s in scratch.values()]
    shapes.append(pltpu.SemaphoreType.DMA((last_slot + 8,)))
    shapes.append(pltpu.VMEM((16, 2048), F32))
    results = pl.pallas_call(
        kernel,
        out_shape=[jax.ShapeDtypeStruct(per_micro(s), s.dtype) for s in outs.values()] + list(once.values()),
        in_specs=[pl.BlockSpec(memory_space=pltpu.SMEM), pl.BlockSpec(memory_space=pltpu.VMEM)] + [hbm] * (len(ins) + len(extra) + len(flat)),
        out_specs=[hbm] * (len(outs) + len(once)),
        scratch_shapes=shapes,
        compiler_params=pltpu.CompilerParams(vmem_limit_bytes=VMEM_LIMIT),
        cost_estimate=pl.CostEstimate(flops=int(flops), bytes_accessed=int(moved), transcendentals=0),
    )(bounds, tab, *ins.values(), *extra.values(), *flat)
    return dict(zip(out_names + once_names, results))


def shape(rows, columns, kind):
    return jax.ShapeDtypeStruct((rows, columns), kind)


WIDE = shape(512, 512, F32)
NARROW = shape(512, 512, BF16)
TRIPLE = shape(512, 1536, BF16)
FOUR = shape(512, 2048, BF16)
STATE = shape(272, 128, BF16)
SMALL = shape(8, 2048, F32)
CARRY = {"state": jax.ShapeDtypeStruct((2, QUAD, QUAD), F32), "total": jax.ShapeDtypeStruct((2, 8, QUAD), F32)}

PACKED = {"in": 1536, "out": 512, "up": 2048, "down": 2048}
SMALL_ROWS = 32


def parts_of(columns):
    return {"send": jax.ShapeDtypeStruct((2, 128, columns), BF16), "keep": jax.ShapeDtypeStruct((2, 128, columns), BF16)}


def weight_grads(full, names, dp, finish):
    owners = [flip(dp, j) for j in (1, 3, 0, 2)]
    at = 0

    def put(k, cols, value):
        if k < 2:
            full["send"][k, :, cols] = value.astype(BF16)
        else:
            full["keep"][k - 2, :, cols] = value.astype(BF16)

    for name, a, b in names:
        both = lambda refs, cols: jnp.concatenate([r[m, :, cols] for r, m in refs], 0)
        a, b = (n if isinstance(n, list) else [(full[n], 0), (full[n], 1)] for n in (a, b))
        if name == "down":
            b_all = both(b, slice(None))
            for k in range(4):
                for c in range(2):
                    cols = pl.ds(pl.multiple_of(owners[k] * 512 + c * 256, 128), 256)
                    value = tn(both(a, cols), b_all)
                    for half in range(2):
                        start = at + (2 * c + half) * 512
                        put(k, slice(start, start + 512), value[half * 128 : (half + 1) * 128])
        else:
            a_all = jnp.concatenate([both(a, pl.ds(pl.multiple_of(o * 128, 128), 128)) for o in owners], 1)
            for c in range(PACKED[name] // 512):
                value = tn(a_all, both(b, slice(c * 512, (c + 1) * 512)))
                for k in range(4):
                    put(k, slice(at + c * 512, at + (c + 1) * 512), value[k * 128 : (k + 1) * 128])
        finish(at, at + PACKED[name])
        at += PACKED[name]
    return at


def enter(bounds, tab, x, w):
    def body(e, wait, done, bounds, tab):
        wait("x")
        f1_body(e["x"], tab.at[0:8], e["in"], e["low_a"], e["qkv"], e["st"], bounds, wait)
        done("low_a", "qkv", "st")

    return call(body, bounds, tab, {"x": x}, {"in": w["in"]}, {"low_a": NARROW, "qkv": TRIPLE, "st": STATE}, {}, 6e9, 8e6)


def inner(bounds, tab, x, qkv, prior, w, w_next):
    def body(e, wait, done, bounds, tab):
        here, there = tab.at[0:8], tab.at[8:16]
        wait("qkv", "prior")
        f2_body(e["x"], e["qkv"], e["prior"], here, e["out"], e["up"], e["down"], e["state"], e["total"], e["att"], e["inv"], e["middle"], e["low_b"], e["act"], e["slope"], e["x1"], bounds, wait, done)
        done("act", "slope", "x1")
        f1_body(e["x1"], there, e["in"], e["low_a"], e["qkv1"], e["st"], bounds, wait)
        done("low_a", "qkv1", "st")

    outs = {"att": NARROW, "inv": WIDE, "middle": WIDE, "low_b": NARROW, "act": FOUR, "slope": FOUR, "x1": WIDE, "low_a": NARROW, "qkv1": TRIPLE, "st": STATE}
    return call(body, bounds, tab, {"qkv": qkv, "prior": prior, "x": x}, {"out": w["out"], "up": w["up"], "down": w["down"], "in": w_next["in"]}, outs, CARRY, 25e9, 32e6, order=("qkv", "prior", "out", "x", "up", "down", "in"))


BRANCHES = [("down", "act", "bb"), ("out", "att", "ba"), ("up", "low_b", "hid")]


def turn(bounds, tab, x, qkv, prior, g, w):
    def body(e, wait, done, bounds, tab):
        tab = tab.at[8:16]
        wait("qkv", "prior")
        f2_body(e["x"], e["qkv"], e["prior"], tab, e["out"], e["up"], e["down"], e["state"], e["total"], e["att"], e["inv"], e["middle"], e["low_b"], e["act"], e["slope"], e["y"], bounds, wait)
        done("y")
        wait("g")
        b1_body(e["g"], tab, e["out"], e["up"], e["down"], e["qkv"], e["att"], e["inv"], e["middle"], e["slope"], e["bb"], e["hid"], e["ba"], e["dm"], e["dnum"], e["dden"], e["st"], e["small"], bounds)
        done("dm", "dnum", "dden", "st", "small")

    def after(full, wait, finish, dp):
        weight_grads(full, BRANCHES, dp, finish)

    outs = {"y": WIDE, "dm": WIDE, "dnum": NARROW, "dden": WIDE, "st": STATE, "small": SMALL}
    kept = {"att": NARROW, "low_b": NARROW, "act": FOUR, "bb": NARROW, "hid": FOUR, "ba": NARROW}
    scratch = {"inv": WIDE, "middle": WIDE, "slope": FOUR, **CARRY}
    return call(body, bounds, tab, {"qkv": qkv, "prior": prior, "x": x, "g": g}, {"out": w["out"], "up": w["up"], "down": w["down"]}, outs, scratch, 34e9, 36e6, kept, after, parts_of(4608), order=("qkv", "prior", "out", "x", "up", "down", "g"))


def back(bounds, tab, layer, x, dm, qkv, dnum, dden, prior, later, w, which, low_a=None, first=None, smalls=None):
    def body(e, wait, done, bounds, tab):
        wait("qkv", "dnum", "dden", "prior")
        b2_body(e["x"], e["dm"], e["qkv"], e["dnum"], e["dden"], e["prior"], e["later"], tab.at[8 * layer : 8 * layer + 8], e["in"], e["state"], e["total"], e["dpre"], e["dx"], e["small2"], bounds, wait, done if low_a is None else lambda name: None)
        done("dx", "small2")

    def after(full, wait, finish, dp):
        for name in extra:
            wait(name)
        pre = "dpre" if first is None else [(full["dpre0"], 0), (full["dpre"], 0)]
        at = weight_grads(full, [("in", "low_a", pre)], dp, finish)
        if smalls:
            for k, j in enumerate((1, 3, 0, 2)):
                second = [(full["first2"], 0), (full["small2"], 0)] if first is not None else [(full["small2"], 0), (full["small2"], 1)]
                two = lambda n: [(full[n], 0), (full[n], 1)]
                lines = small_lines([two("small0"), second, two("small1"), two("other2")], flip(dp, j))
                lines = jnp.concatenate([lines, jnp.zeros((128 - SMALL_ROWS, 128), F32)], 0)
                if k < 2:
                    full["send"][k, :, at : at + 128] = lines.astype(BF16)
                else:
                    full["keep"][k - 2, :, at : at + 128] = lines.astype(BF16)
            finish(at, at + 128)

    ins = {"qkv": qkv, "dnum": dnum, "dden": dden, "prior": prior, "later": later, "dm": dm, "x": x}
    outs = {"dx": WIDE, "small2": SMALL}
    if low_a is None:
        return call(body, bounds, tab, ins, {"in": w["in"]}, {**outs, "dpre": TRIPLE}, CARRY, 10e9, 10e6, which=which)
    extra = {"low_a": low_a, **(smalls or {})}
    if first is not None:
        extra.update({"dpre0": first["dpre"], "first2": first["small2"]})
    return call(body, bounds, tab, ins, {"in": w["in"]}, outs, CARRY, 20e9, 20e6, {"dpre": TRIPLE}, after, parts_of(1664 if smalls else 1536), extra, which)


def descend(bounds, tab, g, qkv, att, inv, middle, slope, act, low_b, w):
    def body(e, wait, done, bounds, tab):
        b1_body(e["g"], tab.at[0:8], e["out"], e["up"], e["down"], e["qkv"], e["att"], e["inv"], e["middle"], e["slope"], e["bb"], e["hid"], e["ba"], e["dm"], e["dnum"], e["dden"], e["st"], e["small"], bounds, wait)
        done("dm", "dnum", "dden", "st", "small")

    def after(full, wait, finish, dp):
        wait("act")
        wait("low_b")
        weight_grads(full, BRANCHES, dp, finish)

    ins = {"g": g, "slope": slope, "middle": middle, "inv": inv, "att": att, "qkv": qkv}
    outs = {"dm": WIDE, "dnum": NARROW, "dden": WIDE, "st": STATE, "small": SMALL}
    kept = {"bb": NARROW, "hid": FOUR, "ba": NARROW}
    return call(body, bounds, tab, ins, {"down": w["down"], "up": w["up"], "out": w["out"]}, outs, {}, 16e9, 30e6, kept, after, parts_of(4608), {"act": act, "low_b": low_b}, order=("g", "down", "slope", "up", "middle", "out", "inv", "att", "qkv"))


def small_lines(smalls, owner):
    lines = []
    for layer in range(2):
        first, second = smalls[2 * layer], smalls[2 * layer + 1]
        for ref, row, width in ((second, 0, 384), (first, 0, 128), (first, 1, 512), (first, 2, 128), (second, 1, 128), (first, 3, 128), (second, 2, 128), (first, 4, 128)):
            for i in range(width // 128):
                at = pl.ds(pl.multiple_of(owner * width + i * 128, 128), 128)
                lines.append(sum(r[m, row : row + 1, at] for r, m in ref))
    return jnp.concatenate(lines + [jnp.zeros((SMALL_ROWS - len(lines), 128), F32)], 0)


def prepare(segments, weight, params):
    def kernel(seg, weight, *refs):
        *small, out, bounds, lines = refs
        out[:128, :] = weight[0]
        lines[...] = jnp.zeros_like(lines)
        at = 0
        for layer in range(2):
            for ref, row in zip(small, (0, 0, 0, 0, 0, 1, 0, 1)):
                line = ref[layer, row : row + 1, :] if len(ref.shape) == 3 else ref[layer : layer + 1, :]
                line = line.astype(F32)
                for i in range(line.shape[1] // 128):
                    lines[at // 12 : at // 12 + 1, at % 12 * 128 : at % 12 * 128 + 128] = line[:, i * 128 : (i + 1) * 128]
                    at += 1
        out[128:, :] = lines[...].astype(BF16)
        middle_id = 3 * lax.axis_index("dp") + 1
        for m in range(2):
            row = seg[m : m + 1, :]
            for i, inside in enumerate((row < middle_id, row <= middle_id)):
                bounds[m, i] = jnp.sum(jnp.where(inside, 1.0, 0.0)).astype(jnp.int32)

    vmem = pl.BlockSpec(memory_space=pltpu.VMEM)
    return pl.pallas_call(
        kernel,
        out_shape=[jax.ShapeDtypeStruct((144, 1536), BF16), jax.ShapeDtypeStruct((2, 2), jnp.int32)],
        in_specs=[vmem] * (2 + len(params)),
        out_specs=[vmem, pl.BlockSpec(memory_space=pltpu.SMEM)],
        scratch_shapes=[pltpu.VMEM((16, 1536), F32)],
    )(segments, weight, *params)


def swap(x, axis, bit):
    n = lax.axis_size(axis)
    return lax.ppermute(x, axis, [(i, i ^ bit) for i in range(n)])


def tied(x, *after):
    return lax.optimization_barrier((x,) + after)[0]


def absolute(pieces, dp):
    stacked = jnp.stack(pieces)
    return jnp.stack([lax.dynamic_index_in_dim(stacked, dp ^ j, 0, False) for j in range(4)])


def prefix_sums(x, forward, gate=None):
    n = lax.axis_size("seq")
    place = lax.axis_index("seq")
    total, result, bit = x, 0.0, 1
    while bit < n:
        got = swap(total, "seq", bit)
        if gate is not None and bit == 4:
            got = tied(got, gate)
        got = got.astype(F32)
        high = (place // bit) % 2 == 1
        result = result + jnp.where(high if forward else ~high, got, 0.0)
        total = (total.astype(F32) + got).astype(BF16)
        if bit == 1:
            pair = total
        bit *= 2
    return result, pair


def reduce_x(near, far, gate=None):
    y = lax.axis_index("seq") % 2
    got = swap(far, "dp", 2)
    if gate is not None:
        got = tied(got, gate)
    near = near.astype(F32) + got.astype(F32)
    half = near.shape[0] // 2
    mine = lax.dynamic_slice_in_dim(near, y * half, half, 0)
    return mine, lax.dynamic_slice_in_dim(near, (1 - y) * half, half, 0).astype(BF16)


def reduce_y(mine, other, gate=None):
    got = swap(other, "seq", 1)
    if gate is not None:
        got = tied(got, gate)
    return (mine + got.astype(F32)).astype(BF16)


def scatter_z(part, bit, gate=None):
    if bit >= lax.axis_size("seq"):
        return part
    high = (lax.axis_index("seq") // bit) % 2
    half = part.shape[0] // 2
    mine = lax.dynamic_slice_in_dim(part, high * half, half, 0).astype(F32)
    got = swap(lax.dynamic_slice_in_dim(part, (1 - high) * half, half, 0), "seq", bit)
    if gate is not None:
        got = tied(got, gate)
    return (mine + got.astype(F32)).astype(BF16)


def add_z(part, bit):
    while bit < lax.axis_size("seq"):
        part = (part.astype(F32) + swap(part, "seq", bit).astype(F32)).astype(BF16)
        bit *= 2
    return part


def gather_z(part, bit):
    if bit >= lax.axis_size("seq"):
        return part
    other = swap(part, "seq", bit)
    return jnp.where((lax.axis_index("seq") // bit) % 2 == 0, jnp.concatenate([part, other]), jnp.concatenate([other, part]))


def both_halves(part):
    other = swap(part, "seq", 1)
    y = lax.axis_index("seq") % 2
    return jnp.where(y == 0, jnp.concatenate([part, other]), jnp.concatenate([other, part])).astype(F32)


def per_device(tokens, cotangent, segments, input_weight, input_bias, output_weight, output_bias, up_weight, up_bias, down_weight, down_bias, norm_gain, norm_shift):
    shard, bounds = prepare(segments, input_weight, (input_bias, output_bias, up_bias, down_bias, norm_gain, norm_gain, norm_shift, norm_shift))

    def fetch(shard, gate=None):
        across = swap(shard, "dp", 2)
        last = across if gate is None else tied(across, gate)
        return [shard, swap(shard, "dp", 1), across, swap(last, "dp", 1)]

    def packed(l):
        return [output_weight[l], up_weight[l]] + [down_weight[l][i * 128 : (i + 1) * 128] for i in range(4)]

    first = fetch(shard)
    tab = jnp.stack([p[128:144] for p in first]).astype(F32)
    second = tied(jnp.concatenate(packed(0) + [input_weight[1]], 1), first[1])
    e = enter(bounds, tab, tokens, {"in": (first, 0)})
    prior0, _ = prefix_sums(e["st"], True)
    second = fetch(second, prior0)
    ws = [{"in": (first, 0), "out": (second, 0), "up": (second, 512), "down": (second, 2560)}, {"in": (second, 4608)}]
    i = inner(bounds, tab, tokens, e["qkv"], prior0, ws[0], ws[1])
    third = fetch(tied(jnp.concatenate(packed(1), 1), prior0), i["st"])
    ws[1].update({"out": (third, 0), "up": (third, 512), "down": (third, 2560)})
    prior1, _ = prefix_sums(i["st"], True)
    t = turn(bounds, tab, i["x1"], i["qkv1"], prior1, cotangent, ws[1])

    def cores(parts, *after):
        both = parts["keep"].astype(F32) + swap(tied(parts["send"], *after), "dp", 1).astype(F32)
        both = both.astype(BF16)
        return both[0], both[1]

    near_a, far_a = cores(t)
    later1, _ = prefix_sums(t["st"], False, far_a)
    b = back(bounds, tab, 1, i["x1"], tied(t["dm"], far_a), i["qkv1"], t["dnum"], t["dden"], prior1, later1, ws[1], (0, 1), i["low_a"])
    ready_1 = reduce_x(near_a[:, :2560], far_a[:, :2560], b["small2"])
    near_b, far_b = cores(b, *ready_1)
    near_2, far_2 = jnp.concatenate([near_a[:, 2560:], near_b], 1), jnp.concatenate([far_a[:, 2560:], far_b], 1)
    d = descend(bounds, tab, tied(b["dx"], far_2, *ready_1), e["qkv"], i["att"], i["inv"], i["middle"], i["slope"], i["act"], i["low_b"], ws[0])
    ready_2 = reduce_x(near_2, far_2, d["small"])
    near_d, far_d = cores(d)
    later0, pair = prefix_sums(tied(d["st"], *ready_2), False, far_d)
    part_2 = jnp.concatenate([reduce_y(*ready_1, d["small"]), reduce_y(ready_2[0], tied(ready_2[1], pair), far_d)], 1)
    lower = lambda which, dm, **more: back(bounds, tab, 0, tokens, dm, e["qkv"], d["dnum"], d["dden"], prior0, later0, ws[0], which, **more)
    v0 = lower((0,), tied(d["dm"], far_d, part_2))
    part_2 = scatter_z(part_2, 2, v0["small2"])
    ready_d1 = reduce_x(near_d[:, :2048], far_d[:, :2048], v0["small2"])
    v = lower((1,), tied(d["dm"], part_2, *ready_d1), low_a=e["low_a"], first=v0, smalls={"small0": d["small"], "small1": t["small"], "other2": b["small2"]})
    part_2 = add_z(scatter_z(part_2, 4, v["small2"]), 8)
    ready_d2 = reduce_x(near_d[:, 2048:], far_d[:, 2048:], v["small2"])
    near_c, far_c = cores(v, *ready_d2)
    ready_c = reduce_x(near_c, far_c)
    part_d = jnp.concatenate([reduce_y(*ready_d1, v["small2"]), reduce_y(ready_d2[0], tied(ready_d2[1], far_c))], 1)
    part_2 = gather_z(tied(part_2, far_c), 4)
    part_d = scatter_z(tied(part_d, ready_c[1], part_2), 2)
    part_c = reduce_y(*ready_c)
    part_d = scatter_z(tied(part_d, part_c), 4)
    part_2 = gather_z(part_2, 2)
    part_c = add_z(part_c, 2)
    part_d = gather_z(gather_z(tied(add_z(part_d, 8), part_2), 4), 2)
    in0, sum_2, sum_d = both_halves(part_c), both_halves(part_2), both_halves(part_d)
    down1, out1, up1, in1 = sum_2[:, :2048], sum_2[:, 2048:2560], sum_2[:, 2560:4608], sum_2[:, 4608:]
    down0, out0, up0 = sum_d[:, :2048], sum_d[:, 2048:2560], sum_d[:, 2560:]
    lines = in0[:SMALL_ROWS, 1536:].reshape(-1)
    layers = []
    for l in range(2):
        at, got = l * 1664, []
        for width in (384, 128, 512, 128, 128, 128, 128, 128):
            got.append(lines[at : at + width])
            at += width
        layers.append(got)
    small = lambda k: jnp.stack([layers[l][k] for l in range(2)])
    stacked = lambda d: jnp.concatenate([d[:, c * 512 : (c + 1) * 512] for c in range(4)])
    return (
        t["y"],
        jnp.concatenate([v0["dx"], tied(v["dx"], far_c)]),
        jnp.stack([in0[:, :1536], in1]),
        small(0),
        jnp.stack([out0, out1]),
        small(1),
        jnp.stack([up0, up1]),
        small(2),
        jnp.stack([stacked(down0), stacked(down1)]),
        small(3),
        jnp.stack([small(4), small(5)], 1),
        jnp.stack([small(6), small(7)], 1),
    )


def solution(mesh):
    rows = P(None, ("dp", "seq"), None)
    split = P(None, "dp", None)
    flat = P(None, "dp")
    last = P(None, None, "dp")
    params = (split, flat, split, flat, split, flat, split, flat, last, last)
    return jax.shard_map(
        per_device,
        mesh=mesh,
        in_specs=(rows, rows, P(None, ("dp", "seq"))) + params,
        out_specs=(rows, rows) + params,
        check_vma=False,
    )
```
